32 devices in a mesh: seq: 8 (over z, y), head: 4 (over x, core).
Axes of the slice: x: 2, y: 2, z: 4, core: 2. Of those that a mesh axis runs over, the one named last changes fastest.
Arguments:
- hidden_in: bfloat16 [2048, 2304], P(('seq', 'head')), may hold values from -6 to 6
- qkv_weight: bfloat16 [2304, 3, 2048], P(None, None, 'head'), may hold values from -0.125 to 0.125
- conv_weight: bfloat16 [3, 4, 2048], P(None, None, 'head'), may hold values from -3 to 3
- decay_log: float32 [16], P('head'), may hold values from -9 to -3
- dt_bias: float32 [2048], P('head'), may hold values from -3 to 3
- decay_down: bfloat16 [2304, 128], replicated, may hold values from -0.125 to 0.125
- decay_up: bfloat16 [128, 2048], P(None, 'head'), may hold values from -0.5 to 0.5
- beta_weight: bfloat16 [2304, 16], P(None, 'head'), may hold values from -0.125 to 0.125
- gate_down: bfloat16 [2304, 128], replicated, may hold values from -0.125 to 0.125
- gate_up: bfloat16 [128, 2048], P(None, 'head'), may hold values from -0.5 to 0.5
- norm_gain: float32 [128], replicated, may hold values from 0.1 to 1.9
- out_weight: bfloat16 [2048, 2304], P('head'), may hold values from -0.125 to 0.125
Outputs:
- layer_out: bfloat16 [2048, 2304], P(('seq', 'head'))
The draws below stay inside these ranges and needn't reach their ends.
All inputs are finite; a program needn't handle non-finite values.
Results may differ from the reference program's by a relative error of at most 0.015.
Values may be sent and summed in bfloat16 or wider, within the bound.
No kernel may reach another device: no remote copies, remote signals or barrier semaphores. Data moves between devices by JAX's collectives and lax.ppermute only.
A program may use at most 128 MiB of HBM per device.

```python
import jax
import jax.numpy as jnp
from jax import lax

D = 2304
H = 16
DK = 128
RANK = 128
KERNEL = 4
TOKENS = 2048


def level_of(key, extent, shards, smallest, high):
    loudness, own = 1.0, jax.random.fold_in(key, 6)
    for position, parts in shards:
        heights = jnp.exp(jax.random.uniform(jax.random.fold_in(own, position), (parts,), jnp.float32, smallest / len(shards), high / len(shards)))
        loudness = loudness * jnp.repeat(heights, extent[position] // parts).reshape([-1 if axis == position else 1 for axis in range(len(extent))])
    return loudness


def noise(own_key, extent, scale, limit, cuts=(), dtype=jnp.bfloat16):
    array = jax.random.normal(own_key, extent, jnp.float32) * scale
    if len(cuts) > 0:
        array = level_of(own_key, extent, cuts, -0.22, 0.18) * array
    return jnp.clip(array, min=-limit, max=limit).astype(dtype)


def setup_inputs(seed: int = 0) -> dict:
    key_of = jax.random.split(jax.random.key(seed), 13)
    return {
        "hidden_in": noise(key_of[0], (TOKENS, D), 1.0, 6.0, ((0, 32),)),
        "qkv_weight": noise(key_of[1], (D, 3, H * DK), D ** -0.5, 0.125, ((2, 4),)),
        "conv_weight": noise(key_of[2], (3, KERNEL, H * DK), 0.5, 3.0, ((2, 4),)),
        "decay_log": jnp.clip(-9.0 + 6.0 * jax.random.uniform(key_of[3], (H,), jnp.float32) ** level_of(key_of[3], (H,), ((0, 4),), -0.2, 0.2), -9.0, -3.0),
        "dt_bias": noise(key_of[4], (H * DK,), 1.0, 3.0, ((0, 4),), jnp.float32),
        "decay_down": noise(key_of[5], (D, RANK), D ** -0.5, 0.125),
        "decay_up": noise(key_of[6], (RANK, H * DK), RANK ** -0.5, 0.5, ((1, 4),)),
        "beta_weight": noise(key_of[7], (D, H), D ** -0.5, 0.125, ((1, 4),)),
        "gate_down": noise(key_of[8], (D, RANK), D ** -0.5, 0.125),
        "gate_up": noise(key_of[9], (RANK, H * DK), RANK ** -0.5, 0.5, ((1, 4),)),
        "norm_gain": jnp.clip(1.0 + 0.18 * jax.random.normal(key_of[10], (DK,), jnp.float32), 0.1, 1.9),
        "out_weight": noise(key_of[11], (H * DK, D), (H * DK) ** -0.5, 0.125, ((0, 4),)),
    }


def l2_normalize(values):
    return values * lax.rsqrt(lax.optimization_barrier(jnp.sum(values * values, axis=-1, keepdims=True)) + 1e-06)

def reference(hidden_in, qkv_weight, conv_weight, decay_log, dt_bias, decay_down, decay_up, beta_weight, gate_down, gate_up, norm_gain, out_weight):
    token_count = hidden_in.shape[0]
    full_width = H * DK
    projected = jnp.dot(hidden_in, qkv_weight.reshape(D, 3 * full_width), preferred_element_type=jnp.float32).astype(jnp.bfloat16)
    projected = projected.reshape(token_count, 3, full_width)
    padded = jnp.concatenate([jnp.zeros((KERNEL - 1, 3, full_width), jnp.bfloat16), projected], axis=0).astype(jnp.float32)
    taps = conv_weight.astype(jnp.float32)
    convolved = jnp.zeros((token_count, 3, full_width), jnp.float32)
    for tap_index in range(KERNEL):
        convolved = convolved + padded[tap_index:tap_index + token_count] * taps[:, tap_index][None]
    convolved = jax.nn.silu(convolved).astype(jnp.bfloat16)
    decay_low = jnp.dot(hidden_in, decay_down, preferred_element_type=jnp.float32).astype(jnp.bfloat16)
    raw_decay = jnp.dot(decay_low, decay_up, preferred_element_type=jnp.float32) + dt_bias
    log_decay = -jnp.exp(decay_log)[None, :, None] * jax.nn.softplus(raw_decay).reshape(token_count, H, DK)
    strength = jax.nn.sigmoid(jnp.dot(hidden_in, beta_weight, preferred_element_type=jnp.float32))
    queries = l2_normalize(convolved[:, 0].astype(jnp.float32).reshape(token_count, H, DK)) * DK ** (-0.5)
    keys = l2_normalize(convolved[:, 1].astype(jnp.float32).reshape(token_count, H, DK))
    values = convolved[:, 2].astype(jnp.float32).reshape(token_count, H, DK)
    fading = jnp.exp(log_decay)

    def advance(memory_state, inputs):
        current_query_vector, current_key_vector, value_row, fade_row, strength_row = inputs
        memory_state = memory_state * fade_row[:, :, None]
        retrieved_value = jnp.einsum('ci,ciu->cu', current_key_vector, memory_state, precision=lax.Precision.HIGHEST)
        memory_state = memory_state + strength_row[:, None, None] * current_key_vector[:, :, None] * (value_row - retrieved_value)[:, None, :]
        return (memory_state, jnp.einsum('ci,ciu->cu', current_query_vector, memory_state, precision=lax.Precision.HIGHEST))
    initial = jnp.zeros((H, DK, DK), jnp.float32)
    _, attended = lax.scan(advance, initial, (queries, keys, values, fading, strength))
    gate_low = jnp.dot(hidden_in, gate_down, preferred_element_type=jnp.float32).astype(jnp.bfloat16)
    out_gate = jax.nn.sigmoid(jnp.dot(gate_low, gate_up, preferred_element_type=jnp.float32)).reshape(token_count, H, DK)
    inverse_rms = lax.rsqrt(lax.optimization_barrier(jnp.mean(attended * attended, axis=-1, keepdims=True)) + 1e-05)
    normed = (attended * inverse_rms * norm_gain * out_gate).astype(jnp.bfloat16).reshape(token_count, full_width)
    return jnp.dot(normed, out_weight, preferred_element_type=jnp.float32).astype(jnp.bfloat16)
```

```python
import functools
import math

import jax
import jax.numpy as jnp
from jax import lax
from jax.experimental import pallas as pl
from jax.experimental.pallas import tpu as pltpu
from jax.sharding import PartitionSpec as P

RIM = 16
BASE = 16
VMEM_LIMIT = 40 * 1024 * 1024
f32 = jnp.float32
bf16 = jnp.bfloat16


def dot(left, right, contract=((1,), (0,))):
    return lax.dot_general(left, right, (contract, ((), ())), preferred_element_type=f32)


def passed_along(block, axis, distance):
    size = lax.axis_size(axis)
    return lax.ppermute(block, axis, [(i, i + distance) for i in range(size - distance)])


def swapped(block, axis, bit):
    return lax.ppermute(block, axis, [(i, i ^ bit) for i in range(lax.axis_size(axis))])


def bits_of(size):
    assert size & (size - 1) == 0
    return [1 << i for i in range(size.bit_length() - 1)]


def reversed_order(size):
    width = size.bit_length() - 1
    return sorted(range(size), key=lambda k: int(f"{k:0{width}b}"[::-1], 2) if width else 0)


def slabs_of(own, axis):
    size = lax.axis_size(axis)
    slabs = {0: own}
    for bit in reversed(bits_of(size)):
        for k in sorted(slabs):
            slabs[k ^ bit] = swapped(slabs[k], axis, bit)
    return [slabs[k] for k in range(size)]


def rim_of(own, size_rows):
    heads, seqs = lax.axis_size("head"), lax.axis_size("seq")
    tail = own[own.shape[0] - size_rows :]
    rim = jnp.zeros_like(tail)
    for k in range(heads):
        route = [(s * heads + heads - 1, (s + 1) * heads + k) for s in range(seqs - 1)]
        rim = rim + lax.ppermute(tail, ("seq", "head"), route)
    return rim


def vmem_call(body, out_shape, args, scratch=(), in_specs=None, flops=0, moved=0):
    return pl.pallas_call(
        body,
        out_shape=out_shape,
        in_specs=in_specs or [pl.BlockSpec(memory_space=pltpu.VMEM)] * len(args),
        out_specs=jax.tree.map(lambda _: pl.BlockSpec(memory_space=pltpu.VMEM), out_shape),
        scratch_shapes=list(scratch),
        compiler_params=pltpu.CompilerParams(vmem_limit_bytes=VMEM_LIMIT),
        cost_estimate=pl.CostEstimate(flops=flops, bytes_accessed=moved, transcendentals=0),
    )(*args)


def front_body(
    slab_count,
    order_ref,
    rim_ref,
    *refs,
):
    slab_refs = refs[:slab_count]
    (
        weight_ref,
        small_ref,
        taps_ref,
        rate_ref,
        bias_ref,
        decay_up_ref,
        pair_ref,
        solved_ref,
        attend_ref,
        start_ref,
        gate_ref,
        rows_ref,
        weights,
        projected,
        mixing,
        inverse,
        inverse_low,
        row_sem,
        weight_sem,
    ) = refs[slab_count:]
    slab_rows = slab_refs[0].shape[0]
    heads, size = pair_ref.shape[0], pair_ref.shape[1]
    count = start_ref.shape[1]
    tap_count = taps_ref.shape[0] // 3
    chunk = math.gcd(count, 64)
    chunks = count // chunk

    copies = [pltpu.make_async_copy(rim_ref, rows_ref.at[pl.ds(0, RIM)], row_sem.at[slab_count])]
    for k in range(slab_count):
        begin = pl.multiple_of(RIM + order_ref[k] * slab_rows, 16)
        copies.append(
            pltpu.make_async_copy(
                slab_refs[k], rows_ref.at[pl.ds(begin, slab_rows)], row_sem.at[k]
            )
        )
    loads = [
        pltpu.make_async_copy(weight_ref.at[c], weights.at[c], weight_sem.at[c]) for c in range(3)
    ]
    for copy in copies + loads:
        copy.start()
    for copy in copies:
        copy.wait()

    low = dot(rows_ref[RIM:, :], small_ref[...])
    rank = decay_up_ref.shape[0]
    decay_low = low[:, :rank].astype(bf16)
    gate_ref[...] = low[:, rank : 2 * rank].astype(bf16)
    strength = jax.nn.sigmoid(low[:, 2 * rank :])
    raw = dot(decay_low, decay_up_ref[...]) + bias_ref[...]
    softplus = jnp.maximum(raw, 0.0) + jnp.log1p(jnp.exp(-jnp.abs(raw)))
    log_decay = -rate_ref[...] * softplus
    row = lax.broadcasted_iota(jnp.int32, (count, count), 0)
    col = lax.broadcasted_iota(jnp.int32, (count, count), 1)
    lower = jnp.where(row >= col, 1.0, 0.0).astype(bf16)
    high = log_decay.astype(bf16)
    cumulative = dot(lower, high) + dot(lower, (log_decay - high.astype(f32)).astype(bf16))

    convolved = []
    for c in range(3):
        loads[c].wait()
        projected[c] = dot(rows_ref[...], weights[c]).astype(bf16).astype(f32)
        total = None
        for i in range(tap_count):
            term = projected[c, pl.ds(RIM - tap_count + 1 + i, count), :] * taps_ref[
                pl.ds(c * tap_count + i, 1), :
            ]
            total = term if total is None else total + term
        convolved.append((total / (1.0 + jnp.exp(-total))).astype(bf16).astype(f32))

    def by_chunk(rows):
        return jnp.concatenate([jnp.broadcast_to(r, (chunk, size)) for r in rows], axis=0)

    eye = row == col
    stops, sides = [], []
    for h in range(heads):
        lanes = slice(h * size, (h + 1) * size)
        queries, keys, values = (part[:, lanes] for part in convolved)
        queries = queries * lax.rsqrt(jnp.sum(queries * queries, -1, keepdims=True) + 1e-06)
        queries = queries * size ** (-0.5)
        keys = keys * lax.rsqrt(jnp.sum(keys * keys, -1, keepdims=True) + 1e-06)
        running = cumulative[:, lanes]
        middles = [running[a * chunk + chunk // 2 : a * chunk + chunk // 2 + 1] for a in range(chunks)]
        middle = by_chunk(middles)
        rise = jnp.exp(running - middle)
        key_rise, query_rise = keys * rise, queries * rise
        key_fall = keys * strength[:, h : h + 1] * jnp.exp(middle - running)
        last = running[count - 1 :]
        stops.append(
            ((key_fall * by_chunk([jnp.exp(last - m) for m in middles])).astype(bf16), jnp.exp(last))
        )
        entry = by_chunk([jnp.exp(m) for m in middles])
        start_ref[h] = query_rise * entry
        sides.append(
            jnp.concatenate([(key_rise * entry).astype(bf16), values.astype(bf16)], axis=1)
        )
        for a in range(chunks):
            here = slice(a * chunk, (a + 1) * chunk)
            left = jnp.concatenate([key_rise[here], query_rise[here]], axis=0).astype(bf16)
            falls = []
            for b in range(chunks):
                there = slice(b * chunk, (b + 1) * chunk)
                if b < a:
                    falls.append(key_fall[there] * jnp.exp(middles[a] - middles[b]))
                elif b == a:
                    falls.append(key_fall[there])
                else:
                    falls.append(jnp.zeros((chunk, size), f32))
            right = jnp.concatenate(falls, axis=0).astype(bf16)
            scores = dot(left, right, ((1,), (1,)))
            mixing[h, here, :] = jnp.where(row[here] > col[here], scores[:chunk], 0.0).astype(bf16)
            attend_ref[h, here, :] = jnp.where(row[here] >= col[here], scores[chunk:], 0.0).astype(
                bf16
            )

    base = math.gcd(count, BASE)
    same = row // base == col // base
    powers = [None] * heads
    for h in range(heads):
        nilpotent = jnp.where(same, -mixing[h].astype(f32), 0.0)
        powers[h] = nilpotent.astype(bf16)
        inverse[h] = jnp.where(eye, 1.0, nilpotent)
    for _ in range(1, (base - 1).bit_length()):
        for h in range(heads):
            powers[h] = dot(powers[h], powers[h]).astype(bf16)
        for h in range(heads):
            inverse[h] = inverse[h] + dot(inverse[h].astype(bf16), powers[h])
    for h in range(heads):
        inverse_low[h] = inverse[h].astype(bf16)
    width = base
    while width < count:
        odd = [slice(i, i + width) for i in range(width, count, 2 * width)]
        pair_mask = jnp.where(
            (row // width % 2 == 1) & (col // width == row // width - 1), 1.0, 0.0
        ).astype(bf16)
        halves = []
        for h in range(heads):
            chosen = jnp.concatenate([inverse_low[h, rows, :] for rows in odd], axis=0)
            halves.append(dot(chosen, mixing[h] * pair_mask).astype(bf16))
        for h in range(heads):
            change = dot(halves[h], inverse_low[h])
            for i, rows in enumerate(odd):
                new = inverse_low[h, rows, :].astype(f32) - change[i * width : (i + 1) * width]
                inverse_low[h, rows, :] = new.astype(bf16)
        width *= 2

    for h in range(heads):
        solved = dot(inverse_low[h], sides[h]).astype(bf16)
        solved_ref[h] = solved
        stop, fade = stops[h]
        moved = dot(stop, solved, ((0,), (0,)))
        diagonal = jnp.where(eye[:size, :size], jnp.broadcast_to(fade, (size, size)), 0.0)
        pair_ref[h, :, :size] = (diagonal - moved[:, :size]).astype(bf16)
        pair_ref[h, :, size:] = moved[:, size:].astype(bf16)


def front(order, rim, slabs, weight, small, taps, rate, bias, decay_up, heads, size):
    slab_count, slab_rows = len(slabs), slabs[0].shape[0]
    count = slab_count * slab_rows
    width = weight.shape[1]
    channels = heads * size
    vm, anywhere = pl.BlockSpec(memory_space=pltpu.VMEM), pl.BlockSpec(memory_space=pl.ANY)
    args = (order, rim, *slabs, weight, small, taps, rate, bias, decay_up)
    specs = [pl.BlockSpec(memory_space=pltpu.SMEM)] + [anywhere] * (slab_count + 2) + [vm] * 5
    return vmem_call(
        functools.partial(front_body, slab_count),
        (
            jax.ShapeDtypeStruct((heads, size, 2 * size), bf16),
            jax.ShapeDtypeStruct((heads, count, 2 * size), bf16),
            jax.ShapeDtypeStruct((heads, count, count), bf16),
            jax.ShapeDtypeStruct((heads, count, size), f32),
            jax.ShapeDtypeStruct((count, decay_up.shape[0]), bf16),
        ),
        args,
        scratch=[
            pltpu.VMEM((RIM + count, width), bf16),
            pltpu.VMEM((3, width, channels), bf16),
            pltpu.VMEM((3, RIM + count, channels), f32),
            pltpu.VMEM((heads, count, count), bf16),
            pltpu.VMEM((heads, count, count), f32),
            pltpu.VMEM((heads, count, count), bf16),
            pltpu.SemaphoreType.DMA((slab_count + 1,)),
            pltpu.SemaphoreType.DMA((3,)),
        ],
        in_specs=specs,
        flops=2 * count * width * channels * 4,
        moved=2 * 4 * width * channels,
    )


def rows_body(attend_ref, solved_ref, start_ref, low_ref, up_ref, raised_ref, output_ref, gate_ref):
    heads, _, size = start_ref.shape
    gate_ref[...] = jax.nn.sigmoid(dot(low_ref[...], up_ref[...]))
    for h in range(heads):
        both = dot(attend_ref[h], solved_ref[h])
        raised_ref[h] = (start_ref[h] - both[:, :size]).astype(bf16)
        output_ref[:, h * size : (h + 1) * size] = both[:, size:]


def compose_body(later_ref, first_ref, out_ref):
    heads, size, _ = later_ref.shape
    for h in range(heads):
        both = dot(later_ref[h, :, :size], first_ref[h])
        out_ref[h, :, :size] = both[:, :size].astype(bf16)
        out_ref[h, :, size:] = (both[:, size:] + later_ref[h, :, size:].astype(f32)).astype(bf16)


def compose(later, first):
    return vmem_call(
        compose_body,
        jax.ShapeDtypeStruct(later.shape, bf16),
        (later, first),
        flops=2 * math.prod(later.shape) * later.shape[1],
        moved=6 * math.prod(later.shape),
    )


def back_body(
    order_ref, near_ref, far_ref, raised_ref, output_ref, gate_ref, gain_ref, weight_ref,
    keep_ref, send_ref, normed,
):
    heads, count, size = raised_ref.shape
    slab_count = order_ref.shape[0]
    slab_rows = count // slab_count
    for h in range(heads):
        lanes = slice(h * size, (h + 1) * size)
        state = dot(near_ref[h, :, :size], far_ref[h]) + near_ref[h, :, size:].astype(f32)
        attended = dot(raised_ref[h], state.astype(bf16)) + output_ref[:, lanes]
        power = jnp.sum(attended * attended, -1, keepdims=True) * (1.0 / size)
        normed[:, lanes] = (
            attended * lax.rsqrt(power + 1e-05) * gain_ref[...] * gate_ref[:, lanes]
        ).astype(bf16)
    ordered = jnp.concatenate(
        [
            normed[pl.ds(pl.multiple_of(order_ref[k] * slab_rows, 16), slab_rows), :]
            for k in range(slab_count)
        ],
        axis=0,
    )
    total = dot(ordered, weight_ref[...])
    half = keep_ref.shape[0]
    keep_ref[...] = total[:half]
    send_ref[...] = total[half:].astype(bf16)


def shards(
    hidden_in,
    qkv_weight,
    conv_weight,
    decay_log,
    dt_bias,
    decay_down,
    decay_up,
    beta_weight,
    gate_down,
    gate_up,
    norm_gain,
    out_weight,
):
    heads, size = decay_log.shape[0], norm_gain.shape[0]
    channels = heads * size
    devices, here = lax.axis_size("head"), lax.axis_index("head")
    slabs = slabs_of(hidden_in, "head")
    rim = rim_of(hidden_in, RIM)
    order = jnp.arange(devices, dtype=jnp.int32) ^ here.astype(jnp.int32)
    beta = jnp.pad(beta_weight, ((0, 0), (0, 128 - heads)))
    small = jnp.concatenate([decay_down, gate_down, beta], axis=1)
    taps = conv_weight.astype(f32).reshape(-1, channels)
    rate = jnp.repeat(jnp.exp(decay_log), size)[None]
    pair, solved, attend, start, gate_low = front(
        order,
        rim,
        slabs,
        qkv_weight.transpose(1, 0, 2),
        small,
        taps,
        rate,
        dt_bias[None],
        decay_up,
        heads,
        size,
    )
    count = start.shape[1]
    raised, output_rows, out_gate = vmem_call(
        rows_body,
        (
            jax.ShapeDtypeStruct((heads, count, size), bf16),
            jax.ShapeDtypeStruct((count, channels), f32),
            jax.ShapeDtypeStruct((count, channels), f32),
        ),
        (attend, solved, start, gate_low, gate_up),
        flops=2 * heads * count * count * 2 * size,
        moved=4 * heads * count * count,
    )
    blocks = lax.axis_size("seq")
    near, far = jnp.zeros_like(pair), jnp.zeros((heads, size, size), bf16)
    distance = 1
    while distance < blocks:
        if 2 * distance < blocks:
            arrived = passed_along(pair, "seq", distance)
            near = arrived if distance == 1 else compose(near, arrived)
            pair = compose(pair, arrived)
        else:
            far = passed_along(pair[:, :, size:], "seq", distance)
            if distance == 1:
                near = jnp.concatenate([jnp.zeros_like(far), far], axis=2)
        distance *= 2
    order_out = jnp.asarray(reversed_order(devices), jnp.int32) ^ here.astype(jnp.int32)
    half = count // 2 if devices > 1 else count
    vm = pl.BlockSpec(memory_space=pltpu.VMEM)
    keep, send = vmem_call(
        back_body,
        (
            jax.ShapeDtypeStruct((half, out_weight.shape[1]), f32),
            jax.ShapeDtypeStruct((half, out_weight.shape[1]), bf16),
        ),
        (order_out, near, far, raised, output_rows, out_gate, norm_gain[None], out_weight),
        scratch=[pltpu.VMEM((count, channels), bf16)],
        in_specs=[pl.BlockSpec(memory_space=pltpu.SMEM)] + [vm] * 7,
        flops=2 * count * channels * out_weight.shape[1],
        moved=2 * channels * out_weight.shape[1],
    )
    for bit in bits_of(devices):
        keep = keep + swapped(send, "head", bit).astype(f32)
        if 2 * bit < devices:
            half = keep.shape[0] // 2
            keep, send = keep[:half], keep[half:].astype(bf16)
    return keep.astype(bf16)


def solution(mesh):
    return jax.shard_map(
        shards,
        mesh=mesh,
        in_specs=(
            P(("seq", "head"), None),
            P(None, None, "head"),
            P(None, None, "head"),
            P("head"),
            P("head"),
            P(),
            P(None, "head"),
            P(None, "head"),
            P(),
            P(None, "head"),
            P(),
            P("head", None),
        ),
        out_specs=P(("seq", "head"), None),
        check_vma=False,
    )
```

```python
import functools
import math

import jax
import jax.numpy as jnp
from jax import lax
from jax.experimental import pallas as pl
from jax.experimental.pallas import tpu as pltpu
from jax.sharding import PartitionSpec as P

RIM = 16
BASE = 16
GROUPS = 2
VMEM_LIMIT = 40 * 1024 * 1024
f32 = jnp.float32
bf16 = jnp.bfloat16


def dot(left, right, contract=((1,), (0,))):
    return lax.dot_general(left, right, (contract, ((), ())), preferred_element_type=f32)


def swapped(block, axis, bit):
    return lax.ppermute(block, axis, [(i, i ^ bit) for i in range(lax.axis_size(axis))])


def bits_of(size):
    assert size & (size - 1) == 0
    return [1 << i for i in range(size.bit_length() - 1)]


def slabs_of(own, axis):
    size = lax.axis_size(axis)
    slabs = {0: own}
    for bit in reversed(bits_of(size)):
        for k in sorted(slabs):
            slabs[k ^ bit] = swapped(slabs[k], axis, bit)
    return [slabs[k] for k in range(size)]


def rim_of(own, row_count):
    heads, seqs = lax.axis_size("head"), lax.axis_size("seq")
    tail = own[own.shape[0] - row_count :]
    rim = jnp.zeros_like(tail)
    for k in range(min(1, heads - 1), heads, 2):
        route = [(s * heads + heads - 1, (s + 1) * heads + k) for s in range(seqs - 1)]
        rim = rim + lax.ppermute(tail, ("seq", "head"), route)
    return rim + swapped(rim, "head", 1) if heads > 1 else rim


def vmem_call(body, out_shape, args, scratch=(), scalars=0, flops=0, moved=0):
    spaces = [pltpu.SMEM] * scalars + [pltpu.VMEM] * (len(args) - scalars)
    return pl.pallas_call(
        body,
        out_shape=out_shape,
        in_specs=[pl.BlockSpec(memory_space=space) for space in spaces],
        out_specs=jax.tree.map(lambda _: pl.BlockSpec(memory_space=pltpu.VMEM), out_shape),
        scratch_shapes=list(scratch),
        compiler_params=pltpu.CompilerParams(vmem_limit_bytes=VMEM_LIMIT),
        cost_estimate=pl.CostEstimate(flops=flops, bytes_accessed=moved, transcendentals=0),
    )(*args)


def front_body(
    slab_count,
    order_ref,
    rim_ref,
    *refs,
):
    slab_refs = refs[:slab_count]
    (
        weight_ref,
        _,
        decay_down_ref,
        gate_down_ref,
        beta_ref,
        taps_ref,
        rate_ref,
        bias_ref,
        decay_up_ref,
        pair_ref,
        solved_ref,
        attend_ref,
        start_ref,
        gate_ref,
        rows_ref,
        projected,
        mixing,
        inverse,
        inverse_low,
    ) = refs[slab_count:]
    slab_rows = slab_refs[0].shape[0]
    heads, size = pair_ref.shape[0], pair_ref.shape[1]
    count = start_ref.shape[1]
    tap_count = taps_ref.shape[0] // 3
    chunk = math.gcd(count, 64)
    chunks = count // chunk

    rows_ref[:RIM, :] = rim_ref[...]
    for k in range(slab_count):
        begin = pl.multiple_of(RIM + order_ref[k] * slab_rows, 16)
        rows_ref[pl.ds(begin, slab_rows), :] = slab_refs[k][...]

    here_rows = rows_ref[RIM:, :]
    rank = decay_up_ref.shape[0]
    low = dot(here_rows, jnp.concatenate([decay_down_ref[...], gate_down_ref[...]], axis=1))
    decay_low = low[:, :rank].astype(bf16)
    gate_ref[...] = low[:, rank:].astype(bf16)
    strength = jax.nn.sigmoid(dot(here_rows, beta_ref[...], ((1,), (1,))))
    raw = dot(decay_low, decay_up_ref[...]) + bias_ref[...]
    softplus = jnp.maximum(raw, 0.0) + jnp.log1p(jnp.exp(-jnp.abs(raw)))
    log_decay = -rate_ref[...] * softplus
    row = lax.broadcasted_iota(jnp.int32, (count, count), 0)
    col = lax.broadcasted_iota(jnp.int32, (count, count), 1)
    lower = jnp.where(row >= col, 1.0, 0.0).astype(bf16)
    high = log_decay.astype(bf16)
    cumulative = dot(lower, high) + dot(lower, (log_decay - high.astype(f32)).astype(bf16))

    convolved = []
    for c in range(3):
        projected[c] = dot(rows_ref[...], weight_ref[c]).astype(bf16).astype(f32)
        total = None
        for i in range(tap_count):
            term = projected[c, pl.ds(RIM - tap_count + 1 + i, count), :] * taps_ref[
                pl.ds(c * tap_count + i, 1), :
            ]
            total = term if total is None else total + term
        convolved.append((total / (1.0 + jnp.exp(-total))).astype(bf16).astype(f32))

    def by_chunk(rows):
        return jnp.concatenate([jnp.broadcast_to(r, (chunk, size)) for r in rows], axis=0)

    eye = row == col
    stops, sides = [], []
    for h in range(heads):
        lanes = slice(h * size, (h + 1) * size)
        queries, keys, values = (part[:, lanes] for part in convolved)
        queries = queries * lax.rsqrt(jnp.sum(queries * queries, -1, keepdims=True) + 1e-06)
        queries = queries * size ** (-0.5)
        keys = keys * lax.rsqrt(jnp.sum(keys * keys, -1, keepdims=True) + 1e-06)
        running = cumulative[:, lanes]
        middles = [running[a * chunk + chunk // 2 : a * chunk + chunk // 2 + 1] for a in range(chunks)]
        middle = by_chunk(middles)
        rise = jnp.exp(running - middle)
        key_rise, query_rise = keys * rise, queries * rise
        key_fall = keys * strength[:, h : h + 1] * jnp.exp(middle - running)
        last = running[count - 1 :]
        stops.append(
            ((key_fall * by_chunk([jnp.exp(last - m) for m in middles])).astype(bf16), jnp.exp(last))
        )
        entry = by_chunk([jnp.exp(m) for m in middles])
        start_ref[h] = query_rise * entry
        sides.append(
            jnp.concatenate([(key_rise * entry).astype(bf16), values.astype(bf16)], axis=1)
        )
        for a in range(chunks):
            here = slice(a * chunk, (a + 1) * chunk)
            left = jnp.concatenate([key_rise[here], query_rise[here]], axis=0).astype(bf16)
            falls = []
            for b in range(chunks):
                there = slice(b * chunk, (b + 1) * chunk)
                if b < a:
                    falls.append(key_fall[there] * jnp.exp(middles[a] - middles[b]))
                elif b == a:
                    falls.append(key_fall[there])
                else:
                    falls.append(jnp.zeros((chunk, size), f32))
            right = jnp.concatenate(falls, axis=0).astype(bf16)
            scores = dot(left, right, ((1,), (1,)))
            mixing[h, here, :] = jnp.where(row[here] > col[here], scores[:chunk], 0.0).astype(bf16)
            attend_ref[h, here, :] = jnp.where(row[here] >= col[here], scores[chunk:], 0.0).astype(
                bf16
            )

    base = math.gcd(count, BASE)
    same = row // base == col // base
    powers = [None] * heads
    for h in range(heads):
        nilpotent = jnp.where(same, -mixing[h].astype(f32), 0.0)
        powers[h] = nilpotent.astype(bf16)
        inverse[h] = jnp.where(eye, 1.0, nilpotent)
    for _ in range(1, (base - 1).bit_length()):
        for h in range(heads):
            powers[h] = dot(powers[h], powers[h]).astype(bf16)
        for h in range(heads):
            inverse[h] = inverse[h] + dot(inverse[h].astype(bf16), powers[h])
    for h in range(heads):
        inverse_low[h] = inverse[h].astype(bf16)
    width = base
    while width < count:
        odd = [slice(i, i + width) for i in range(width, count, 2 * width)]
        pair_mask = jnp.where(
            (row // width % 2 == 1) & (col // width == row // width - 1), 1.0, 0.0
        ).astype(bf16)
        halves = []
        for h in range(heads):
            chosen = jnp.concatenate([inverse_low[h, rows, :] for rows in odd], axis=0)
            halves.append(dot(chosen, mixing[h] * pair_mask).astype(bf16))
        for h in range(heads):
            change = dot(halves[h], inverse_low[h])
            for i, rows in enumerate(odd):
                new = inverse_low[h, rows, :].astype(f32) - change[i * width : (i + 1) * width]
                inverse_low[h, rows, :] = new.astype(bf16)
        width *= 2

    for h in range(heads):
        solved = dot(inverse_low[h], sides[h]).astype(bf16)
        solved_ref[h] = solved
        stop, fade = stops[h]
        moved = dot(stop, solved, ((0,), (0,)))
        diagonal = jnp.where(eye[:size, :size], jnp.broadcast_to(fade, (size, size)), 0.0)
        pair_ref[h, :, :size] = (diagonal - moved[:, :size]).astype(bf16)
        pair_ref[h, :, size:] = moved[:, size:].astype(bf16)


def front(order, rim, slabs, weight, ready, downs, taps, rate, bias, decay_up, heads, size):
    slab_count, slab_rows = len(slabs), slabs[0].shape[0]
    count = slab_count * slab_rows
    width = weight.shape[1]
    channels = heads * size
    args = (order, rim, *slabs, weight, ready, *downs, taps, rate, bias, decay_up)
    return vmem_call(
        functools.partial(front_body, slab_count),
        (
            jax.ShapeDtypeStruct((heads, size, 2 * size), bf16),
            jax.ShapeDtypeStruct((heads, count, 2 * size), bf16),
            jax.ShapeDtypeStruct((heads, count, count), bf16),
            jax.ShapeDtypeStruct((heads, count, size), f32),
            jax.ShapeDtypeStruct((count, decay_up.shape[0]), bf16),
        ),
        args,
        scratch=[
            pltpu.VMEM((RIM + count, width), bf16),
            pltpu.VMEM((3, RIM + count, channels), f32),
            pltpu.VMEM((heads, count, count), bf16),
            pltpu.VMEM((heads, count, count), f32),
            pltpu.VMEM((heads, count, count), bf16),
        ],
        scalars=1,
        flops=2 * count * width * channels * 4,
        moved=2 * 4 * width * channels,
    )


def ready_body(weight_ref, out_ref):
    out_ref[...] = weight_ref[0, :8, :128].astype(f32)


def rows_body(attend_ref, solved_ref, start_ref, low_ref, up_ref, raised_ref, output_ref, gate_ref):
    heads, _, size = start_ref.shape
    gate_ref[...] = jax.nn.sigmoid(dot(low_ref[...], up_ref[...]))
    for h in range(heads):
        both = dot(attend_ref[h], solved_ref[h])
        raised_ref[h] = (start_ref[h] - both[:, :size]).astype(bf16)
        output_ref[:, h * size : (h + 1) * size] = both[:, size:]


def composed(later, first, size):
    both = dot(later[:, :size], first)
    return both[:, :size], both[:, size:] + later[:, size:].astype(f32)


def turn_body(first, last, flag_ref, own_ref, far_ref, near_ref, total_ref, out_ref):
    heads, size, _ = own_ref.shape
    upper = flag_ref[0] == 1

    def put(ref, h, pair):
        if ref.shape[2] == size:
            ref[h] = pair[1].astype(bf16)
        else:
            ref[h, :, :size] = pair[0].astype(bf16)
            ref[h, :, size:] = pair[1].astype(bf16)

    @pl.when(upper)
    def _():
        for h in range(heads):
            put(total_ref, h, composed(own_ref[h], far_ref[h], size))
        for h in range(heads):
            if first:
                out_ref[h] = far_ref[h]
            else:
                put(out_ref, h, composed(near_ref[h], far_ref[h], size))

    @pl.when(jnp.logical_not(upper))
    def _():
        for h in range(heads):
            put(total_ref, h, composed(far_ref[h], own_ref[h], size))
        if first:
            row = lax.broadcasted_iota(jnp.int32, (size, 2 * size), 0)
            col = lax.broadcasted_iota(jnp.int32, (size, 2 * size), 1)
            for h in range(heads):
                out_ref[h] = jnp.where(row == col, 1.0, 0.0).astype(bf16)
        else:
            out_ref[...] = near_ref[...]


def turn(flag, own, far, near, first, last):
    heads, size, width = own.shape
    return vmem_call(
        functools.partial(turn_body, first, last),
        (
            jax.ShapeDtypeStruct((heads, size, size if last else width), bf16),
            jax.ShapeDtypeStruct(own.shape, bf16),
        ),
        (flag, own, far, near),
        scalars=1,
        flops=4 * heads * size * size * width,
        moved=10 * heads * size * width,
    )


def entry_body(flag_ref, near_ref, far_ref, state_ref):
    heads, size, _ = near_ref.shape
    for h in range(heads):
        moved = dot(near_ref[h, :, :size], far_ref[h])
        moved = jnp.where(flag_ref[0] == 1, moved, 0.0) + near_ref[h, :, size:].astype(f32)
        state_ref[h] = moved.astype(bf16)


def entry_state(pair):
    heads, size, width = pair.shape
    bits = bits_of(lax.axis_size("seq"))
    here = lax.axis_index("seq").astype(jnp.int32)
    shift, near = pair, pair
    for i, bit in enumerate(bits[:-1]):
        flag = (here & bit != 0).astype(jnp.int32)[None]
        far = swapped(shift, "seq", bit)
        shift, near = turn(flag, shift, far, near, i == 0, i == len(bits) - 2)
    if not bits:
        return jnp.zeros((heads, size, size), bf16)
    if len(bits) == 1:
        shift = pair[:, :, size:]
        near = jnp.broadcast_to(jnp.eye(size, width, dtype=bf16), pair.shape)
    flag = (here & bits[-1] != 0).astype(jnp.int32)[None]
    return vmem_call(
        entry_body,
        jax.ShapeDtypeStruct((heads, size, size), bf16),
        (flag, near, swapped(shift, "seq", bits[-1])),
        scalars=1,
        flops=2 * heads * size * size * size,
        moved=8 * heads * size * size,
    )


def back_body(groups, place_ref, *refs):
    state_refs = refs[:groups]
    raised_ref, output_ref, gate_ref, gain_ref, weight_ref, keep_ref, *rest = refs[groups:]
    normed = rest[-1]
    size = gain_ref.shape[1]
    slab_rows = keep_ref.shape[0]
    group_heads = state_refs[0].shape[0]
    for k in range(place_ref.shape[0]):
        rows = pl.ds(pl.multiple_of(place_ref[k] * slab_rows, 16), slab_rows)
        for h in range(raised_ref.shape[0]):
            lanes = slice(h * size, (h + 1) * size)
            state = state_refs[h // group_heads][h % group_heads]
            attended = dot(raised_ref[h, rows, :], state) + output_ref[rows, lanes]
            power = jnp.sum(attended * attended, -1, keepdims=True) * (1.0 / size)
            normed[k * slab_rows : (k + 1) * slab_rows, lanes] = (
                attended * lax.rsqrt(power + 1e-05) * gain_ref[...] * gate_ref[rows, lanes]
            ).astype(bf16)
    total = dot(normed[...], weight_ref[...])
    keep_ref[...] = total[:slab_rows]
    if len(rest) > 1:
        rest[0][...] = total[slab_rows:].astype(bf16)


def back(places, states, raised, output_rows, out_gate, gain, weight, slab_rows):
    slab_count, width = places.shape[0], weight.shape[1]
    shapes = [jax.ShapeDtypeStruct((slab_rows, width), f32)]
    if slab_count > 1:
        shapes.append(jax.ShapeDtypeStruct((slab_rows, width), bf16))
    return vmem_call(
        functools.partial(back_body, len(states)),
        shapes,
        (places, *states, raised, output_rows, out_gate, gain, weight),
        scratch=[pltpu.VMEM((slab_count * slab_rows, weight.shape[0]), bf16)],
        scalars=1,
        flops=2 * slab_count * slab_rows * weight.shape[0] * width,
        moved=2 * weight.shape[0] * width,
    )


def shards(
    hidden_in,
    qkv_weight,
    conv_weight,
    decay_log,
    dt_bias,
    decay_down,
    decay_up,
    beta_weight,
    gate_down,
    gate_up,
    norm_gain,
    out_weight,
):
    heads, size = decay_log.shape[0], norm_gain.shape[0]
    channels = heads * size
    devices, here = lax.axis_size("head"), lax.axis_index("head").astype(jnp.int32)
    order = jnp.arange(devices, dtype=jnp.int32) ^ here
    weight = qkv_weight.transpose(1, 0, 2)
    ready = vmem_call(
        ready_body, jax.ShapeDtypeStruct((8, 128), f32), (weight,), moved=2 * weight.size
    )
    slabs = slabs_of(hidden_in, "head")
    rim = rim_of(hidden_in, RIM)
    taps = conv_weight.astype(f32).reshape(-1, channels)
    rate = jnp.repeat(jnp.exp(decay_log), size)[None]
    pair, solved, attend, start, gate_low = front(
        order,
        rim,
        slabs,
        weight,
        ready,
        (decay_down, gate_down, beta_weight.T),
        taps,
        rate,
        dt_bias[None],
        decay_up,
        heads,
        size,
    )
    count = start.shape[1]
    raised, output_rows, out_gate = vmem_call(
        rows_body,
        (
            jax.ShapeDtypeStruct((heads, count, size), bf16),
            jax.ShapeDtypeStruct((count, channels), f32),
            jax.ShapeDtypeStruct((count, channels), f32),
        ),
        (attend, solved, start, gate_low, gate_up),
        flops=2 * heads * count * count * 2 * size,
        moved=4 * heads * count * count,
    )
    step = max(heads // GROUPS, 1)
    states = [entry_state(pair[h : h + step]) for h in range(0, heads, step)]
    slab_rows = count // devices
    sums = {}
    for g in reversed(range(max(devices // 2, 1))):
        places = jnp.asarray([2 * g, 2 * g + 1][:devices], jnp.int32) ^ here
        keep, *send = back(
            places, states, raised, output_rows, out_gate, norm_gain[None], out_weight, slab_rows
        )
        sums[g] = [keep] + [swapped(part, "head", 1).astype(f32) for part in send]
    for bit in bits_of(devices)[1:]:
        for g in sorted(sums):
            if 2 * g & bit:
                arrived = swapped(sum(sums.pop(g)).astype(bf16), "head", bit)
                sums[g ^ bit // 2].append(arrived.astype(f32))
    return sum(sums[0]).astype(bf16)


def solution(mesh):
    return jax.shard_map(
        shards,
        mesh=mesh,
        in_specs=(
            P(("seq", "head"), None),
            P(None, None, "head"),
            P(None, None, "head"),
            P("head"),
            P("head"),
            P(),
            P(None, "head"),
            P(None, "head"),
            P(),
            P(None, "head"),
            P(),
            P("head", None),
        ),
        out_specs=P(("seq", "head"), None),
        check_vma=False,
    )
```

```python
import functools
import math

import jax
import jax.numpy as jnp
from jax import lax
from jax.experimental import pallas as pl
from jax.experimental.pallas import tpu as pltpu
from jax.sharding import PartitionSpec as P

RIM = 16
BASE = 16
MIB = 1024 * 1024
f32 = jnp.float32
bf16 = jnp.bfloat16


def dot(left, right, contract=((1,), (0,))):
    return lax.dot_general(left, right, (contract, ((), ())), preferred_element_type=f32)


def swapped(block, axis, bit):
    return lax.ppermute(block, axis, [(i, i ^ bit) for i in range(lax.axis_size(axis))])


def bits_of(size):
    assert size & (size - 1) == 0
    return [1 << i for i in range(size.bit_length() - 1)]


def gathered(own, row_count):
    heads, seqs = lax.axis_size("head"), lax.axis_size("seq")
    slabs = {0: own}
    for bit in reversed(bits_of(heads)[1:]):
        for k in sorted(slabs):
            slabs[k ^ bit] = swapped(slabs[k], "head", bit)
    tail = own[own.shape[0] - row_count :]
    rim = jnp.zeros_like(tail)
    for k in range(min(1, heads - 1), heads, 2):
        route = [(s * heads + heads - 1, (s + 1) * heads + k) for s in range(seqs - 1)]
        rim = rim + lax.ppermute(tail, ("seq", "head"), route)
    if heads > 1:
        slabs[1] = swapped(own, "head", 1)
        arrived = [k for k in sorted(slabs) if k > 1]
        moved, rim = lax.optimization_barrier(([slabs[k] for k in arrived], rim))
        for k, slab in zip(arrived, moved):
            slabs[k], slabs[k ^ 1] = slab, swapped(slab, "head", 1)
        rim = rim + swapped(rim, "head", 1)
    return [slabs[k] for k in range(heads)], rim


def vmem_call(body, out_shape, args, scratch=(), hbm=0, grant=4, flops=0, moved=0):
    here = len(args) - hbm
    args = [pltpu.with_memory_space_constraint(a, pltpu.HBM) if i >= here else a for i, a in enumerate(args)]
    spaces = [pltpu.VMEM] * here + [pltpu.HBM] * hbm
    return pl.pallas_call(
        body,
        out_shape=out_shape,
        in_specs=[pl.BlockSpec(memory_space=space) for space in spaces],
        out_specs=jax.tree.map(lambda _: pl.BlockSpec(memory_space=pltpu.VMEM), out_shape),
        scratch_shapes=list(scratch),
        compiler_params=pltpu.CompilerParams(vmem_limit_bytes=grant * MIB),
        cost_estimate=pl.CostEstimate(flops=flops, bytes_accessed=moved, transcendentals=0),
    )(*args)


def place(axis, bit=None):
    here = lax.axis_index(axis)
    return here if bit is None else here // bit % 2


def front_body(slab_count, *refs):
    arrived_refs, refs = refs[:slab_count], refs[slab_count:]
    hbm_refs, refs = refs[:9], refs[9:]
    (own_ref, other_ref, solved_ref, attend_ref, start_ref, gate_ref), refs = refs[:6], refs[6:]
    loaded, refs = refs[:8], refs[8:]
    rows_ref, projected, mixing, inverse, inverse_low, sems = refs
    rates, decay_down_ref, gate_down_ref, beta_ref, decay_up_ref, bias_ref, conv_ref, weights = loaded
    hidden_ref, weight_ref = hbm_refs[0], hbm_refs[-1]
    rim_ref, *slab_refs = arrived_refs
    slab_rows = hidden_ref.shape[0]
    heads, count, size = start_ref.shape
    tap_count = conv_ref.shape[1]
    chunk = math.gcd(count, 64)
    chunks = count // chunk
    here = place("head")

    def rows_of(k):
        return pl.ds(pl.multiple_of(RIM + (here ^ k) * slab_rows, 16), slab_rows)

    firsts = [pltpu.make_async_copy(hidden_ref, rows_ref.at[rows_of(0)], sems.at[0])]
    for i in range(7):
        firsts.append(pltpu.make_async_copy(hbm_refs[1 + i], loaded[i], sems.at[1 + i]))
    pieces = [slice(i, i + 2 * size) for i in range(0, heads * size, 2 * size)]
    loads = {}
    for c in range(3):
        for piece in pieces:
            loads[c, piece.start] = pltpu.make_async_copy(
                weight_ref.at[c, :, piece], weights.at[c, :, piece], sems.at[8 + len(loads)]
            )
    for copy in firsts + list(loads.values()):
        copy.start()
    rows_ref[:RIM, :] = rim_ref[...]
    for k, ref in enumerate(slab_refs):
        rows_ref[rows_of(k + 1), :] = ref[...]
    for copy in firsts:
        copy.wait()

    here_rows = rows_ref[RIM:, :]
    rank = decay_up_ref.shape[0]
    low = dot(here_rows, jnp.concatenate([decay_down_ref[...], gate_down_ref[...]], axis=1))
    decay_low = low[:, :rank].astype(bf16)
    gate_ref[...] = low[:, rank:].astype(bf16)
    strength = jax.nn.sigmoid(dot(here_rows, beta_ref[...], ((1,), (1,))))
    raw = dot(decay_low, decay_up_ref[...]) + bias_ref[...]
    rate = jnp.concatenate(
        [jnp.exp(jnp.full((1, size), rates[h], f32)) for h in range(heads)], axis=1
    )
    softplus = jnp.maximum(raw, 0.0) + jnp.log1p(jnp.exp(-jnp.abs(raw)))
    log_decay = -rate * softplus
    row = lax.broadcasted_iota(jnp.int32, (count, count), 0)
    col = lax.broadcasted_iota(jnp.int32, (count, count), 1)
    lower = jnp.where(row >= col, 1.0, 0.0).astype(bf16)
    high = log_decay.astype(bf16)
    cumulative = dot(lower, high) + dot(lower, (log_decay - high.astype(f32)).astype(bf16))

    convolved = []
    for c in range(3):
        parts = []
        taps = conv_ref[c].astype(f32)
        for piece in pieces:
            loads[c, piece.start].wait()
            projected[c, :, piece] = (
                dot(rows_ref[...], weights[c, :, piece]).astype(bf16).astype(f32)
            )
            total = None
            for i in range(tap_count):
                shifted = projected[c, pl.ds(RIM - tap_count + 1 + i, count), piece]
                term = shifted * taps[i : i + 1, piece]
                total = term if total is None else total + term
            parts.append((total / (1.0 + jnp.exp(-total))).astype(bf16).astype(f32))
        convolved.append(jnp.concatenate(parts, axis=1))

    def by_chunk(rows):
        return jnp.concatenate([jnp.broadcast_to(r, (chunk, size)) for r in rows], axis=0)

    eye = row == col
    stops, sides = [], []
    for h in range(heads):
        lanes = slice(h * size, (h + 1) * size)
        queries, keys, values = (part[:, lanes] for part in convolved)
        queries = queries * lax.rsqrt(jnp.sum(queries * queries, -1, keepdims=True) + 1e-06)
        queries = queries * size ** (-0.5)
        keys = keys * lax.rsqrt(jnp.sum(keys * keys, -1, keepdims=True) + 1e-06)
        running = cumulative[:, lanes]
        middles = [running[a * chunk + chunk // 2 : a * chunk + chunk // 2 + 1] for a in range(chunks)]
        middle = by_chunk(middles)
        rise = jnp.exp(running - middle)
        key_rise, query_rise = keys * rise, queries * rise
        key_fall = keys * strength[:, h : h + 1] * jnp.exp(middle - running)
        last = running[count - 1 :]
        stops.append(
            ((key_fall * by_chunk([jnp.exp(last - m) for m in middles])).astype(bf16), jnp.exp(last))
        )
        entry = by_chunk([jnp.exp(m) for m in middles])
        start_ref[h] = query_rise * entry
        sides.append(
            jnp.concatenate([(key_rise * entry).astype(bf16), values.astype(bf16)], axis=1)
        )
        for a in range(chunks):
            here = slice(a * chunk, (a + 1) * chunk)
            left = jnp.concatenate([key_rise[here], query_rise[here]], axis=0).astype(bf16)
            falls = []
            for b in range(chunks):
                there = slice(b * chunk, (b + 1) * chunk)
                if b < a:
                    falls.append(key_fall[there] * jnp.exp(middles[a] - middles[b]))
                elif b == a:
                    falls.append(key_fall[there])
                else:
                    falls.append(jnp.zeros((chunk, size), f32))
            right = jnp.concatenate(falls, axis=0).astype(bf16)
            scores = dot(left, right, ((1,), (1,)))
            mixing[h, here, :] = jnp.where(row[here] > col[here], scores[:chunk], 0.0).astype(bf16)
            attend_ref[h, here, :] = jnp.where(row[here] >= col[here], scores[chunk:], 0.0).astype(
                bf16
            )

    base = math.gcd(count, BASE)
    same = row // base == col // base
    powers = [None] * heads
    for h in range(heads):
        nilpotent = jnp.where(same, -mixing[h].astype(f32), 0.0)
        powers[h] = nilpotent.astype(bf16)
        inverse[h] = jnp.where(eye, 1.0, nilpotent)
    for _ in range(1, (base - 1).bit_length()):
        for h in range(heads):
            powers[h] = dot(powers[h], powers[h]).astype(bf16)
        for h in range(heads):
            inverse[h] = inverse[h] + dot(inverse[h].astype(bf16), powers[h])
    for h in range(heads):
        inverse_low[h] = inverse[h].astype(bf16)
    width = base
    while width < count:
        odd = [slice(i, i + width) for i in range(width, count, 2 * width)]
        pair_mask = jnp.where(
            (row // width % 2 == 1) & (col // width == row // width - 1), 1.0, 0.0
        ).astype(bf16)
        halves = []
        for h in range(heads):
            chosen = jnp.concatenate([inverse_low[h, rows, :] for rows in odd], axis=0)
            halves.append(dot(chosen, mixing[h] * pair_mask).astype(bf16))
        for h in range(heads):
            change = dot(halves[h], inverse_low[h])
            for i, rows in enumerate(odd):
                new = inverse_low[h, rows, :].astype(f32) - change[i * width : (i + 1) * width]
                inverse_low[h, rows, :] = new.astype(bf16)
        width *= 2

    pairs = []
    for h in range(heads):
        solved = dot(inverse_low[h], sides[h]).astype(bf16)
        solved_ref[h] = solved
        stop, fade = stops[h]
        moved = dot(stop, solved, ((0,), (0,)))
        diagonal = jnp.where(eye[:size, :size], jnp.broadcast_to(fade, (size, size)), 0.0)
        pairs.append(jnp.concatenate([diagonal - moved[:, :size], moved[:, size:]], axis=1))
    upper = place("seq", 1) == 1
    for h in range(heads // 2):
        low, high = pairs[h], pairs[heads // 2 + h]
        own_ref[h] = jnp.where(upper, high, low).astype(bf16)
        other_ref[h] = jnp.where(upper, low, high).astype(bf16)


def front(rim, slabs, loaded, weight, size):
    slab_count, slab_rows = len(slabs), slabs[0].shape[0]
    count = slab_count * slab_rows
    _, width, channels = weight.shape
    heads = channels // size
    rank = loaded[1].shape[1]
    buffers = [pltpu.SMEM(loaded[0].shape, f32)]
    buffers += [pltpu.VMEM(part.shape, part.dtype) for part in (*loaded[1:], weight)]
    return vmem_call(
        functools.partial(front_body, slab_count),
        (
            jax.ShapeDtypeStruct((heads // 2, size, 2 * size), bf16),
            jax.ShapeDtypeStruct((heads // 2, size, 2 * size), bf16),
            jax.ShapeDtypeStruct((heads, count, 2 * size), bf16),
            jax.ShapeDtypeStruct((heads, count, count), bf16),
            jax.ShapeDtypeStruct((heads, count, size), f32),
            jax.ShapeDtypeStruct((count, rank), bf16),
        ),
        (rim, *slabs[1:], slabs[0], *loaded, weight),
        scratch=[
            *buffers,
            pltpu.VMEM((RIM + count, width), bf16),
            pltpu.VMEM((3, RIM + count, channels), f32),
            pltpu.VMEM((heads, count, count), bf16),
            pltpu.VMEM((heads, count, count), f32),
            pltpu.VMEM((heads, count, count), bf16),
            pltpu.SemaphoreType.DMA((8 + 3 * pl.cdiv(heads, 2),)),
        ],
        hbm=2 + len(loaded),
        grant=24,
        flops=2 * count * width * channels * 4,
        moved=2 * 4 * width * channels,
    )


def rows_body(attend_ref, solved_ref, start_ref, low_ref, up_ref, raised_ref, output_ref, gate_ref):
    heads, _, size = start_ref.shape
    gate_ref[...] = jax.nn.sigmoid(dot(low_ref[...], up_ref[...]))
    for h in range(heads):
        both = dot(attend_ref[h], solved_ref[h])
        raised_ref[h] = (start_ref[h] - both[:, :size]).astype(bf16)
        output_ref[:, h * size : (h + 1) * size] = both[:, size:]


def composed(later, first, size):
    both = dot(later[:, :size], first)
    return both[:, :size], both[:, size:] + later[:, size:].astype(f32)


def put(ref, h, pair):
    size = ref.shape[1]
    if ref.shape[2] > size:
        ref[h, :, :size] = pair[0].astype(bf16)
    ref[h, :, ref.shape[2] - size :] = pair[1].astype(bf16)


def join_body(bit, own_ref, far_ref, total_ref):
    heads, size, _ = own_ref.shape
    for h in range(heads):
        own, far = own_ref[h], far_ref[h]
        upper = place("seq", bit) == 1
        later, first = jnp.where(upper, own, far), jnp.where(upper, far, own)
        put(total_ref, h, composed(later, first, size))


def join(bit, own, far, last):
    heads, size, width = own.shape
    return vmem_call(
        functools.partial(join_body, bit),
        jax.ShapeDtypeStruct((heads, size, size if last else width), bf16),
        (own, far),
        flops=2 * heads * size * size * width,
        moved=6 * heads * size * width,
    )


def before_body(bit, near_ref, far_ref, out_ref):
    heads, size, _ = near_ref.shape
    for h in range(heads):
        near = near_ref[h]
        pair = jnp.concatenate(composed(near, far_ref[h], size), axis=1)
        out_ref[h] = jnp.where(place("seq", bit) == 1, pair, near.astype(f32)).astype(bf16)


def before(bit, near, far):
    return vmem_call(
        functools.partial(before_body, bit),
        jax.ShapeDtypeStruct(near.shape, bf16),
        (near, far),
        flops=2 * math.prod(near.shape) * near.shape[1],
        moved=6 * math.prod(near.shape),
    )


def entry_body(bit, near_ref, far_ref, own_ref, partner_ref, keep_ref, send_ref):
    heads, size, _ = near_ref.shape
    arrived, upper = place("seq", bit) == 1, place("seq", 1) == 1
    for h in range(heads):
        state = dot(near_ref[h, :, :size], far_ref[h])
        state = jnp.where(arrived, state, 0.0) + near_ref[h, :, size:].astype(f32)
        first = jnp.where(upper, partner_ref[h], own_ref[h])
        state = state.astype(bf16)
        later = dot(first[:, :size], state) + first[:, size:].astype(f32)
        later = later.astype(bf16)
        keep_ref[h] = jnp.where(upper, later, state)
        send_ref[h] = jnp.where(upper, state, later)


def entry_states(own, other):
    heads, size, width = own.shape
    bits = bits_of(lax.axis_size("seq"))
    partner = swapped(other, "seq", 1)
    total = join(1, own, partner, len(bits) == 2)
    near = jnp.broadcast_to(jnp.eye(size, width, dtype=bf16), own.shape)
    for bit in bits[1:-1]:
        far = swapped(total, "seq", bit)
        total = join(bit, total, far, 2 * bit == bits[-1])
        near = before(bit, near, far)
    far = swapped(total, "seq", bits[-1])
    state = jax.ShapeDtypeStruct((heads, size, size), bf16)
    keep, send = vmem_call(
        functools.partial(entry_body, bits[-1]),
        (state, state),
        (near, far, own, partner),
        flops=4 * heads * size * size * size,
        moved=14 * heads * size * size,
    )
    return keep, swapped(send, "seq", 1)


def back_body(
    places, own_ref, other_ref, raised_ref, output_ref, gate_ref, gain_ref, weight_ref, keep_ref,
    *rest,
):
    normed = rest[-1]
    size = gain_ref.shape[1]
    slab_rows = keep_ref.shape[0]
    half = own_ref.shape[0]
    upper = place("seq", 1) == 1
    for k, away in enumerate(places):
        rows = pl.ds(pl.multiple_of((place("head") ^ away) * slab_rows, 16), slab_rows)
        for h in range(raised_ref.shape[0]):
            lanes = slice(h * size, (h + 1) * size)
            own, other = own_ref[h % half], other_ref[h % half]
            state = jnp.where(upper, other, own) if h < half else jnp.where(upper, own, other)
            attended = dot(raised_ref[h, rows, :], state) + output_ref[rows, lanes]
            power = jnp.sum(attended * attended, -1, keepdims=True) * (1.0 / size)
            normed[k * slab_rows : (k + 1) * slab_rows, lanes] = (
                attended * lax.rsqrt(power + 1e-05) * gain_ref[...] * gate_ref[rows, lanes]
            ).astype(bf16)
    total = dot(normed[...], weight_ref[...])
    keep_ref[...] = total[:slab_rows]
    if len(rest) > 1:
        rest[0][...] = total[slab_rows:].astype(bf16)


def back(places, states, raised, output_rows, out_gate, gain, weight, slab_rows):
    slab_count, width = len(places), weight.shape[1]
    shapes = [jax.ShapeDtypeStruct((slab_rows, width), f32)]
    if slab_count > 1:
        shapes.append(jax.ShapeDtypeStruct((slab_rows, width), bf16))
    return vmem_call(
        functools.partial(back_body, places),
        shapes,
        (*states, raised, output_rows, out_gate, gain, weight),
        scratch=[pltpu.VMEM((slab_count * slab_rows, weight.shape[0]), bf16)],
        grant=10,
        flops=2 * slab_count * slab_rows * weight.shape[0] * width,
        moved=2 * weight.shape[0] * width,
    )


def shards(
    hidden_in,
    qkv_weight,
    conv_weight,
    decay_log,
    dt_bias,
    decay_down,
    decay_up,
    beta_weight,
    gate_down,
    gate_up,
    norm_gain,
    out_weight,
):
    heads, size = decay_log.shape[0], norm_gain.shape[0]
    channels = heads * size
    devices = lax.axis_size("head")
    slabs, rim = gathered(hidden_in, RIM)
    own, other, solved, attend, start, gate_low = front(
        rim,
        slabs,
        (decay_log, decay_down, gate_down, beta_weight.T, decay_up, dt_bias[None], conv_weight),
        qkv_weight.transpose(1, 0, 2),
        size,
    )
    count = start.shape[1]
    raised, output_rows, out_gate = vmem_call(
        rows_body,
        (
            jax.ShapeDtypeStruct((heads, count, size), bf16),
            jax.ShapeDtypeStruct((count, channels), f32),
            jax.ShapeDtypeStruct((count, channels), f32),
        ),
        (attend, solved, start, gate_low, gate_up),
        grant=8,
        flops=2 * heads * count * count * 2 * size,
        moved=4 * heads * count * count,
    )
    states = entry_states(own, other)
    slab_rows = count // devices
    sums = {}
    for g in reversed(range(max(devices // 2, 1))):
        places = [2 * g, 2 * g + 1][:devices]
        keep, *send = back(
            places, states, raised, output_rows, out_gate, norm_gain[None], out_weight, slab_rows
        )
        sums[g] = [keep] + [swapped(part, "head", 1).astype(f32) for part in send]
    for bit in bits_of(devices)[1:]:
        for g in sorted(sums):
            if 2 * g & bit:
                arrived = swapped(sum(sums.pop(g)).astype(bf16), "head", bit)
                sums[g ^ bit // 2].append(arrived.astype(f32))
    return sum(sums[0]).astype(bf16)


def solution(mesh):
    return jax.shard_map(
        shards,
        mesh=mesh,
        in_specs=(
            P(("seq", "head"), None),
            P(None, None, "head"),
            P(None, None, "head"),
            P("head"),
            P("head"),
            P(),
            P(None, "head"),
            P(None, "head"),
            P(),
            P(None, "head"),
            P(),
            P("head", None),
        ),
        out_specs=P(("seq", "head"), None),
        check_vma=False,
    )
```

```python
import functools
import math

import jax
import jax.numpy as jnp
from jax import lax
from jax.experimental import pallas as pl
from jax.experimental.pallas import tpu as pltpu
from jax.sharding import PartitionSpec as P

RIM = 16
BASE = 16
MIB = 1024 * 1024
f32 = jnp.float32
bf16 = jnp.bfloat16


def dot(left, right, contract=((1,), (0,))):
    return lax.dot_general(left, right, (contract, ((), ())), preferred_element_type=f32)


def swapped(block, axis, bit):
    return lax.ppermute(block, axis, [(i, i ^ bit) for i in range(lax.axis_size(axis))])


def bits_of(size):
    assert size & (size - 1) == 0
    return [1 << i for i in range(size.bit_length() - 1)]


def tail_body(own_ref, tail_ref):
    tail_ref[...] = own_ref[own_ref.shape[0] - tail_ref.shape[0] :, :]


def tail_of(own, row_count):
    return vmem_call(tail_body, jax.ShapeDtypeStruct((row_count, own.shape[1]), own.dtype), (own,))


def rim_at_last(tail):
    heads, seqs = lax.axis_size("head"), lax.axis_size("seq")
    swaps = []
    for parity in range(2):
        route = []
        for s in range(parity, seqs - 1, 2):
            one, two = s * heads + heads - 1, (s + 1) * heads + heads - 1
            route += [(one, two), (two, one)]
        swaps.append(lax.ppermute(tail, ("seq", "head"), route))
    return jnp.where(lax.axis_index("seq") % 2 == 1, swaps[0], swaps[1])


def gathered(own, row_count, early):
    bits = bits_of(lax.axis_size("head"))
    assert bits
    slabs = {0: own}
    for bit in reversed(bits[1:]):
        for k in sorted(slabs):
            slabs[k ^ bit] = swapped(slabs[k], "head", bit)
    rim = rim_at_last(tail_of(own, row_count))
    slabs[1] = swapped(own, "head", 1)
    arrived = [k for k in sorted(slabs) if k > 1]
    moved, rim, done = lax.optimization_barrier(
        ([slabs[k] for k in arrived], rim, early(slabs[0], slabs[1]))
    )
    for k, slab in zip(arrived, moved):
        slabs[k], slabs[k ^ 1] = slab, swapped(slab, "head", 1)
    for bit in reversed(bits):
        rim = rim + swapped(rim, "head", bit)
    return [slabs[k] for k in range(2, 2 ** len(bits))], rim, done


def vmem_call(body, out_shape, args, scratch=(), hbm=0, grant=4, flops=0, moved=0):
    here = len(args) - hbm
    args = [pltpu.with_memory_space_constraint(a, pltpu.HBM) if i >= here else a for i, a in enumerate(args)]
    spaces = [pltpu.VMEM] * here + [pltpu.HBM] * hbm
    return pl.pallas_call(
        body,
        out_shape=out_shape,
        in_specs=[pl.BlockSpec(memory_space=space) for space in spaces],
        out_specs=jax.tree.map(lambda _: pl.BlockSpec(memory_space=pltpu.VMEM), out_shape),
        scratch_shapes=list(scratch),
        compiler_params=pltpu.CompilerParams(vmem_limit_bytes=grant * MIB),
        cost_estimate=pl.CostEstimate(flops=flops, bytes_accessed=moved, transcendentals=0),
    )(*args)


def place(axis, bit=None):
    here = lax.axis_index(axis)
    return here if bit is None else here // bit % 2


def column_pieces(width):
    step = math.gcd(width, 256)
    return [slice(i, i + step) for i in range(0, width, step)]


def early_body(
    near_ref, hidden_ref, decay_down_ref, gate_down_ref, beta_ref, weight_ref,
    weights, downs, betas, projected_ref, low_ref, strength_ref, rows_ref, sems,
):
    slab_rows, rank = hidden_ref.shape[0], decay_down_ref.shape[1]
    firsts = [
        pltpu.make_async_copy(hidden_ref, rows_ref.at[pl.ds(0, slab_rows)], sems.at[0]),
        pltpu.make_async_copy(decay_down_ref, downs.at[:, pl.ds(0, rank)], sems.at[1]),
        pltpu.make_async_copy(gate_down_ref, downs.at[:, pl.ds(rank, rank)], sems.at[2]),
        pltpu.make_async_copy(beta_ref, betas, sems.at[3]),
    ]
    pieces = column_pieces(weight_ref.shape[2])
    loads = {}
    for c in range(3):
        for piece in pieces:
            loads[c, piece.start] = pltpu.make_async_copy(
                weight_ref.at[c, :, piece], weights.at[c, :, piece], sems.at[4 + len(loads)]
            )
    for copy in firsts + list(loads.values()):
        copy.start()
    rows_ref[slab_rows:, :] = near_ref[...]
    for copy in firsts:
        copy.wait()
    low_ref[...] = dot(rows_ref[...], downs[...]).astype(bf16)
    strength_ref[...] = dot(rows_ref[...], betas[...], ((1,), (1,)))
    for c in range(3):
        for piece in pieces:
            loads[c, piece.start].wait()
            projected_ref[c, :, piece] = dot(rows_ref[...], weights[c, :, piece]).astype(bf16)


def early(own, near, decay_down, gate_down, beta, weight):
    slab_rows, width = own.shape
    channels, rank, count = weight.shape[2], decay_down.shape[1], 2 * slab_rows
    return vmem_call(
        early_body,
        (
            jax.ShapeDtypeStruct(weight.shape, bf16),
            jax.ShapeDtypeStruct((width, 2 * rank), bf16),
            jax.ShapeDtypeStruct(beta.shape, bf16),
            jax.ShapeDtypeStruct((3, count, channels), bf16),
            jax.ShapeDtypeStruct((count, 2 * rank), bf16),
            jax.ShapeDtypeStruct((count, beta.shape[0]), f32),
        ),
        (near, own, decay_down, gate_down, beta, weight),
        scratch=[
            pltpu.VMEM((count, width), bf16),
            pltpu.SemaphoreType.DMA((4 + 3 * len(column_pieces(channels)),)),
        ],
        hbm=5,
        grant=14,
        flops=1024,
        moved=1024,
    )


def front_body(slab_count, *refs):
    rim_ref, slab_refs, refs = refs[0], refs[1 : slab_count - 1], refs[slab_count - 1 :]
    (weights, downs, betas, pair_ref, pair_low_ref, pair_strength_ref), refs = refs[:6], refs[6:]
    hbm_refs, refs = refs[:4], refs[4:]
    (own_ref, other_ref, solved_ref, attend_ref, start_ref, gate_ref), refs = refs[:6], refs[6:]
    loaded, refs = refs[:4], refs[4:]
    rows_ref, projected, low_ref, strength_ref, mixing, inverse, inverse_low, sems = refs
    rates, decay_up_ref, bias_ref, conv_ref = loaded
    heads, count, size = start_ref.shape
    slab_rows = count // slab_count
    tap_count = conv_ref.shape[1]
    chunk = math.gcd(count, 64)
    chunks = count // chunk
    here = place("head")
    copies = [pltpu.make_async_copy(hbm_refs[i], loaded[i], sems.at[i]) for i in range(4)]
    for copy in copies:
        copy.start()

    def rows_of(k, above=0):
        return pl.ds(pl.multiple_of(above + (here ^ k) * slab_rows, 16), slab_rows)

    rows_ref[:RIM, :] = rim_ref[...]
    for k, ref in enumerate(slab_refs):
        rows_ref[RIM + k * slab_rows : RIM + (k + 1) * slab_rows, :] = ref[...]
    for k in range(2):
        part = slice(k * slab_rows, (k + 1) * slab_rows)
        low_ref[rows_of(k), :] = pair_low_ref[part, :]
        strength_ref[rows_of(k), :] = pair_strength_ref[part, :]
        for c in range(3):
            projected[c, rows_of(k, RIM), :] = pair_ref[c, part, :].astype(f32)
    far_low = dot(rows_ref[RIM:, :], downs[...]).astype(bf16)
    far_strength = dot(rows_ref[RIM:, :], betas[...], ((1,), (1,)))
    for k in range(2, slab_count):
        part = slice((k - 2) * slab_rows, (k - 1) * slab_rows)
        low_ref[rows_of(k), :] = far_low[part]
        strength_ref[rows_of(k), :] = far_strength[part]
    for copy in copies:
        copy.wait()
    rank = decay_up_ref.shape[0]
    low = low_ref[...]
    decay_low = low[:, :rank]
    gate_ref[...] = low[:, rank:]
    strength = jax.nn.sigmoid(strength_ref[...])
    raw = dot(decay_low, decay_up_ref[...]) + bias_ref[...]
    rate = jnp.concatenate(
        [jnp.exp(jnp.full((1, size), rates[h], f32)) for h in range(heads)], axis=1
    )
    softplus = jnp.maximum(raw, 0.0) + jnp.log1p(jnp.exp(-jnp.abs(raw)))
    log_decay = -rate * softplus
    row = lax.broadcasted_iota(jnp.int32, (count, count), 0)
    col = lax.broadcasted_iota(jnp.int32, (count, count), 1)
    lower = jnp.where(row >= col, 1.0, 0.0).astype(bf16)
    high = log_decay.astype(bf16)
    cumulative = dot(lower, high) + dot(lower, (log_decay - high.astype(f32)).astype(bf16))

    convolved = []
    for c in range(3):
        parts = []
        taps = conv_ref[c].astype(f32)
        for piece in column_pieces(heads * size):
            part = dot(rows_ref[...], weights[c, :, piece]).astype(bf16).astype(f32)
            projected[c, :RIM, piece] = part[:RIM]
            for k in range(2, slab_count):
                begin = RIM + (k - 2) * slab_rows
                projected[c, rows_of(k, RIM), piece] = part[begin : begin + slab_rows]
            total = None
            for i in range(tap_count):
                shifted = projected[c, pl.ds(RIM - tap_count + 1 + i, count), piece]
                term = shifted * taps[i : i + 1, piece]
                total = term if total is None else total + term
            parts.append((total / (1.0 + jnp.exp(-total))).astype(bf16).astype(f32))
        convolved.append(jnp.concatenate(parts, axis=1))

    def by_chunk(rows):
        return jnp.concatenate([jnp.broadcast_to(r, (chunk, size)) for r in rows], axis=0)

    eye = row == col
    stops, sides = [], []
    for h in range(heads):
        lanes = slice(h * size, (h + 1) * size)
        queries, keys, values = (part[:, lanes] for part in convolved)
        queries = queries * lax.rsqrt(jnp.sum(queries * queries, -1, keepdims=True) + 1e-06)
        queries = queries * size ** (-0.5)
        keys = keys * lax.rsqrt(jnp.sum(keys * keys, -1, keepdims=True) + 1e-06)
        running = cumulative[:, lanes]
        middles = [running[a * chunk + chunk // 2 : a * chunk + chunk // 2 + 1] for a in range(chunks)]
        middle = by_chunk(middles)
        rise = jnp.exp(running - middle)
        key_rise, query_rise = keys * rise, queries * rise
        key_fall = keys * strength[:, h : h + 1] * jnp.exp(middle - running)
        last = running[count - 1 :]
        stops.append(
            ((key_fall * by_chunk([jnp.exp(last - m) for m in middles])).astype(bf16), jnp.exp(last))
        )
        entry = by_chunk([jnp.exp(m) for m in middles])
        start_ref[h] = query_rise * entry
        sides.append(
            jnp.concatenate([(key_rise * entry).astype(bf16), values.astype(bf16)], axis=1)
        )
        for a in range(chunks):
            here = slice(a * chunk, (a + 1) * chunk)
            left = jnp.concatenate([key_rise[here], query_rise[here]], axis=0).astype(bf16)
            falls = []
            for b in range(chunks):
                there = slice(b * chunk, (b + 1) * chunk)
                if b < a:
                    falls.append(key_fall[there] * jnp.exp(middles[a] - middles[b]))
                elif b == a:
                    falls.append(key_fall[there])
                else:
                    falls.append(jnp.zeros((chunk, size), f32))
            right = jnp.concatenate(falls, axis=0).astype(bf16)
            scores = dot(left, right, ((1,), (1,)))
            mixing[h, here, :] = jnp.where(row[here] > col[here], scores[:chunk], 0.0).astype(bf16)
            attend_ref[h, here, :] = jnp.where(row[here] >= col[here], scores[chunk:], 0.0).astype(
                bf16
            )

    base = math.gcd(count, BASE)
    same = row // base == col // base
    powers = [None] * heads
    for h in range(heads):
        nilpotent = jnp.where(same, -mixing[h].astype(f32), 0.0)
        powers[h] = nilpotent.astype(bf16)
        inverse[h] = jnp.where(eye, 1.0, nilpotent)
    for _ in range(1, (base - 1).bit_length()):
        for h in range(heads):
            powers[h] = dot(powers[h], powers[h]).astype(bf16)
        for h in range(heads):
            inverse[h] = inverse[h] + dot(inverse[h].astype(bf16), powers[h])
    for h in range(heads):
        inverse_low[h] = inverse[h].astype(bf16)
    width = base
    while width < count:
        odd = [slice(i, i + width) for i in range(width, count, 2 * width)]
        pair_mask = jnp.where(
            (row // width % 2 == 1) & (col // width == row // width - 1), 1.0, 0.0
        ).astype(bf16)
        halves = []
        for h in range(heads):
            chosen = jnp.concatenate([inverse_low[h, rows, :] for rows in odd], axis=0)
            halves.append(dot(chosen, mixing[h] * pair_mask).astype(bf16))
        for h in range(heads):
            change = dot(halves[h], inverse_low[h])
            for i, rows in enumerate(odd):
                new = inverse_low[h, rows, :].astype(f32) - change[i * width : (i + 1) * width]
                inverse_low[h, rows, :] = new.astype(bf16)
        width *= 2

    pairs = []
    for h in range(heads):
        solved = dot(inverse_low[h], sides[h]).astype(bf16)
        solved_ref[h] = solved
        stop, fade = stops[h]
        moved = dot(stop, solved, ((0,), (0,)))
        diagonal = jnp.where(eye[:size, :size], jnp.broadcast_to(fade, (size, size)), 0.0)
        pairs.append(jnp.concatenate([diagonal - moved[:, :size], moved[:, size:]], axis=1))
    upper = place("seq", 1) == 1
    for h in range(heads // 2):
        low, high = pairs[h], pairs[heads // 2 + h]
        own_ref[h] = jnp.where(upper, high, low).astype(bf16)
        other_ref[h] = jnp.where(upper, low, high).astype(bf16)


def front(rim, slabs, fetched, loaded, size):
    weight, downs = fetched[:2]
    slab_count, slab_rows = 2 + len(slabs), fetched[3].shape[1] // 2
    count = slab_count * slab_rows
    _, width, channels = weight.shape
    heads = channels // size
    buffers = [pltpu.SMEM(loaded[0].shape, f32)]
    buffers += [pltpu.VMEM(part.shape, part.dtype) for part in loaded[1:]]
    return vmem_call(
        functools.partial(front_body, slab_count),
        (
            jax.ShapeDtypeStruct((heads // 2, size, 2 * size), bf16),
            jax.ShapeDtypeStruct((heads // 2, size, 2 * size), bf16),
            jax.ShapeDtypeStruct((heads, count, 2 * size), bf16),
            jax.ShapeDtypeStruct((heads, count, count), bf16),
            jax.ShapeDtypeStruct((heads, count, size), f32),
            jax.ShapeDtypeStruct((count, downs.shape[1] // 2), bf16),
        ),
        (rim, *slabs, *fetched, *loaded),
        scratch=[
            *buffers,
            pltpu.VMEM((RIM + count - 2 * slab_rows, width), bf16),
            pltpu.VMEM((3, RIM + count, channels), f32),
            pltpu.VMEM((count, downs.shape[1]), bf16),
            pltpu.VMEM((count, heads), f32),
            pltpu.VMEM((heads, count, count), bf16),
            pltpu.VMEM((heads, count, count), f32),
            pltpu.VMEM((heads, count, count), bf16),
            pltpu.SemaphoreType.DMA((len(loaded),)),
        ],
        hbm=len(loaded),
        grant=24,
        flops=2 * count * width * channels * 4,
        moved=2 * 4 * width * channels,
    )


def rows_body(attend_ref, solved_ref, start_ref, low_ref, up_ref, raised_ref, output_ref, gate_ref):
    heads, _, size = start_ref.shape
    gate_ref[...] = jax.nn.sigmoid(dot(low_ref[...], up_ref[...]))
    for h in range(heads):
        both = dot(attend_ref[h], solved_ref[h])
        raised_ref[h] = (start_ref[h] - both[:, :size]).astype(bf16)
        output_ref[:, h * size : (h + 1) * size] = both[:, size:]


def composed(later, first, size):
    both = dot(later[:, :size], first)
    return both[:, :size], both[:, size:] + later[:, size:].astype(f32)


def put(ref, h, pair):
    size = ref.shape[1]
    if ref.shape[2] > size:
        ref[h, :, :size] = pair[0].astype(bf16)
    ref[h, :, ref.shape[2] - size :] = pair[1].astype(bf16)


def join_body(bit, own_ref, far_ref, total_ref):
    heads, size, _ = own_ref.shape
    for h in range(heads):
        own, far = own_ref[h], far_ref[h]
        upper = place("seq", bit) == 1
        later, first = jnp.where(upper, own, far), jnp.where(upper, far, own)
        put(total_ref, h, composed(later, first, size))


def join(bit, own, far, last):
    heads, size, width = own.shape
    return vmem_call(
        functools.partial(join_body, bit),
        jax.ShapeDtypeStruct((heads, size, size if last else width), bf16),
        (own, far),
        flops=2 * heads * size * size * width,
        moved=6 * heads * size * width,
    )


def before_body(bit, near_ref, far_ref, out_ref):
    heads, size, _ = near_ref.shape
    for h in range(heads):
        near = near_ref[h]
        pair = jnp.concatenate(composed(near, far_ref[h], size), axis=1)
        out_ref[h] = jnp.where(place("seq", bit) == 1, pair, near.astype(f32)).astype(bf16)


def before(bit, near, far):
    return vmem_call(
        functools.partial(before_body, bit),
        jax.ShapeDtypeStruct(near.shape, bf16),
        (near, far),
        flops=2 * math.prod(near.shape) * near.shape[1],
        moved=6 * math.prod(near.shape),
    )


def entry_body(bit, near_ref, far_ref, own_ref, partner_ref, keep_ref, send_ref):
    heads, size, _ = near_ref.shape
    arrived, upper = place("seq", bit) == 1, place("seq", 1) == 1
    for h in range(heads):
        state = dot(near_ref[h, :, :size], far_ref[h])
        state = jnp.where(arrived, state, 0.0) + near_ref[h, :, size:].astype(f32)
        first = jnp.where(upper, partner_ref[h], own_ref[h])
        state = state.astype(bf16)
        later = dot(first[:, :size], state) + first[:, size:].astype(f32)
        later = later.astype(bf16)
        keep_ref[h] = jnp.where(upper, later, state)
        send_ref[h] = jnp.where(upper, state, later)


def entry_states(own, other):
    heads, size, width = own.shape
    bits = bits_of(lax.axis_size("seq"))
    partner = swapped(other, "seq", 1)
    total = join(1, own, partner, len(bits) == 2)
    near = jnp.broadcast_to(jnp.eye(size, width, dtype=bf16), own.shape)
    for bit in bits[1:-1]:
        far = swapped(total, "seq", bit)
        total = join(bit, total, far, 2 * bit == bits[-1])
        near = before(bit, near, far)
    far = swapped(total, "seq", bits[-1])
    state = jax.ShapeDtypeStruct((heads, size, size), bf16)
    keep, send = vmem_call(
        functools.partial(entry_body, bits[-1]),
        (state, state),
        (near, far, own, partner),
        flops=4 * heads * size * size * size,
        moved=14 * heads * size * size,
    )
    return keep, swapped(send, "seq", 1)


def back_body(
    places, own_ref, other_ref, raised_ref, output_ref, gate_ref, gain_ref, weight_ref, keep_ref,
    *rest,
):
    normed = rest[-1]
    size = gain_ref.shape[1]
    slab_rows = keep_ref.shape[0]
    half = own_ref.shape[0]
    upper = place("seq", 1) == 1
    for k, away in enumerate(places):
        rows = pl.ds(pl.multiple_of((place("head") ^ away) * slab_rows, 16), slab_rows)
        for h in range(raised_ref.shape[0]):
            lanes = slice(h * size, (h + 1) * size)
            own, other = own_ref[h % half], other_ref[h % half]
            state = jnp.where(upper, other, own) if h < half else jnp.where(upper, own, other)
            attended = dot(raised_ref[h, rows, :], state) + output_ref[rows, lanes]
            power = jnp.sum(attended * attended, -1, keepdims=True) * (1.0 / size)
            normed[k * slab_rows : (k + 1) * slab_rows, lanes] = (
                attended * lax.rsqrt(power + 1e-05) * gain_ref[...] * gate_ref[rows, lanes]
            ).astype(bf16)
    total = dot(normed[...], weight_ref[...])
    keep_ref[...] = total[:slab_rows]
    if len(rest) > 1:
        rest[0][...] = total[slab_rows:].astype(bf16)


def back(places, states, raised, output_rows, out_gate, gain, weight, slab_rows):
    slab_count, width = len(places), weight.shape[1]
    shapes = [jax.ShapeDtypeStruct((slab_rows, width), f32)]
    if slab_count > 1:
        shapes.append(jax.ShapeDtypeStruct((slab_rows, width), bf16))
    return vmem_call(
        functools.partial(back_body, places),
        shapes,
        (*states, raised, output_rows, out_gate, gain, weight),
        scratch=[pltpu.VMEM((slab_count * slab_rows, weight.shape[0]), bf16)],
        grant=10,
        flops=2 * slab_count * slab_rows * weight.shape[0] * width,
        moved=2 * weight.shape[0] * width,
    )


def shards(
    hidden_in,
    qkv_weight,
    conv_weight,
    decay_log,
    dt_bias,
    decay_down,
    decay_up,
    beta_weight,
    gate_down,
    gate_up,
    norm_gain,
    out_weight,
):
    heads, size = decay_log.shape[0], norm_gain.shape[0]
    channels = heads * size
    devices = lax.axis_size("head")
    weight = qkv_weight.transpose(1, 0, 2)
    slabs, rim, fetched = gathered(
        hidden_in,
        RIM,
        lambda one, two: early(one, two, decay_down, gate_down, beta_weight.T, weight),
    )
    own, other, solved, attend, start, gate_low = front(
        rim, slabs, fetched, (decay_log, decay_up, dt_bias[None], conv_weight), size
    )
    count = start.shape[1]
    raised, output_rows, out_gate = vmem_call(
        rows_body,
        (
            jax.ShapeDtypeStruct((heads, count, size), bf16),
            jax.ShapeDtypeStruct((count, channels), f32),
            jax.ShapeDtypeStruct((count, channels), f32),
        ),
        (attend, solved, start, gate_low, gate_up),
        grant=8,
        flops=2 * heads * count * count * 2 * size,
        moved=4 * heads * count * count,
    )
    states = entry_states(own, other)
    slab_rows = count // devices
    sums = {}
    for g in reversed(range(max(devices // 2, 1))):
        places = [2 * g, 2 * g + 1][:devices]
        keep, *send = back(
            places, states, raised, output_rows, out_gate, norm_gain[None], out_weight, slab_rows
        )
        sums[g] = [keep] + [swapped(part, "head", 1).astype(f32) for part in send]
    for bit in bits_of(devices)[1:]:
        for g in sorted(sums):
            if 2 * g & bit:
                arrived = swapped(sum(sums.pop(g)).astype(bf16), "head", bit)
                sums[g ^ bit // 2].append(arrived.astype(f32))
    return sum(sums[0]).astype(bf16)


def solution(mesh):
    return jax.shard_map(
        shards,
        mesh=mesh,
        in_specs=(
            P(("seq", "head"), None),
            P(None, None, "head"),
            P(None, None, "head"),
            P("head"),
            P("head"),
            P(),
            P(None, "head"),
            P(None, "head"),
            P(),
            P(None, "head"),
            P(),
            P("head", None),
        ),
        out_specs=P(("seq", "head"), None),
        check_vma=False,
    )
```

```python
import functools
import math

import jax
import jax.numpy as jnp
from jax import lax
from jax.experimental import pallas as pl
from jax.experimental.pallas import tpu as pltpu
from jax.sharding import PartitionSpec as P

RIM = 16
BASE = 16
MIB = 1024 * 1024
f32 = jnp.float32
bf16 = jnp.bfloat16


def dot(left, right, contract=((1,), (0,))):
    return lax.dot_general(left, right, (contract, ((), ())), preferred_element_type=f32)


def swapped(block, axis, bit):
    return lax.ppermute(block, axis, [(i, i ^ bit) for i in range(lax.axis_size(axis))])


def bits_of(size):
    assert size & (size - 1) == 0
    return [1 << i for i in range(size.bit_length() - 1)]


def rim_route(target):
    heads, seqs = lax.axis_size("head"), lax.axis_size("seq")
    pairs = [(s * heads + heads - 1, (s + 1) * heads + target) for s in range(seqs - 1)]
    return pairs + [(two, one) for one, two in pairs]


def gathered(own, tail):
    bits = bits_of(lax.axis_size("head"))
    assert bits
    heads, here = lax.axis_size("head"), lax.axis_index("head")
    slabs = {0: own}
    for bit in reversed(bits[1:]):
        for k in sorted(slabs):
            slabs[k ^ bit] = swapped(slabs[k], "head", bit)
    targets = [first if first == heads - 2 else first + 1 for first in range(0, heads, 2)]
    tails = [lax.ppermute(tail, ("seq", "head"), rim_route(target)) for target in targets]
    slabs[1] = swapped(own, "head", 1)
    arrived = [k for k in sorted(slabs) if k > 1]
    moved, tails = lax.optimization_barrier(([slabs[k] for k in arrived], tails))
    rim = jnp.zeros_like(tail)
    for target, received in zip(targets, tails):
        rim = jnp.where(here == target, received, rim)
    for k, slab in zip(arrived, moved):
        slabs[k], slabs[k ^ 1] = slab, swapped(slab, "head", 1)
    rim = rim + swapped(rim, "head", 1)
    return [slabs[k] for k in range(heads)], rim


def vmem_call(body, out_shape, args, scratch=(), hbm=0, grant=4, flops=0, moved=0):
    here = len(args) - hbm
    args = [pltpu.with_memory_space_constraint(a, pltpu.HBM) if i >= here else a for i, a in enumerate(args)]
    spaces = [pltpu.VMEM] * here + [pltpu.HBM] * hbm
    return pl.pallas_call(
        body,
        out_shape=out_shape,
        in_specs=[pl.BlockSpec(memory_space=space) for space in spaces],
        out_specs=jax.tree.map(lambda _: pl.BlockSpec(memory_space=pltpu.VMEM), out_shape),
        scratch_shapes=list(scratch),
        compiler_params=pltpu.CompilerParams(vmem_limit_bytes=grant * MIB),
        cost_estimate=pl.CostEstimate(flops=flops, bytes_accessed=moved, transcendentals=0),
    )(*args)


def place(axis, bit=None):
    here = lax.axis_index(axis)
    return here if bit is None else here // bit % 2


def column_pieces(width):
    step = math.gcd(width, 256)
    return [slice(i, i + step) for i in range(0, width, step)]


def load_body(
    hidden_ref, decay_down_ref, gate_down_ref, beta_ref, weight_ref,
    tail_ref, weights, downs, betas, sems,
):
    first, rank = hidden_ref.shape[0] - tail_ref.shape[0], decay_down_ref.shape[1]
    copies = [
        pltpu.make_async_copy(hidden_ref.at[pl.ds(first, tail_ref.shape[0])], tail_ref, sems.at[0]),
        pltpu.make_async_copy(decay_down_ref, downs.at[:, pl.ds(0, rank)], sems.at[1]),
        pltpu.make_async_copy(gate_down_ref, downs.at[:, pl.ds(rank, rank)], sems.at[2]),
        pltpu.make_async_copy(beta_ref, betas, sems.at[3]),
    ]
    for c in range(2):
        copies.append(pltpu.make_async_copy(weight_ref.at[c], weights.at[c], sems.at[4 + c]))
    for copy in copies:
        copy.start()
    for copy in copies:
        copy.wait()


def load(own, decay_down, gate_down, beta, weight):
    width, rank = decay_down.shape
    return vmem_call(
        load_body,
        (
            jax.ShapeDtypeStruct((RIM, width), bf16),
            jax.ShapeDtypeStruct((2, *weight.shape[1:]), bf16),
            jax.ShapeDtypeStruct((width, 2 * rank), bf16),
            jax.ShapeDtypeStruct(beta.shape, bf16),
        ),
        (own, decay_down, gate_down, beta, weight),
        scratch=[pltpu.SemaphoreType.DMA((6,))],
        hbm=5,
        grant=8,
    )


def front_body(slab_count, *refs):
    (rim_ref, *slab_refs), refs = refs[:slab_count], refs[slab_count:]
    (weights, downs, betas), refs = refs[:3], refs[3:]
    hbm_refs, refs = refs[:6], refs[6:]
    (own_ref, other_ref, solved_ref, attend_ref, start_ref, gate_ref), refs = refs[:6], refs[6:]
    loaded, refs = refs[:5], refs[5:]
    rows_ref, projected, mixing, inverse, sems = refs
    rates, decay_up_ref, bias_ref, conv_ref, value_weight = loaded
    hidden_ref, weight_ref = hbm_refs[0], hbm_refs[-1]
    heads, count, size = start_ref.shape
    slab_rows = count // slab_count
    tap_count = conv_ref.shape[1]
    rank = decay_up_ref.shape[0]
    chunk = math.gcd(count, 64)
    chunks = count // chunk
    block = math.gcd(count, 128)
    blocks = count // block
    here = place("head")

    def rows_of(k):
        return pl.ds(pl.multiple_of(RIM + (here ^ k) * slab_rows, 16), slab_rows)

    fetch = pltpu.make_async_copy(hidden_ref, rows_ref.at[rows_of(0)], sems.at[0])
    small = [pltpu.make_async_copy(hbm_refs[1 + i], loaded[i], sems.at[1 + i]) for i in range(4)]
    pieces = column_pieces(heads * size)
    streams = []
    for i, piece in enumerate(pieces):
        streams.append(
            pltpu.make_async_copy(
                weight_ref.at[2, :, piece], value_weight.at[:, piece], sems.at[5 + i]
            )
        )
    for copy in [fetch] + small + streams:
        copy.start()
    rows_ref[:RIM, :] = rim_ref[...]
    for k, ref in enumerate(slab_refs):
        rows_ref[rows_of(k + 1), :] = ref[...]
    fetch.wait()
    for c in range(2):
        for piece in pieces:
            projected[c, :, piece] = dot(rows_ref[...], weights[c, :, piece])
    low = dot(rows_ref[RIM:, :], downs[...]).astype(bf16)
    gate_ref[...] = low[:, rank:]
    strength = jax.nn.sigmoid(dot(rows_ref[RIM:, :], betas[...], ((1,), (1,))))
    for copy in small:
        copy.wait()
    raw = dot(low[:, :rank], decay_up_ref[...]) + bias_ref[...]
    softplus = jnp.maximum(raw, 0.0) + jnp.log(1.0 + jnp.exp(-jnp.abs(raw)))
    rate = jnp.concatenate(
        [jnp.exp(jnp.full((1, size), rates[h], f32)) for h in range(heads)], axis=1
    )
    log_decay = -rate * softplus
    row = lax.broadcasted_iota(jnp.int32, (count, count), 0)
    col = lax.broadcasted_iota(jnp.int32, (count, count), 1)
    lower = jnp.where(row >= col, 1.0, 0.0).astype(bf16)

    def exact(left, right):
        high = right.astype(bf16)
        return dot(left, high) + dot(left, (right - high.astype(f32)).astype(bf16))

    cumulative = exact(lower, log_decay)
    spread = lax.broadcasted_iota(jnp.int32, (heads, heads * size), 1) // size
    spread = spread == lax.broadcasted_iota(jnp.int32, (heads, heads * size), 0)
    spread = jnp.where(spread, 1.0, 0.0).astype(bf16)
    high = strength.astype(bf16)
    strengths = dot(high, spread) + dot((strength - high.astype(f32)).astype(bf16), spread)
    for i, piece in enumerate(pieces):
        streams[i].wait()
        projected[2, :, piece] = dot(rows_ref[...], value_weight[:, piece])

    def convolved(c, lanes):
        taps = conv_ref[c].astype(f32)
        total = None
        for i in range(tap_count):
            shifted = projected[c, pl.ds(RIM - tap_count + 1 + i, count), lanes]
            term = shifted * taps[i : i + 1, lanes]
            total = term if total is None else total + term
        half = 0.5 * total
        return half + half * jnp.tanh(half)

    def by_chunk(rows):
        return jnp.concatenate([jnp.broadcast_to(r, (chunk, size)) for r in rows], axis=0)

    ones = jnp.full((size, size), 1.0, bf16)
    scaled = jnp.full((size, size), float(size), bf16)
    stops, sides = [], []
    for h in range(heads):
        lanes = slice(h * size, (h + 1) * size)
        queries, keys, values = (convolved(c, lanes) for c in range(3))
        power = dot((queries * queries).astype(bf16), scaled)
        queries = queries * lax.rsqrt(power + size * 1e-06)
        power = dot((keys * keys).astype(bf16), ones)
        keys = keys * lax.rsqrt(power + 1e-06)
        running = cumulative[:, lanes]
        middles = [running[a * chunk + chunk // 2 : a * chunk + chunk // 2 + 1] for a in range(chunks)]
        above = running - by_chunk(middles)
        rise = jnp.exp(above)
        key_rise, query_rise = keys * rise, queries * rise
        key_fall = keys * strengths[:, lanes] * jnp.exp(-above)
        last = running[count - 1 :]
        stops.append(
            ((key_fall * by_chunk([jnp.exp(last - m) for m in middles])).astype(bf16), jnp.exp(last))
        )
        entry = by_chunk([jnp.exp(m) for m in middles])
        start_ref[h] = (query_rise * entry).astype(bf16)
        sides.append(
            jnp.concatenate([(key_rise * entry).astype(bf16), values.astype(bf16)], axis=1)
        )
        key_rise, query_rise = key_rise.astype(bf16), query_rise.astype(bf16)
        for a in range(chunks):
            rows = slice(a * chunk, (a + 1) * chunk)
            left = jnp.concatenate([key_rise[rows], query_rise[rows]], axis=0)
            reach = (a * chunk // block + 1) * block
            falls = []
            for b in range(reach // chunk):
                there = slice(b * chunk, (b + 1) * chunk)
                if b < a:
                    falls.append(key_fall[there] * jnp.exp(middles[a] - middles[b]))
                elif b == a:
                    falls.append(key_fall[there])
                else:
                    falls.append(jnp.zeros((chunk, size), f32))
            right = jnp.concatenate(falls, axis=0).astype(bf16)
            scores = dot(left, right, ((1,), (1,)))
            inside = slice(reach - block, reach)
            if reach > block:
                before = slice(0, reach - block)
                mixing[h, rows, before] = scores[:chunk, before].astype(bf16)
                attend_ref[h, rows, before] = scores[chunk:, before].astype(bf16)
            at, to = row[rows, inside], col[rows, inside]
            mixing[h, rows, inside] = jnp.where(at > to, scores[:chunk, inside], 0.0).astype(bf16)
            attend_ref[h, rows, inside] = jnp.where(
                at >= to, scores[chunk:, inside], 0.0
            ).astype(bf16)

    at, to = row[:block, :block], col[:block, :block]
    eye = jnp.where(at == to, 1.0, 0.0).astype(bf16)
    base = math.gcd(block, BASE)
    near = jnp.where(at // base == to // base, -1.0, 0.0).astype(bf16)
    corners = [(h, slice(d * block, (d + 1) * block)) for h in range(heads) for d in range(blocks)]
    powers = [mixing[h, d, d] * near for h, d in corners]
    totals = [power + eye for power in powers]
    for _ in range(1, (base - 1).bit_length()):
        powers = [dot(power, power).astype(bf16) for power in powers]
        totals = [dot(t, power + eye).astype(bf16) for t, power in zip(totals, powers)]
    for (h, d), total in zip(corners, totals):
        inverse[h, d, :] = total
    width = base
    while width < block:
        odd = range(width, block, 2 * width)
        pair_mask = (at // width % 2 == 1) & (to // width == at // width - 1)
        pair_mask = jnp.where(pair_mask, 1.0, 0.0).astype(bf16)
        halves = []
        for h, d in corners:
            parts = [inverse[h, d.start + i : d.start + i + width, :] for i in odd]
            chosen = jnp.concatenate(parts, axis=0)
            halves.append((chosen, dot(chosen, mixing[h, d, d] * pair_mask).astype(bf16)))
        for (h, d), (chosen, half) in zip(corners, halves):
            new = (chosen.astype(f32) - dot(half, inverse[h, d, :])).astype(bf16)
            for n, i in enumerate(odd):
                inverse[h, d.start + i : d.start + i + width, :] = new[n * width : (n + 1) * width]
        width *= 2

    for d in range(blocks):
        rows = slice(d * block, (d + 1) * block)
        for h in range(heads):
            side = sides[h][rows]
            if d:
                done = solved_ref[h, : d * block, :]
                side = (side.astype(f32) - dot(mixing[h, rows, : d * block], done)).astype(bf16)
            solved_ref[h, rows, :] = dot(inverse[h, rows, :], side).astype(bf16)
    pairs = []
    unit = row[:size, :size] == col[:size, :size]
    for h in range(heads):
        stop, fade = stops[h]
        moved = dot(stop, solved_ref[h], ((0,), (0,)))
        diagonal = jnp.where(unit, jnp.broadcast_to(fade, (size, size)), 0.0)
        pairs.append(jnp.concatenate([diagonal - moved[:, :size], moved[:, size:]], axis=1))
    upper = place("seq", 1) == 1
    for h in range(heads // 2):
        low, high = pairs[h], pairs[heads // 2 + h]
        own_ref[h] = jnp.where(upper, high, low).astype(bf16)
        other_ref[h] = jnp.where(upper, low, high).astype(bf16)


def front(rim, slabs, fetched, loaded, weight, size):
    slab_count, slab_rows = len(slabs), slabs[0].shape[0]
    count = slab_count * slab_rows
    _, width, channels = weight.shape
    heads, block = channels // size, math.gcd(count, 128)
    buffers = [pltpu.SMEM(loaded[0].shape, f32)]
    buffers += [pltpu.VMEM(part.shape, part.dtype) for part in loaded[1:]]
    return vmem_call(
        functools.partial(front_body, slab_count),
        (
            jax.ShapeDtypeStruct((heads // 2, size, 2 * size), bf16),
            jax.ShapeDtypeStruct((heads // 2, size, 2 * size), bf16),
            jax.ShapeDtypeStruct((heads, count, 2 * size), bf16),
            jax.ShapeDtypeStruct((heads, count, count), bf16),
            jax.ShapeDtypeStruct((heads, count, size), bf16),
            jax.ShapeDtypeStruct((count, fetched[1].shape[1] // 2), bf16),
        ),
        (rim, *slabs[1:], *fetched, slabs[0], *loaded, weight),
        scratch=[
            *buffers,
            pltpu.VMEM((width, channels), bf16),
            pltpu.VMEM((RIM + count, width), bf16),
            pltpu.VMEM((3, RIM + count, channels), f32),
            pltpu.VMEM((heads, count, count), bf16),
            pltpu.VMEM((heads, count, block), bf16),
            pltpu.SemaphoreType.DMA((5 + len(column_pieces(channels)),)),
        ],
        hbm=2 + len(loaded),
        grant=24,
        flops=2 * count * width * channels * 4,
        moved=2 * 4 * width * channels,
    )


def rows_body(attend_ref, solved_ref, start_ref, low_ref, up_ref, raised_ref, output_ref, gate_ref):
    heads, _, size = start_ref.shape
    gate_ref[...] = jax.nn.sigmoid(dot(low_ref[...], up_ref[...]))
    count = attend_ref.shape[1]
    block = math.gcd(count, 128)
    for h in range(heads):
        for begin in range(0, count, block):
            rows, reach = slice(begin, begin + block), slice(0, begin + block)
            both = dot(attend_ref[h, rows, reach], solved_ref[h, reach, :])
            raised_ref[h, rows, :] = (start_ref[h, rows, :].astype(f32) - both[:, :size]).astype(bf16)
            output_ref[rows, h * size : (h + 1) * size] = both[:, size:]


def composed(later, first, size):
    both = dot(later[:, :size], first)
    return both[:, :size], both[:, size:] + later[:, size:].astype(f32)


def put(ref, h, pair):
    size = ref.shape[1]
    if ref.shape[2] > size:
        ref[h, :, :size] = pair[0].astype(bf16)
    ref[h, :, ref.shape[2] - size :] = pair[1].astype(bf16)


def join_body(bit, own_ref, far_ref, total_ref):
    heads, size, _ = own_ref.shape
    for h in range(heads):
        own, far = own_ref[h], far_ref[h]
        upper = place("seq", bit) == 1
        later, first = jnp.where(upper, own, far), jnp.where(upper, far, own)
        put(total_ref, h, composed(later, first, size))


def join(bit, own, far, last):
    heads, size, width = own.shape
    return vmem_call(
        functools.partial(join_body, bit),
        jax.ShapeDtypeStruct((heads, size, size if last else width), bf16),
        (own, far),
        flops=2 * heads * size * size * width,
        moved=6 * heads * size * width,
    )


def before_body(bit, near_ref, far_ref, out_ref):
    heads, size, _ = near_ref.shape
    for h in range(heads):
        near = near_ref[h]
        pair = jnp.concatenate(composed(near, far_ref[h], size), axis=1)
        out_ref[h] = jnp.where(place("seq", bit) == 1, pair, near.astype(f32)).astype(bf16)


def before(bit, near, far):
    return vmem_call(
        functools.partial(before_body, bit),
        jax.ShapeDtypeStruct(near.shape, bf16),
        (near, far),
        flops=2 * math.prod(near.shape) * near.shape[1],
        moved=6 * math.prod(near.shape),
    )


def entry_body(bit, near_ref, far_ref, own_ref, partner_ref, keep_ref, send_ref):
    heads, size, _ = near_ref.shape
    arrived, upper = place("seq", bit) == 1, place("seq", 1) == 1
    for h in range(heads):
        state = dot(near_ref[h, :, :size], far_ref[h])
        state = jnp.where(arrived, state, 0.0) + near_ref[h, :, size:].astype(f32)
        first = jnp.where(upper, partner_ref[h], own_ref[h])
        state = state.astype(bf16)
        later = dot(first[:, :size], state) + first[:, size:].astype(f32)
        later = later.astype(bf16)
        keep_ref[h] = jnp.where(upper, later, state)
        send_ref[h] = jnp.where(upper, state, later)


def entry_states(own, other):
    heads, size, width = own.shape
    bits = bits_of(lax.axis_size("seq"))
    partner = swapped(other, "seq", 1)
    total = join(1, own, partner, len(bits) == 2)
    near = jnp.broadcast_to(jnp.eye(size, width, dtype=bf16), own.shape)
    for bit in bits[1:-1]:
        far = swapped(total, "seq", bit)
        total = join(bit, total, far, 2 * bit == bits[-1])
        near = before(bit, near, far)
    far = swapped(total, "seq", bits[-1])
    state = jax.ShapeDtypeStruct((heads, size, size), bf16)
    keep, send = vmem_call(
        functools.partial(entry_body, bits[-1]),
        (state, state),
        (near, far, own, partner),
        flops=4 * heads * size * size * size,
        moved=14 * heads * size * size,
    )
    return keep, swapped(send, "seq", 1)


def back_body(
    places, own_ref, other_ref, raised_ref, output_ref, gate_ref, gain_ref, weight_ref, keep_ref,
    *rest,
):
    normed = rest[-1]
    size = gain_ref.shape[1]
    slab_rows = keep_ref.shape[0]
    half = own_ref.shape[0]
    upper = place("seq", 1) == 1
    for k, away in enumerate(places):
        rows = pl.ds(pl.multiple_of((place("head") ^ away) * slab_rows, 16), slab_rows)
        for h in range(raised_ref.shape[0]):
            lanes = slice(h * size, (h + 1) * size)
            own, other = own_ref[h % half], other_ref[h % half]
            state = jnp.where(upper, other, own) if h < half else jnp.where(upper, own, other)
            attended = dot(raised_ref[h, rows, :], state) + output_ref[rows, lanes]
            power = jnp.sum(attended * attended, -1, keepdims=True) * (1.0 / size)
            normed[k * slab_rows : (k + 1) * slab_rows, lanes] = (
                attended * lax.rsqrt(power + 1e-05) * gain_ref[...] * gate_ref[rows, lanes]
            ).astype(bf16)
    total = dot(normed[...], weight_ref[...])
    keep_ref[...] = total[:slab_rows]
    if len(rest) > 1:
        rest[0][...] = total[slab_rows:].astype(bf16)


def back(places, states, raised, output_rows, out_gate, gain, weight, slab_rows):
    slab_count, width = len(places), weight.shape[1]
    shapes = [jax.ShapeDtypeStruct((slab_rows, width), f32)]
    if slab_count > 1:
        shapes.append(jax.ShapeDtypeStruct((slab_rows, width), bf16))
    return vmem_call(
        functools.partial(back_body, places),
        shapes,
        (*states, raised, output_rows, out_gate, gain, weight),
        scratch=[pltpu.VMEM((slab_count * slab_rows, weight.shape[0]), bf16)],
        grant=10,
        flops=2 * slab_count * slab_rows * weight.shape[0] * width,
        moved=2 * weight.shape[0] * width,
    )


def shards(
    hidden_in,
    qkv_weight,
    conv_weight,
    decay_log,
    dt_bias,
    decay_down,
    decay_up,
    beta_weight,
    gate_down,
    gate_up,
    norm_gain,
    out_weight,
):
    heads, size = decay_log.shape[0], norm_gain.shape[0]
    channels = heads * size
    devices = lax.axis_size("head")
    weight = qkv_weight.transpose(1, 0, 2)
    tail, *fetched = load(hidden_in, decay_down, gate_down, beta_weight.T, weight)
    slabs, rim = gathered(hidden_in, tail)
    own, other, solved, attend, start, gate_low = front(
        rim, slabs, fetched, (decay_log, decay_up, dt_bias[None], conv_weight), weight, size
    )
    count = start.shape[1]
    raised, output_rows, out_gate = vmem_call(
        rows_body,
        (
            jax.ShapeDtypeStruct((heads, count, size), bf16),
            jax.ShapeDtypeStruct((count, channels), f32),
            jax.ShapeDtypeStruct((count, channels), f32),
        ),
        (attend, solved, start, gate_low, gate_up),
        grant=8,
        flops=2 * heads * count * count * 2 * size,
        moved=4 * heads * count * count,
    )
    states = entry_states(own, other)
    slab_rows = count // devices
    sums = {}
    for g in reversed(range(max(devices // 2, 1))):
        places = [2 * g, 2 * g + 1][:devices]
        keep, *send = back(
            places, states, raised, output_rows, out_gate, norm_gain[None], out_weight, slab_rows
        )
        sums[g] = [keep] + [swapped(part, "head", 1).astype(f32) for part in send]
    for bit in bits_of(devices)[1:]:
        for g in sorted(sums):
            if 2 * g & bit:
                arrived = swapped(sum(sums.pop(g)).astype(bf16), "head", bit)
                sums[g ^ bit // 2].append(arrived.astype(f32))
    return sum(sums[0]).astype(bf16)


def solution(mesh):
    return jax.shard_map(
        shards,
        mesh=mesh,
        in_specs=(
            P(("seq", "head"), None),
            P(None, None, "head"),
            P(None, None, "head"),
            P("head"),
            P("head"),
            P(),
            P(None, "head"),
            P(None, "head"),
            P(),
            P(None, "head"),
            P(),
            P("head", None),
        ),
        out_specs=P(("seq", "head"), None),
        check_vma=False,
    )
```

```python
import functools
import math

import jax
import jax.numpy as jnp
from jax import lax
from jax.experimental import pallas as pl
from jax.experimental.pallas import tpu as pltpu
from jax.sharding import PartitionSpec as P

RIM = 16
BASE = 16
MIB = 1024 * 1024
f32 = jnp.float32
bf16 = jnp.bfloat16


def dot(left, right, contract=((1,), (0,))):
    return lax.dot_general(left, right, (contract, ((), ())), preferred_element_type=f32)


def swapped(block, axis, bit):
    return lax.ppermute(block, axis, [(i, i ^ bit) for i in range(lax.axis_size(axis))])


def bits_of(size):
    assert size & (size - 1) == 0
    return [1 << i for i in range(size.bit_length() - 1)]


def rim_route(target):
    heads, seqs = lax.axis_size("head"), lax.axis_size("seq")
    return [(s * heads + heads - 1, (s + 1) * heads + target) for s in range(seqs - 1)]


def pick_body(targets, *refs):
    *tail_refs, rim_ref = refs
    rim = jnp.zeros(rim_ref.shape, f32)
    for target, ref in zip(targets, tail_refs):
        rim = jnp.where(place("head") == target, ref[...].astype(f32), rim)
    rim_ref[...] = rim.astype(rim_ref.dtype)


def gathered(own, loaded):
    heads = lax.axis_size("head")
    bits = bits_of(heads)
    assert bits
    slabs = {0: own}
    for bit in reversed(bits[1:]):
        for k in sorted(slabs):
            slabs[k ^ bit] = swapped(slabs[k], "head", bit)
    tail = own[own.shape[0] - RIM :]
    targets = [first if first == heads - 2 else first + 1 for first in range(0, heads, 2)]
    tails = [lax.ppermute(tail, ("seq", "head"), rim_route(target)) for target in targets]
    slabs[1] = swapped(own, "head", 1)
    arrived = [k for k in sorted(slabs) if k > 1]
    moved, tails, loaded = lax.optimization_barrier(
        ([slabs[k] for k in arrived], tails, loaded)
    )
    for k, slab in zip(arrived, moved):
        slabs[k], slabs[k ^ 1] = slab, swapped(slab, "head", 1)
    rim = vmem_call(
        functools.partial(pick_body, targets), jax.ShapeDtypeStruct(tail.shape, bf16), tails
    )
    return [slabs[k] for k in range(1, heads)], [rim, swapped(rim, "head", 1)], loaded


def vmem_call(body, out_shape, args, scratch=(), hbm=0, grant=4, flops=0, moved=0):
    here = len(args) - hbm
    args = [pltpu.with_memory_space_constraint(a, pltpu.HBM) if i >= here else a for i, a in enumerate(args)]
    spaces = [pltpu.VMEM] * here + [pltpu.HBM] * hbm
    return pl.pallas_call(
        body,
        out_shape=out_shape,
        in_specs=[pl.BlockSpec(memory_space=space) for space in spaces],
        out_specs=jax.tree.map(lambda _: pl.BlockSpec(memory_space=pltpu.VMEM), out_shape),
        scratch_shapes=list(scratch),
        compiler_params=pltpu.CompilerParams(vmem_limit_bytes=grant * MIB),
        cost_estimate=pl.CostEstimate(flops=flops, bytes_accessed=moved, transcendentals=0),
    )(*args)


def place(axis, bit=None):
    here = lax.axis_index(axis)
    return here if bit is None else here // bit % 2


def column_pieces(width):
    step = math.gcd(width, 256)
    return [slice(i, i + step) for i in range(0, width, step)]


def load_body(
    hidden_ref, decay_down_ref, gate_down_ref, beta_ref, weight_ref,
    own_ref, weights, downs, betas, sems,
):
    rank = decay_down_ref.shape[1]
    copies = [
        pltpu.make_async_copy(hidden_ref, own_ref, sems.at[0]),
        pltpu.make_async_copy(decay_down_ref, downs.at[:, pl.ds(0, rank)], sems.at[1]),
        pltpu.make_async_copy(gate_down_ref, downs.at[:, pl.ds(rank, rank)], sems.at[2]),
        pltpu.make_async_copy(beta_ref, betas, sems.at[3]),
    ]
    for c in range(2):
        copies.append(pltpu.make_async_copy(weight_ref.at[c], weights.at[c], sems.at[4 + c]))
    for copy in copies:
        copy.start()
    for copy in copies:
        copy.wait()


def load(own, decay_down, gate_down, beta, weight):
    width, rank = decay_down.shape
    return vmem_call(
        load_body,
        (
            jax.ShapeDtypeStruct(own.shape, bf16),
            jax.ShapeDtypeStruct((2, *weight.shape[1:]), bf16),
            jax.ShapeDtypeStruct((width, 2 * rank), bf16),
            jax.ShapeDtypeStruct(beta.shape, bf16),
        ),
        (own, decay_down, gate_down, beta, weight),
        scratch=[pltpu.SemaphoreType.DMA((6,))],
        hbm=5,
        grant=8,
    )


def front_body(slab_count, *refs):
    (one_ref, two_ref, *slab_refs), refs = refs[: slab_count + 1], refs[slab_count + 1 :]
    (own_rows_ref, weights, downs, betas), refs = refs[:4], refs[4:]
    hbm_refs, refs = refs[:5], refs[5:]
    (own_ref, other_ref, solved_ref, attend_ref, start_ref, gate_ref), refs = refs[:6], refs[6:]
    loaded, refs = refs[:5], refs[5:]
    rows_ref, projected, mixing, inverse, sides, sems = refs
    rates, decay_up_ref, bias_ref, conv_ref, value_weight = loaded
    weight_ref = hbm_refs[-1]
    heads, count, size = start_ref.shape
    slab_rows = count // slab_count
    tap_count = conv_ref.shape[1]
    rank = decay_up_ref.shape[0]
    chunk = math.gcd(count, 64)
    chunks = count // chunk
    block = math.gcd(count, 128)
    blocks = count // block
    here = place("head")

    def rows_of(k):
        return pl.ds(pl.multiple_of(RIM + (here ^ k) * slab_rows, 16), slab_rows)

    small = [pltpu.make_async_copy(hbm_refs[i], loaded[i], sems.at[i]) for i in range(4)]
    pieces = column_pieces(heads * size)
    streams = []
    for i, piece in enumerate(pieces):
        streams.append(
            pltpu.make_async_copy(
                weight_ref.at[2, :, piece], value_weight.at[:, piece], sems.at[4 + i]
            )
        )
    for copy in small + streams:
        copy.start()
    rows_ref[:RIM, :] = (one_ref[...].astype(f32) + two_ref[...].astype(f32)).astype(bf16)
    for k, ref in enumerate([own_rows_ref, *slab_refs]):
        rows_ref[rows_of(k), :] = ref[...]
    for c in range(2):
        for piece in pieces:
            projected[c, :, piece] = dot(rows_ref[...], weights[c, :, piece])
    low = dot(rows_ref[RIM:, :], downs[...]).astype(bf16)
    gate_ref[...] = low[:, rank:]
    strength = jax.nn.sigmoid(dot(rows_ref[RIM:, :], betas[...], ((1,), (1,))))
    for copy in small:
        copy.wait()
    raw = dot(low[:, :rank], decay_up_ref[...]) + bias_ref[...]
    softplus = jnp.maximum(raw, 0.0) + jnp.log(1.0 + jnp.exp(-jnp.abs(raw)))
    rate = jnp.concatenate(
        [jnp.exp(jnp.full((1, size), rates[h], f32)) for h in range(heads)], axis=1
    )
    log_decay = -rate * softplus
    row = lax.broadcasted_iota(jnp.int32, (count, count), 0)
    col = lax.broadcasted_iota(jnp.int32, (count, count), 1)
    lower = jnp.where(row >= col, 1.0, 0.0).astype(bf16)

    def exact(left, right):
        high = right.astype(bf16)
        return dot(left, high) + dot(left, (right - high.astype(f32)).astype(bf16))

    cumulative = exact(lower, log_decay)
    spread = lax.broadcasted_iota(jnp.int32, (heads, heads * size), 1) // size
    spread = spread == lax.broadcasted_iota(jnp.int32, (heads, heads * size), 0)
    spread = jnp.where(spread, 1.0, 0.0).astype(bf16)
    high = strength.astype(bf16)
    strengths = dot(high, spread) + dot((strength - high.astype(f32)).astype(bf16), spread)

    def convolved(c, lanes):
        taps = conv_ref[c].astype(f32)
        total = None
        for i in range(tap_count):
            shifted = projected[c, pl.ds(RIM - tap_count + 1 + i, count), lanes]
            term = shifted * taps[i : i + 1, lanes]
            total = term if total is None else total + term
        half = 0.5 * total
        return half + half * jnp.tanh(half)

    def by_chunk(rows):
        return jnp.concatenate([jnp.broadcast_to(r, (chunk, size)) for r in rows], axis=0)

    ones = jnp.full((size, size), 1.0, bf16)
    scaled = jnp.full((size, size), float(size), bf16)
    stops = []
    for h in range(heads):
        lanes = slice(h * size, (h + 1) * size)
        queries, keys = convolved(0, lanes), convolved(1, lanes)
        power = dot((queries * queries).astype(bf16), scaled)
        queries = queries * lax.rsqrt(power + size * 1e-06)
        power = dot((keys * keys).astype(bf16), ones)
        keys = keys * lax.rsqrt(power + 1e-06)
        running = cumulative[:, lanes]
        middles = [running[a * chunk + chunk // 2 : a * chunk + chunk // 2 + 1] for a in range(chunks)]
        above = running - by_chunk(middles)
        rise = jnp.exp(above)
        key_rise, query_rise = keys * rise, queries * rise
        key_fall = keys * strengths[:, lanes] * jnp.exp(-above)
        last = running[count - 1 :]
        stops.append(
            ((key_fall * by_chunk([jnp.exp(last - m) for m in middles])).astype(bf16), jnp.exp(last))
        )
        entry = by_chunk([jnp.exp(m) for m in middles])
        start_ref[h] = (query_rise * entry).astype(bf16)
        sides[h, :, :size] = (key_rise * entry).astype(bf16)
        key_rise, query_rise = key_rise.astype(bf16), query_rise.astype(bf16)
        for a in range(chunks):
            rows = slice(a * chunk, (a + 1) * chunk)
            left = jnp.concatenate([key_rise[rows], query_rise[rows]], axis=0)
            reach = (a * chunk // block + 1) * block
            falls = []
            for b in range(reach // chunk):
                there = slice(b * chunk, (b + 1) * chunk)
                if b < a:
                    falls.append(key_fall[there] * jnp.exp(middles[a] - middles[b]))
                elif b == a:
                    falls.append(key_fall[there])
                else:
                    falls.append(jnp.zeros((chunk, size), f32))
            right = jnp.concatenate(falls, axis=0).astype(bf16)
            scores = dot(left, right, ((1,), (1,)))
            inside = slice(reach - block, reach)
            if reach > block:
                before = slice(0, reach - block)
                mixing[h, rows, before] = scores[:chunk, before].astype(bf16)
                attend_ref[h, rows, before] = scores[chunk:, before].astype(bf16)
            at, to = row[rows, inside], col[rows, inside]
            mixing[h, rows, inside] = jnp.where(at > to, scores[:chunk, inside], 0.0).astype(bf16)
            attend_ref[h, rows, inside] = jnp.where(
                at >= to, scores[chunk:, inside], 0.0
            ).astype(bf16)

    for i, piece in enumerate(pieces):
        streams[i].wait()
        projected[2, :, piece] = dot(rows_ref[...], value_weight[:, piece])

    at, to = row[:block, :block], col[:block, :block]
    eye = jnp.where(at == to, 1.0, 0.0).astype(bf16)
    base = math.gcd(block, BASE)
    near = jnp.where(at // base == to // base, -1.0, 0.0).astype(bf16)
    corners = [(h, slice(d * block, (d + 1) * block)) for h in range(heads) for d in range(blocks)]
    powers = [mixing[h, d, d] * near for h, d in corners]
    totals = [power + eye for power in powers]
    for _ in range(1, (base - 1).bit_length()):
        powers = [dot(power, power).astype(bf16) for power in powers]
        totals = [dot(t, power + eye).astype(bf16) for t, power in zip(totals, powers)]
    for (h, d), total in zip(corners, totals):
        inverse[h, d, :] = total
    width = base
    while width < block:
        odd = range(width, block, 2 * width)
        pair_mask = (at // width % 2 == 1) & (to // width == at // width - 1)
        pair_mask = jnp.where(pair_mask, 1.0, 0.0).astype(bf16)
        halves = []
        for h, d in corners:
            parts = [inverse[h, d.start + i : d.start + i + width, :] for i in odd]
            chosen = jnp.concatenate(parts, axis=0)
            halves.append((chosen, dot(chosen, mixing[h, d, d] * pair_mask).astype(bf16)))
        for (h, d), (chosen, half) in zip(corners, halves):
            new = (chosen.astype(f32) - dot(half, inverse[h, d, :])).astype(bf16)
            for n, i in enumerate(odd):
                inverse[h, d.start + i : d.start + i + width, :] = new[n * width : (n + 1) * width]
        width *= 2

    for h in range(heads):
        sides[h, :, size:] = convolved(2, slice(h * size, (h + 1) * size)).astype(bf16)
    for d in range(blocks):
        rows = slice(d * block, (d + 1) * block)
        for h in range(heads):
            side = sides[h, rows, :]
            if d:
                done = solved_ref[h, : d * block, :]
                side = (side.astype(f32) - dot(mixing[h, rows, : d * block], done)).astype(bf16)
            solved_ref[h, rows, :] = dot(inverse[h, rows, :], side).astype(bf16)
    pairs = []
    unit = row[:size, :size] == col[:size, :size]
    for h in range(heads):
        stop, fade = stops[h]
        moved = dot(stop, solved_ref[h], ((0,), (0,)))
        diagonal = jnp.where(unit, jnp.broadcast_to(fade, (size, size)), 0.0)
        pairs.append(jnp.concatenate([diagonal - moved[:, :size], moved[:, size:]], axis=1))
    upper = place("seq", 1) == 1
    for h in range(heads // 2):
        low, high = pairs[h], pairs[heads // 2 + h]
        own_ref[h] = jnp.where(upper, high, low).astype(bf16)
        other_ref[h] = jnp.where(upper, low, high).astype(bf16)


def front(rims, slabs, fetched, loaded, weight, size):
    slab_count, slab_rows = 1 + len(slabs), slabs[0].shape[0]
    count = slab_count * slab_rows
    _, width, channels = weight.shape
    heads, block = channels // size, math.gcd(count, 128)
    buffers = [pltpu.SMEM(loaded[0].shape, f32)]
    buffers += [pltpu.VMEM(part.shape, part.dtype) for part in loaded[1:]]
    return vmem_call(
        functools.partial(front_body, slab_count),
        (
            jax.ShapeDtypeStruct((heads // 2, size, 2 * size), bf16),
            jax.ShapeDtypeStruct((heads // 2, size, 2 * size), bf16),
            jax.ShapeDtypeStruct((heads, count, 2 * size), bf16),
            jax.ShapeDtypeStruct((heads, count, count), bf16),
            jax.ShapeDtypeStruct((heads, count, size), bf16),
            jax.ShapeDtypeStruct((count, fetched[2].shape[1] // 2), bf16),
        ),
        (*rims, *slabs, *fetched, *loaded, weight),
        scratch=[
            *buffers,
            pltpu.VMEM((width, channels), bf16),
            pltpu.VMEM((RIM + count, width), bf16),
            pltpu.VMEM((3, RIM + count, channels), f32),
            pltpu.VMEM((heads, count, count), bf16),
            pltpu.VMEM((heads, count, block), bf16),
            pltpu.VMEM((heads, count, 2 * size), bf16),
            pltpu.SemaphoreType.DMA((4 + len(column_pieces(channels)),)),
        ],
        hbm=1 + len(loaded),
        grant=24,
        flops=2 * count * width * channels * 4,
        moved=2 * 4 * width * channels,
    )


def rows_body(attend_ref, solved_ref, start_ref, low_ref, up_ref, raised_ref, output_ref, gate_ref):
    heads, _, size = start_ref.shape
    gate_ref[...] = jax.nn.sigmoid(dot(low_ref[...], up_ref[...]))
    count = attend_ref.shape[1]
    block = math.gcd(count, 128)
    for h in range(heads):
        for begin in range(0, count, block):
            rows, reach = slice(begin, begin + block), slice(0, begin + block)
            both = dot(attend_ref[h, rows, reach], solved_ref[h, reach, :])
            raised_ref[h, rows, :] = (start_ref[h, rows, :].astype(f32) - both[:, :size]).astype(bf16)
            output_ref[rows, h * size : (h + 1) * size] = both[:, size:]


def composed(later, first, size):
    both = dot(later[:, :size], first)
    return both[:, :size], both[:, size:] + later[:, size:].astype(f32)


def put(ref, h, pair):
    size = ref.shape[1]
    if ref.shape[2] > size:
        ref[h, :, :size] = pair[0].astype(bf16)
    ref[h, :, ref.shape[2] - size :] = pair[1].astype(bf16)


def join_body(bit, own_ref, far_ref, total_ref):
    heads, size, _ = own_ref.shape
    for h in range(heads):
        own, far = own_ref[h], far_ref[h]
        upper = place("seq", bit) == 1
        later, first = jnp.where(upper, own, far), jnp.where(upper, far, own)
        put(total_ref, h, composed(later, first, size))


def join(bit, own, far, last):
    heads, size, width = own.shape
    return vmem_call(
        functools.partial(join_body, bit),
        jax.ShapeDtypeStruct((heads, size, size if last else width), bf16),
        (own, far),
        flops=2 * heads * size * size * width,
        moved=6 * heads * size * width,
    )


def before_body(bit, far_ref, *refs):
    *near_refs, out_ref = refs
    heads, size, width = far_ref.shape
    row = lax.broadcasted_iota(jnp.int32, (size, width), 0)
    col = lax.broadcasted_iota(jnp.int32, (size, width), 1)
    for h in range(heads):
        if near_refs:
            near = near_refs[0][h]
            pair = jnp.concatenate(composed(near, far_ref[h], size), axis=1)
            near = near.astype(f32)
        else:
            near, pair = jnp.where(row == col, 1.0, 0.0), far_ref[h].astype(f32)
        out_ref[h] = jnp.where(place("seq", bit) == 1, pair, near).astype(bf16)


def before(bit, near, far):
    return vmem_call(
        functools.partial(before_body, bit),
        jax.ShapeDtypeStruct(far.shape, bf16),
        (far, *near),
        flops=2 * math.prod(far.shape) * far.shape[1],
        moved=6 * math.prod(far.shape),
    )


def entry_body(bit, near_ref, far_ref, own_ref, partner_ref, keep_ref, send_ref):
    heads, size, _ = near_ref.shape
    arrived, upper = place("seq", bit) == 1, place("seq", 1) == 1
    for h in range(heads):
        state = dot(near_ref[h, :, :size], far_ref[h])
        state = jnp.where(arrived, state, 0.0) + near_ref[h, :, size:].astype(f32)
        first = jnp.where(upper, partner_ref[h], own_ref[h])
        state = state.astype(bf16)
        later = dot(first[:, :size], state) + first[:, size:].astype(f32)
        later = later.astype(bf16)
        keep_ref[h] = jnp.where(upper, later, state)
        send_ref[h] = jnp.where(upper, state, later)


def entry_states(own, other):
    heads, size, width = own.shape
    bits = bits_of(lax.axis_size("seq"))
    partner = swapped(other, "seq", 1)
    total = join(1, own, partner, len(bits) == 2)
    near = ()
    assert len(bits) > 2
    for bit in bits[1:-1]:
        far = swapped(total, "seq", bit)
        total = join(bit, total, far, 2 * bit == bits[-1])
        near = (before(bit, near, far),)
    far = swapped(total, "seq", bits[-1])
    state = jax.ShapeDtypeStruct((heads, size, size), bf16)
    keep, send = vmem_call(
        functools.partial(entry_body, bits[-1]),
        (state, state),
        (*near, far, own, partner),
        flops=4 * heads * size * size * size,
        moved=14 * heads * size * size,
    )
    return keep, swapped(send, "seq", 1)


def back_body(
    places, own_ref, other_ref, raised_ref, output_ref, gate_ref, gain_ref, weight_ref, keep_ref,
    *rest,
):
    normed = rest[-1]
    size = gain_ref.shape[1]
    slab_rows = keep_ref.shape[0]
    half = own_ref.shape[0]
    upper = place("seq", 1) == 1
    for k, away in enumerate(places):
        rows = pl.ds(pl.multiple_of((place("head") ^ away) * slab_rows, 16), slab_rows)
        for h in range(raised_ref.shape[0]):
            lanes = slice(h * size, (h + 1) * size)
            own, other = own_ref[h % half], other_ref[h % half]
            state = jnp.where(upper, other, own) if h < half else jnp.where(upper, own, other)
            attended = dot(raised_ref[h, rows, :], state) + output_ref[rows, lanes]
            power = jnp.sum(attended * attended, -1, keepdims=True) * (1.0 / size)
            normed[k * slab_rows : (k + 1) * slab_rows, lanes] = (
                attended * lax.rsqrt(power + 1e-05) * gain_ref[...] * gate_ref[rows, lanes]
            ).astype(bf16)
    total = dot(normed[...], weight_ref[...])
    keep_ref[...] = total[:slab_rows]
    if len(rest) > 1:
        rest[0][...] = total[slab_rows:].astype(bf16)


def back(places, states, raised, output_rows, out_gate, gain, weight, slab_rows):
    slab_count, width = len(places), weight.shape[1]
    shapes = [jax.ShapeDtypeStruct((slab_rows, width), f32)]
    if slab_count > 1:
        shapes.append(jax.ShapeDtypeStruct((slab_rows, width), bf16))
    return vmem_call(
        functools.partial(back_body, places),
        shapes,
        (*states, raised, output_rows, out_gate, gain, weight),
        scratch=[pltpu.VMEM((slab_count * slab_rows, weight.shape[0]), bf16)],
        grant=10,
        flops=2 * slab_count * slab_rows * weight.shape[0] * width,
        moved=2 * weight.shape[0] * width,
    )


def shards(
    hidden_in,
    qkv_weight,
    conv_weight,
    decay_log,
    dt_bias,
    decay_down,
    decay_up,
    beta_weight,
    gate_down,
    gate_up,
    norm_gain,
    out_weight,
):
    heads, size = decay_log.shape[0], norm_gain.shape[0]
    channels = heads * size
    devices = lax.axis_size("head")
    weight = qkv_weight.transpose(1, 0, 2)
    fetched = load(hidden_in, decay_down, gate_down, beta_weight.T, weight)
    slabs, rims, fetched = gathered(hidden_in, fetched)
    own, other, solved, attend, start, gate_low = front(
        rims, slabs, fetched, (decay_log, decay_up, dt_bias[None], conv_weight), weight, size
    )
    count = start.shape[1]
    raised, output_rows, out_gate = vmem_call(
        rows_body,
        (
            jax.ShapeDtypeStruct((heads, count, size), bf16),
            jax.ShapeDtypeStruct((count, channels), f32),
            jax.ShapeDtypeStruct((count, channels), f32),
        ),
        (attend, solved, start, gate_low, gate_up),
        grant=8,
        flops=2 * heads * count * count * 2 * size,
        moved=4 * heads * count * count,
    )
    states = entry_states(own, other)
    slab_rows = count // devices
    sums = {}
    for g in reversed(range(max(devices // 2, 1))):
        places = [2 * g, 2 * g + 1][:devices]
        keep, *send = back(
            places, states, raised, output_rows, out_gate, norm_gain[None], out_weight, slab_rows
        )
        sums[g] = [keep] + [swapped(part, "head", 1).astype(f32) for part in send]
    for bit in bits_of(devices)[1:]:
        for g in sorted(sums):
            if 2 * g & bit:
                arrived = swapped(sum(sums.pop(g)).astype(bf16), "head", bit)
                sums[g ^ bit // 2].append(arrived.astype(f32))
    return sum(sums[0]).astype(bf16)


def solution(mesh):
    return jax.shard_map(
        shards,
        mesh=mesh,
        in_specs=(
            P(("seq", "head"), None),
            P(None, None, "head"),
            P(None, None, "head"),
            P("head"),
            P("head"),
            P(),
            P(None, "head"),
            P(None, "head"),
            P(),
            P(None, "head"),
            P(),
            P("head", None),
        ),
        out_specs=P(("seq", "head"), None),
        check_vma=False,
    )
```

```python
import functools
import math

import jax
import jax.numpy as jnp
from jax import lax
from jax.experimental import pallas as pl
from jax.experimental.pallas import tpu as pltpu
from jax.sharding import PartitionSpec as P

RIM = 16
BASE = 16
MIB = 1024 * 1024
f32 = jnp.float32
bf16 = jnp.bfloat16


def dot(left, right, contract=((1,), (0,))):
    return lax.dot_general(left, right, (contract, ((), ())), preferred_element_type=f32)


def swapped(block, axis, bit):
    return lax.ppermute(block, axis, [(i, i ^ bit) for i in range(lax.axis_size(axis))])


def bits_of(size):
    assert size & (size - 1) == 0
    return [1 << i for i in range(size.bit_length() - 1)]


def rim_route(target):
    heads, seqs = lax.axis_size("head"), lax.axis_size("seq")
    return [(s * heads + heads - 1, (s + 1) * heads + target) for s in range(seqs - 1)]


def pick_body(targets, *refs):
    *tail_refs, rim_ref = refs
    rim = jnp.zeros(rim_ref.shape, f32)
    for target, ref in zip(targets, tail_refs):
        rim = jnp.where(place("head") == target, ref[...].astype(f32), rim)
    rim_ref[...] = rim.astype(rim_ref.dtype)


def gathered(own, loaded):
    heads = lax.axis_size("head")
    bits = bits_of(heads)
    assert bits
    slabs = {0: own}
    for bit in reversed(bits[1:]):
        for k in sorted(slabs):
            slabs[k ^ bit] = swapped(slabs[k], "head", bit)
    tail = own[own.shape[0] - RIM :]
    targets = [first if first == heads - 2 else first + 1 for first in range(0, heads, 2)]
    tails = [lax.ppermute(tail, ("seq", "head"), rim_route(target)) for target in targets]
    slabs[1] = swapped(own, "head", 1)
    arrived = [k for k in sorted(slabs) if k > 1]
    moved, tails, loaded = lax.optimization_barrier(
        ([slabs[k] for k in arrived], tails, loaded)
    )
    for k, slab in zip(arrived, moved):
        slabs[k], slabs[k ^ 1] = slab, swapped(slab, "head", 1)
    rim = vmem_call(
        functools.partial(pick_body, targets), jax.ShapeDtypeStruct(tail.shape, bf16), tails
    )
    return [slabs[k] for k in range(1, heads)], [rim, swapped(rim, "head", 1)], loaded


def vmem_call(body, out_shape, args, scratch=(), hbm=0, grant=4, flops=0, moved=0):
    here = len(args) - hbm
    args = [pltpu.with_memory_space_constraint(a, pltpu.HBM) if i >= here else a for i, a in enumerate(args)]
    spaces = [pltpu.VMEM] * here + [pltpu.HBM] * hbm
    return pl.pallas_call(
        body,
        out_shape=out_shape,
        in_specs=[pl.BlockSpec(memory_space=space) for space in spaces],
        out_specs=jax.tree.map(lambda _: pl.BlockSpec(memory_space=pltpu.VMEM), out_shape),
        scratch_shapes=list(scratch),
        compiler_params=pltpu.CompilerParams(vmem_limit_bytes=grant * MIB),
        cost_estimate=pl.CostEstimate(flops=flops, bytes_accessed=moved, transcendentals=0),
    )(*args)


def place(axis, bit=None):
    here = lax.axis_index(axis)
    return here if bit is None else here // bit % 2


def column_pieces(width):
    step = math.gcd(width, 256)
    return [slice(i, i + step) for i in range(0, width, step)]


def load_body(
    hidden_ref, decay_down_ref, gate_down_ref, beta_ref, weight_ref,
    own_ref, weights, downs, betas, sems,
):
    rank = decay_down_ref.shape[1]
    copies = [
        pltpu.make_async_copy(hidden_ref, own_ref, sems.at[0]),
        pltpu.make_async_copy(decay_down_ref, downs.at[:, pl.ds(0, rank)], sems.at[1]),
        pltpu.make_async_copy(gate_down_ref, downs.at[:, pl.ds(rank, rank)], sems.at[2]),
        pltpu.make_async_copy(beta_ref, betas, sems.at[3]),
    ]
    for c in range(2):
        copies.append(pltpu.make_async_copy(weight_ref.at[c], weights.at[c], sems.at[4 + c]))
    for copy in copies:
        copy.start()
    for copy in copies:
        copy.wait()


def load(own, decay_down, gate_down, beta, weight):
    width, rank = decay_down.shape
    return vmem_call(
        load_body,
        (
            jax.ShapeDtypeStruct(own.shape, bf16),
            jax.ShapeDtypeStruct((2, *weight.shape[1:]), bf16),
            jax.ShapeDtypeStruct((width, 2 * rank), bf16),
            jax.ShapeDtypeStruct(beta.shape, bf16),
        ),
        (own, decay_down, gate_down, beta, weight),
        scratch=[pltpu.SemaphoreType.DMA((6,))],
        hbm=5,
        grant=8,
    )


def front_body(slab_count, *refs):
    (one_ref, two_ref, *slab_refs), refs = refs[: slab_count + 1], refs[slab_count + 1 :]
    (own_rows_ref, weights, downs, betas), refs = refs[:4], refs[4:]
    hbm_refs, refs = refs[:5], refs[5:]
    (own_ref, other_ref, solved_ref, attend_ref, start_ref, gate_ref), refs = refs[:6], refs[6:]
    loaded, refs = refs[:5], refs[5:]
    rows_ref, projected, running_ref, parts_ref, mixing, inverse, sides, sems = refs
    rates, decay_up_ref, bias_ref, conv_ref, value_weight = loaded
    weight_ref = hbm_refs[-1]
    heads, count, size = start_ref.shape
    slab_rows = count // slab_count
    tap_count = conv_ref.shape[1]
    rank = decay_up_ref.shape[0]
    chunk = math.gcd(count, 64)
    chunks = count // chunk
    block = math.gcd(count, 128)
    blocks = count // block
    here = place("head")

    def rows_of(k):
        return pl.ds(pl.multiple_of(RIM + (here ^ k) * slab_rows, 16), slab_rows)

    small = [pltpu.make_async_copy(hbm_refs[i], loaded[i], sems.at[i]) for i in range(4)]
    pieces = column_pieces(heads * size)
    streams = []
    for i, piece in enumerate(pieces):
        streams.append(
            pltpu.make_async_copy(
                weight_ref.at[2, :, piece], value_weight.at[:, piece], sems.at[4 + i]
            )
        )
    for copy in small + streams:
        copy.start()
    rows_ref[:RIM, :] = (one_ref[...].astype(f32) + two_ref[...].astype(f32)).astype(bf16)
    for k, ref in enumerate([own_rows_ref, *slab_refs]):
        rows_ref[rows_of(k), :] = ref[...]
    for c in range(2):
        for piece in pieces:
            projected[c, :, piece] = dot(rows_ref[...], weights[c, :, piece])
    low = dot(rows_ref[RIM:, :], downs[...]).astype(bf16)
    gate_ref[...] = low[:, rank:]
    strength = jax.nn.sigmoid(dot(rows_ref[RIM:, :], betas[...], ((1,), (1,))))
    for copy in small:
        copy.wait()
    running_ref[...] = dot(low[:, :rank], decay_up_ref[...])
    tiles = [slice(a * chunk, (a + 1) * chunk) for a in range(chunks)]
    for h in range(heads):
        lanes = slice(h * size, (h + 1) * size)
        rate = jnp.exp(jnp.full((1, size), rates[h], f32))
        for rows in tiles:
            raw = running_ref[rows, lanes] + bias_ref[:, lanes]
            softplus = jnp.maximum(raw, 0.0) + jnp.log(1.0 + jnp.exp(-jnp.abs(raw)))
            log_decay = -rate * softplus
            high = log_decay.astype(bf16)
            parts_ref[rows, lanes] = high
            rest = (log_decay - high.astype(f32)).astype(bf16)
            parts_ref[count + rows.start : count + rows.stop, lanes] = rest
    row = lax.broadcasted_iota(jnp.int32, (count, count), 0)
    col = lax.broadcasted_iota(jnp.int32, (count, count), 1)
    lower = jnp.where(row >= col, 1.0, 0.0).astype(bf16)
    running_ref[...] = dot(jnp.concatenate([lower, lower], axis=1), parts_ref[...])

    def convolved(c, rows, lanes):
        taps = conv_ref[c].astype(f32)
        total = None
        for i in range(tap_count):
            first = RIM - tap_count + 1 + i + rows.start
            term = projected[c, pl.ds(first, chunk), lanes] * taps[i : i + 1, lanes]
            total = term if total is None else total + term
        half = 0.5 * total
        return half + half * jnp.tanh(half)

    stops = []
    for h in range(heads):
        lanes = slice(h * size, (h + 1) * size)
        last = running_ref[count - 1 : count, lanes]
        middles, key_falls, stop, lefts = [], [], [], []
        for rows in tiles:
            running = running_ref[rows, lanes]
            middle = running[chunk // 2 : chunk // 2 + 1]
            above = running - middle
            rise, entry = jnp.exp(above), jnp.exp(middle)
            queries = convolved(0, rows, lanes)
            power = jnp.sum(queries * queries, -1, keepdims=True)
            queries = queries * (lax.rsqrt(power + 1e-06) * size ** (-0.5)) * rise
            start_ref[h, rows, :] = (queries * entry).astype(bf16)
            keys = convolved(1, rows, lanes)
            power = jnp.sum(keys * keys, -1, keepdims=True)
            keys = keys * lax.rsqrt(power + 1e-06)
            key_fall = keys * strength[rows, h : h + 1] * jnp.exp(-above)
            keys = keys * rise
            sides[h, rows, :size] = (keys * entry).astype(bf16)
            stop.append((key_fall * jnp.exp(last - middle)).astype(bf16))
            middles.append(middle)
            key_falls.append(key_fall)
            lefts.append(jnp.concatenate([keys.astype(bf16), queries.astype(bf16)], axis=0))
        stops.append((jnp.concatenate(stop, axis=0), jnp.exp(last)))
        for a in range(chunks):
            rows = tiles[a]
            reach = (a * chunk // block + 1) * block
            falls = []
            for b in range(reach // chunk):
                if b < a:
                    falls.append(key_falls[b] * jnp.exp(middles[a] - middles[b]))
                elif b == a:
                    falls.append(key_falls[b])
                else:
                    falls.append(jnp.zeros((chunk, size), f32))
            right = jnp.concatenate(falls, axis=0).astype(bf16)
            scores = dot(lefts[a], right, ((1,), (1,)))
            inside = slice(reach - block, reach)
            if reach > block:
                before = slice(0, reach - block)
                mixing[h, rows, before] = scores[:chunk, before].astype(bf16)
                attend_ref[h, rows, before] = scores[chunk:, before].astype(bf16)
            at, to = row[rows, inside], col[rows, inside]
            mixing[h, rows, inside] = jnp.where(at > to, scores[:chunk, inside], 0.0).astype(bf16)
            attend_ref[h, rows, inside] = jnp.where(
                at >= to, scores[chunk:, inside], 0.0
            ).astype(bf16)

    for i, piece in enumerate(pieces):
        streams[i].wait()
        projected[2, :, piece] = dot(rows_ref[...], value_weight[:, piece])

    at, to = row[:block, :block], col[:block, :block]
    eye = jnp.where(at == to, 1.0, 0.0).astype(bf16)
    base = math.gcd(block, BASE)
    near = jnp.where(at // base == to // base, -1.0, 0.0).astype(bf16)
    corners = [(h, slice(d * block, (d + 1) * block)) for h in range(heads) for d in range(blocks)]
    powers = [mixing[h, d, d] * near for h, d in corners]
    totals = [power + eye for power in powers]
    steps = (base - 1).bit_length() - 1
    if steps:
        powers = [dot(power, power).astype(bf16) for power in powers]
    for step in range(steps):
        for n in range(len(corners)):
            power, total = powers[n], totals[n]
            if step < steps - 1:
                both = dot(jnp.concatenate([power, total], axis=0), power)
                powers[n], more = both[:block].astype(bf16), both[block:]
            else:
                more = dot(total, power)
            totals[n] = (total.astype(f32) + more).astype(bf16)
    for (h, d), total in zip(corners, totals):
        inverse[h, d, :] = total
    width = base
    while width < block:
        odd = range(width, block, 2 * width)
        pair_mask = (at // width % 2 == 1) & (to // width == at // width - 1)
        pair_mask = jnp.where(pair_mask, 1.0, 0.0).astype(bf16)
        halves = []
        for h, d in corners:
            parts = [inverse[h, d.start + i : d.start + i + width, :] for i in odd]
            chosen = jnp.concatenate(parts, axis=0)
            halves.append((chosen, dot(chosen, mixing[h, d, d] * pair_mask).astype(bf16)))
        for (h, d), (chosen, half) in zip(corners, halves):
            new = (chosen.astype(f32) - dot(half, inverse[h, d, :])).astype(bf16)
            for n, i in enumerate(odd):
                inverse[h, d.start + i : d.start + i + width, :] = new[n * width : (n + 1) * width]
        width *= 2

    for h in range(heads):
        for rows in tiles:
            lanes = slice(h * size, (h + 1) * size)
            sides[h, rows, size:] = convolved(2, rows, lanes).astype(bf16)
    for d in range(blocks):
        rows = slice(d * block, (d + 1) * block)
        for h in range(heads):
            side = sides[h, rows, :]
            if d:
                done = solved_ref[h, : d * block, :]
                side = (side.astype(f32) - dot(mixing[h, rows, : d * block], done)).astype(bf16)
            solved_ref[h, rows, :] = dot(inverse[h, rows, :], side).astype(bf16)
    pairs = []
    unit = row[:size, :size] == col[:size, :size]
    for h in range(heads):
        stop, fade = stops[h]
        moved = dot(stop, solved_ref[h], ((0,), (0,)))
        diagonal = jnp.where(unit, jnp.broadcast_to(fade, (size, size)), 0.0)
        pairs.append(jnp.concatenate([diagonal - moved[:, :size], moved[:, size:]], axis=1))
    upper = place("seq", 1) == 1
    for h in range(heads // 2):
        low, high = pairs[h], pairs[heads // 2 + h]
        own_ref[h] = jnp.where(upper, high, low).astype(bf16)
        other_ref[h] = jnp.where(upper, low, high).astype(bf16)


def front(rims, slabs, fetched, loaded, weight, size):
    slab_count, slab_rows = 1 + len(slabs), slabs[0].shape[0]
    count = slab_count * slab_rows
    _, width, channels = weight.shape
    heads, block = channels // size, math.gcd(count, 128)
    buffers = [pltpu.SMEM(loaded[0].shape, f32)]
    buffers += [pltpu.VMEM(part.shape, part.dtype) for part in loaded[1:]]
    return vmem_call(
        functools.partial(front_body, slab_count),
        (
            jax.ShapeDtypeStruct((heads // 2, size, 2 * size), bf16),
            jax.ShapeDtypeStruct((heads // 2, size, 2 * size), bf16),
            jax.ShapeDtypeStruct((heads, count, 2 * size), bf16),
            jax.ShapeDtypeStruct((heads, count, count), bf16),
            jax.ShapeDtypeStruct((heads, count, size), bf16),
            jax.ShapeDtypeStruct((count, fetched[2].shape[1] // 2), bf16),
        ),
        (*rims, *slabs, *fetched, *loaded, weight),
        scratch=[
            *buffers,
            pltpu.VMEM((width, channels), bf16),
            pltpu.VMEM((RIM + count, width), bf16),
            pltpu.VMEM((3, RIM + count, channels), f32),
            pltpu.VMEM((count, channels), f32),
            pltpu.VMEM((2 * count, channels), bf16),
            pltpu.VMEM((heads, count, count), bf16),
            pltpu.VMEM((heads, count, block), bf16),
            pltpu.VMEM((heads, count, 2 * size), bf16),
            pltpu.SemaphoreType.DMA((4 + len(column_pieces(channels)),)),
        ],
        hbm=1 + len(loaded),
        grant=24,
        flops=2 * count * width * channels * 4,
        moved=2 * 4 * width * channels,
    )


def rows_body(attend_ref, solved_ref, start_ref, low_ref, up_ref, raised_ref, output_ref, gate_ref):
    heads, _, size = start_ref.shape
    gate_ref[...] = jax.nn.sigmoid(dot(low_ref[...], up_ref[...]))
    count = attend_ref.shape[1]
    block = math.gcd(count, 128)
    for h in range(heads):
        for begin in range(0, count, block):
            rows, reach = slice(begin, begin + block), slice(0, begin + block)
            both = dot(attend_ref[h, rows, reach], solved_ref[h, reach, :])
            raised_ref[h, rows, :] = (start_ref[h, rows, :].astype(f32) - both[:, :size]).astype(bf16)
            output_ref[rows, h * size : (h + 1) * size] = both[:, size:]


def composed(later, first, size):
    both = dot(later[:, :size], first)
    return both[:, :size], both[:, size:] + later[:, size:].astype(f32)


def put(ref, h, pair):
    size = ref.shape[1]
    if ref.shape[2] > size:
        ref[h, :, :size] = pair[0].astype(bf16)
    ref[h, :, ref.shape[2] - size :] = pair[1].astype(bf16)


def join_body(bit, own_ref, far_ref, total_ref):
    heads, size, _ = own_ref.shape
    for h in range(heads):
        own, far = own_ref[h], far_ref[h]
        upper = place("seq", bit) == 1
        later, first = jnp.where(upper, own, far), jnp.where(upper, far, own)
        put(total_ref, h, composed(later, first, size))


def join(bit, own, far, last):
    heads, size, width = own.shape
    return vmem_call(
        functools.partial(join_body, bit),
        jax.ShapeDtypeStruct((heads, size, size if last else width), bf16),
        (own, far),
        flops=2 * heads * size * size * width,
        moved=6 * heads * size * width,
    )


def before_body(bit, far_ref, *refs):
    *near_refs, out_ref = refs
    heads, size, width = far_ref.shape
    row = lax.broadcasted_iota(jnp.int32, (size, width), 0)
    col = lax.broadcasted_iota(jnp.int32, (size, width), 1)
    for h in range(heads):
        if near_refs:
            near = near_refs[0][h]
            pair = jnp.concatenate(composed(near, far_ref[h], size), axis=1)
            near = near.astype(f32)
        else:
            near, pair = jnp.where(row == col, 1.0, 0.0), far_ref[h].astype(f32)
        out_ref[h] = jnp.where(place("seq", bit) == 1, pair, near).astype(bf16)


def before(bit, near, far):
    return vmem_call(
        functools.partial(before_body, bit),
        jax.ShapeDtypeStruct(far.shape, bf16),
        (far, *near),
        flops=2 * math.prod(far.shape) * far.shape[1],
        moved=6 * math.prod(far.shape),
    )


def entry_body(bit, near_ref, far_ref, own_ref, partner_ref, keep_ref, send_ref):
    heads, size, _ = near_ref.shape
    arrived, upper = place("seq", bit) == 1, place("seq", 1) == 1
    for h in range(heads):
        state = dot(near_ref[h, :, :size], far_ref[h])
        state = jnp.where(arrived, state, 0.0) + near_ref[h, :, size:].astype(f32)
        first = jnp.where(upper, partner_ref[h], own_ref[h])
        state = state.astype(bf16)
        later = dot(first[:, :size], state) + first[:, size:].astype(f32)
        later = later.astype(bf16)
        keep_ref[h] = jnp.where(upper, later, state)
        send_ref[h] = jnp.where(upper, state, later)


def entry_states(own, other):
    heads, size, width = own.shape
    bits = bits_of(lax.axis_size("seq"))
    partner = swapped(other, "seq", 1)
    total = join(1, own, partner, len(bits) == 2)
    near = ()
    assert len(bits) > 2
    for bit in bits[1:-1]:
        far = swapped(total, "seq", bit)
        total = join(bit, total, far, 2 * bit == bits[-1])
        near = (before(bit, near, far),)
    far = swapped(total, "seq", bits[-1])
    state = jax.ShapeDtypeStruct((heads, size, size), bf16)
    keep, send = vmem_call(
        functools.partial(entry_body, bits[-1]),
        (state, state),
        (*near, far, own, partner),
        flops=4 * heads * size * size * size,
        moved=14 * heads * size * size,
    )
    return keep, swapped(send, "seq", 1)


def back_body(
    places, own_ref, other_ref, raised_ref, output_ref, gate_ref, gain_ref, weight_ref, keep_ref,
    *rest,
):
    normed = rest[-1]
    size = gain_ref.shape[1]
    slab_rows = keep_ref.shape[0]
    half = own_ref.shape[0]
    upper = place("seq", 1) == 1
    for k, away in enumerate(places):
        rows = pl.ds(pl.multiple_of((place("head") ^ away) * slab_rows, 16), slab_rows)
        for h in range(raised_ref.shape[0]):
            lanes = slice(h * size, (h + 1) * size)
            own, other = own_ref[h % half], other_ref[h % half]
            state = jnp.where(upper, other, own) if h < half else jnp.where(upper, own, other)
            attended = dot(raised_ref[h, rows, :], state) + output_ref[rows, lanes]
            power = jnp.sum(attended * attended, -1, keepdims=True) * (1.0 / size)
            normed[k * slab_rows : (k + 1) * slab_rows, lanes] = (
                attended * lax.rsqrt(power + 1e-05) * gain_ref[...] * gate_ref[rows, lanes]
            ).astype(bf16)
    total = dot(normed[...], weight_ref[...])
    keep_ref[...] = total[:slab_rows]
    if len(rest) > 1:
        rest[0][...] = total[slab_rows:].astype(bf16)


def back(places, states, raised, output_rows, out_gate, gain, weight, slab_rows):
    slab_count, width = len(places), weight.shape[1]
    shapes = [jax.ShapeDtypeStruct((slab_rows, width), f32)]
    if slab_count > 1:
        shapes.append(jax.ShapeDtypeStruct((slab_rows, width), bf16))
    return vmem_call(
        functools.partial(back_body, places),
        shapes,
        (*states, raised, output_rows, out_gate, gain, weight),
        scratch=[pltpu.VMEM((slab_count * slab_rows, weight.shape[0]), bf16)],
        grant=10,
        flops=2 * slab_count * slab_rows * weight.shape[0] * width,
        moved=2 * weight.shape[0] * width,
    )


def shards(
    hidden_in,
    qkv_weight,
    conv_weight,
    decay_log,
    dt_bias,
    decay_down,
    decay_up,
    beta_weight,
    gate_down,
    gate_up,
    norm_gain,
    out_weight,
):
    heads, size = decay_log.shape[0], norm_gain.shape[0]
    channels = heads * size
    devices = lax.axis_size("head")
    weight = qkv_weight.transpose(1, 0, 2)
    fetched = load(hidden_in, decay_down, gate_down, beta_weight.T, weight)
    slabs, rims, fetched = gathered(hidden_in, fetched)
    own, other, solved, attend, start, gate_low = front(
        rims, slabs, fetched, (decay_log, decay_up, dt_bias[None], conv_weight), weight, size
    )
    count = start.shape[1]
    raised, output_rows, out_gate = vmem_call(
        rows_body,
        (
            jax.ShapeDtypeStruct((heads, count, size), bf16),
            jax.ShapeDtypeStruct((count, channels), f32),
            jax.ShapeDtypeStruct((count, channels), f32),
        ),
        (attend, solved, start, gate_low, gate_up),
        grant=8,
        flops=2 * heads * count * count * 2 * size,
        moved=4 * heads * count * count,
    )
    states = entry_states(own, other)
    slab_rows = count // devices
    sums = {}
    for g in reversed(range(max(devices // 2, 1))):
        places = [2 * g, 2 * g + 1][:devices]
        keep, *send = back(
            places, states, raised, output_rows, out_gate, norm_gain[None], out_weight, slab_rows
        )
        sums[g] = [keep] + [swapped(part, "head", 1).astype(f32) for part in send]
    for bit in bits_of(devices)[1:]:
        for g in sorted(sums):
            if 2 * g & bit:
                arrived = swapped(sum(sums.pop(g)).astype(bf16), "head", bit)
                sums[g ^ bit // 2].append(arrived.astype(f32))
    return sum(sums[0]).astype(bf16)


def solution(mesh):
    return jax.shard_map(
        shards,
        mesh=mesh,
        in_specs=(
            P(("seq", "head"), None),
            P(None, None, "head"),
            P(None, None, "head"),
            P("head"),
            P("head"),
            P(),
            P(None, "head"),
            P(None, "head"),
            P(),
            P(None, "head"),
            P(),
            P("head", None),
        ),
        out_specs=P(("seq", "head"), None),
        check_vma=False,
    )
```

```python
import functools
import math

import jax
import jax.numpy as jnp
from jax import lax
from jax.experimental import pallas as pl
from jax.experimental.pallas import tpu as pltpu
from jax.sharding import PartitionSpec as P

RIM = 16
BASE = 16
GROUPS = 2
MIB = 1024 * 1024
f32 = jnp.float32
bf16 = jnp.bfloat16


def dot(left, right, contract=((1,), (0,))):
    return lax.dot_general(left, right, (contract, ((), ())), preferred_element_type=f32)


def swapped(block, axis, bit):
    return lax.ppermute(block, axis, [(i, i ^ bit) for i in range(lax.axis_size(axis))])


def bits_of(size):
    assert size & (size - 1) == 0
    return [1 << i for i in range(size.bit_length() - 1)]


def rim_route(target):
    heads, seqs = lax.axis_size("head"), lax.axis_size("seq")
    return [(s * heads + heads - 1, (s + 1) * heads + target) for s in range(seqs - 1)]


def pick_body(targets, *refs):
    *tail_refs, rim_ref = refs
    rim = jnp.zeros(rim_ref.shape, f32)
    for target, ref in zip(targets, tail_refs):
        rim = jnp.where(place("head") == target, ref[...].astype(f32), rim)
    rim_ref[...] = rim.astype(rim_ref.dtype)


def gathered(own, loaded):
    heads = lax.axis_size("head")
    bits = bits_of(heads)
    assert bits
    slabs = {0: own}
    for bit in reversed(bits[1:]):
        for k in sorted(slabs):
            slabs[k ^ bit] = swapped(slabs[k], "head", bit)
    tail = own[own.shape[0] - RIM :]
    targets = [first if first == heads - 2 else first + 1 for first in range(0, heads, 2)][::-1]
    tails = [lax.ppermute(tail, ("seq", "head"), rim_route(target)) for target in targets]
    slabs[1] = swapped(own, "head", 1)
    arrived = [k for k in sorted(slabs) if k > 1]
    moved, tails, loaded = lax.optimization_barrier(
        ([slabs[k] for k in arrived], tails, loaded)
    )
    for k, slab in zip(arrived, moved):
        slabs[k], slabs[k ^ 1] = slab, swapped(slab, "head", 1)
    rim = vmem_call(
        functools.partial(pick_body, targets), jax.ShapeDtypeStruct(tail.shape, bf16), tails
    )
    return [slabs[k] for k in range(1, heads)], [rim, swapped(rim, "head", 1)], loaded


def vmem_call(body, out_shape, args, scratch=(), hbm=0, grant=4, flops=0, moved=0):
    here = len(args) - hbm
    args = [pltpu.with_memory_space_constraint(a, pltpu.HBM) if i >= here else a for i, a in enumerate(args)]
    spaces = [pltpu.VMEM] * here + [pltpu.HBM] * hbm
    return pl.pallas_call(
        body,
        out_shape=out_shape,
        in_specs=[pl.BlockSpec(memory_space=space) for space in spaces],
        out_specs=jax.tree.map(lambda _: pl.BlockSpec(memory_space=pltpu.VMEM), out_shape),
        scratch_shapes=list(scratch),
        compiler_params=pltpu.CompilerParams(vmem_limit_bytes=grant * MIB),
        cost_estimate=pl.CostEstimate(flops=flops, bytes_accessed=moved, transcendentals=0),
    )(*args)


def place(axis, bit=None):
    here = lax.axis_index(axis)
    return here if bit is None else here // bit % 2


def column_pieces(width):
    step = math.gcd(width, 256)
    return [slice(i, i + step) for i in range(0, width, step)]


def load_body(
    hidden_ref, decay_down_ref, gate_down_ref, beta_ref, weight_ref,
    own_ref, weights, downs, betas, sems,
):
    rank = decay_down_ref.shape[1]
    copies = [
        pltpu.make_async_copy(hidden_ref, own_ref, sems.at[0]),
        pltpu.make_async_copy(decay_down_ref, downs.at[:, pl.ds(0, rank)], sems.at[1]),
        pltpu.make_async_copy(gate_down_ref, downs.at[:, pl.ds(rank, rank)], sems.at[2]),
        pltpu.make_async_copy(beta_ref, betas, sems.at[3]),
    ]
    for c in range(2):
        copies.append(pltpu.make_async_copy(weight_ref.at[c], weights.at[c], sems.at[4 + c]))
    for copy in copies:
        copy.start()
    for copy in copies:
        copy.wait()


def load(own, decay_down, gate_down, beta, weight):
    width, rank = decay_down.shape
    return vmem_call(
        load_body,
        (
            jax.ShapeDtypeStruct(own.shape, bf16),
            jax.ShapeDtypeStruct((2, *weight.shape[1:]), bf16),
            jax.ShapeDtypeStruct((width, 2 * rank), bf16),
            jax.ShapeDtypeStruct(beta.shape, bf16),
        ),
        (own, decay_down, gate_down, beta, weight),
        scratch=[pltpu.SemaphoreType.DMA((6,))],
        hbm=5,
        grant=8,
    )


def front_body(slab_count, *refs):
    (one_ref, two_ref, *slab_refs), refs = refs[: slab_count + 1], refs[slab_count + 1 :]
    (own_rows_ref, weights, downs, betas), refs = refs[:4], refs[4:]
    hbm_refs, refs = refs[:5], refs[5:]
    (own_refs, other_refs), refs = (refs[:GROUPS], refs[GROUPS : 2 * GROUPS]), refs[2 * GROUPS :]
    (solved_ref, attend_ref, start_ref, gate_ref), refs = refs[:4], refs[4:]
    loaded, refs = refs[:5], refs[5:]
    rows_ref, projected, running_ref, parts_ref, mixing, inverse, sides, sems = refs
    rates, decay_up_ref, bias_ref, conv_ref, value_weight = loaded
    weight_ref = hbm_refs[-1]
    heads, count, size = start_ref.shape
    slab_rows = count // slab_count
    tap_count = conv_ref.shape[1]
    rank = decay_up_ref.shape[0]
    chunk = math.gcd(count, 64)
    chunks = count // chunk
    block = math.gcd(count, 128)
    blocks = count // block
    here = place("head")

    def rows_of(k):
        return pl.ds(pl.multiple_of(RIM + (here ^ k) * slab_rows, 16), slab_rows)

    small = [pltpu.make_async_copy(hbm_refs[i], loaded[i], sems.at[i]) for i in range(4)]
    pieces = column_pieces(heads * size)
    streams = []
    for i, piece in enumerate(pieces):
        streams.append(
            pltpu.make_async_copy(
                weight_ref.at[2, :, piece], value_weight.at[:, piece], sems.at[4 + i]
            )
        )
    for copy in small + streams:
        copy.start()
    rows_ref[:RIM, :] = (one_ref[...].astype(f32) + two_ref[...].astype(f32)).astype(bf16)
    for k, ref in enumerate([own_rows_ref, *slab_refs]):
        rows_ref[rows_of(k), :] = ref[...]

    def project(c, piece, weight):
        result = dot(rows_ref[...], weight)
        for begin in range(piece.start, piece.stop, size):
            at = begin - piece.start
            projected[c * heads + begin // size] = result[:, at : at + size]

    for c in range(2):
        for piece in pieces:
            project(c, piece, weights[c, :, piece])
    low = dot(rows_ref[RIM:, :], downs[...]).astype(bf16)
    gate_ref[...] = low[:, rank:]
    strength = jax.nn.sigmoid(dot(rows_ref[RIM:, :], betas[...], ((1,), (1,))))
    for copy in small:
        copy.wait()
    running_ref[...] = dot(low[:, :rank], decay_up_ref[...])
    tiles = [slice(a * chunk, (a + 1) * chunk) for a in range(chunks)]
    for h in range(heads):
        lanes = slice(h * size, (h + 1) * size)
        rate = jnp.exp(jnp.full((1, size), rates[h], f32))
        for rows in tiles:
            raw = running_ref[rows, lanes] + bias_ref[:, lanes]
            softplus = jnp.maximum(raw, 0.0) + jnp.log(1.0 + jnp.exp(-jnp.abs(raw)))
            log_decay = -rate * softplus
            high = log_decay.astype(bf16)
            parts_ref[rows, lanes] = high
            rest = (log_decay - high.astype(f32)).astype(bf16)
            parts_ref[count + rows.start : count + rows.stop, lanes] = rest
    row = lax.broadcasted_iota(jnp.int32, (count, count), 0)
    col = lax.broadcasted_iota(jnp.int32, (count, count), 1)
    lower = jnp.where(row >= col, 1.0, 0.0).astype(bf16)
    running_ref[...] = dot(jnp.concatenate([lower, lower], axis=1), parts_ref[...])

    def convolved(c, rows, h):
        taps = conv_ref[c].astype(f32)[:, h * size : (h + 1) * size]
        total = None
        for i in range(tap_count):
            first = RIM - tap_count + 1 + i + rows.start
            term = projected[c * heads + h, pl.ds(first, chunk), :] * taps[i : i + 1]
            total = term if total is None else total + term
        half = 0.5 * total
        return half + half * jnp.tanh(half)

    stops = []
    for h in range(heads):
        lanes = slice(h * size, (h + 1) * size)
        last = running_ref[count - 1 : count, lanes]
        middles, key_falls, stop, lefts = [], [], [], []
        for rows in tiles:
            running = running_ref[rows, lanes]
            middle = running[chunk // 2 : chunk // 2 + 1]
            above = running - middle
            rise, entry = jnp.exp(above), jnp.exp(middle)
            queries = convolved(0, rows, h)
            power = jnp.sum(queries * queries, -1, keepdims=True)
            queries = queries * (lax.rsqrt(power + 1e-06) * size ** (-0.5)) * rise
            start_ref[h, rows, :] = (queries * entry).astype(bf16)
            keys = convolved(1, rows, h)
            power = jnp.sum(keys * keys, -1, keepdims=True)
            keys = keys * lax.rsqrt(power + 1e-06)
            key_fall = keys * strength[rows, h : h + 1] * jnp.exp(-above)
            keys = keys * rise
            sides[h, rows, :size] = (keys * entry).astype(bf16)
            stop.append((key_fall * jnp.exp(last - middle)).astype(bf16))
            middles.append(middle)
            key_falls.append(key_fall)
            lefts.append(jnp.concatenate([keys.astype(bf16), queries.astype(bf16)], axis=0))
        stops.append((jnp.concatenate(stop, axis=0), jnp.exp(last)))
        for a in range(chunks):
            rows = tiles[a]
            reach = (a * chunk // block + 1) * block
            falls = []
            for b in range(reach // chunk):
                if b < a:
                    falls.append(key_falls[b] * jnp.exp(middles[a] - middles[b]))
                elif b == a:
                    falls.append(key_falls[b])
                else:
                    falls.append(jnp.zeros((chunk, size), f32))
            right = jnp.concatenate(falls, axis=0).astype(bf16)
            scores = dot(lefts[a], right, ((1,), (1,)))
            inside = slice(reach - block, reach)
            if reach > block:
                before = slice(0, reach - block)
                mixing[h, rows, before] = scores[:chunk, before].astype(bf16)
                attend_ref[h, rows, before] = scores[chunk:, before].astype(bf16)
            at, to = row[rows, inside], col[rows, inside]
            mixing[h, rows, inside] = jnp.where(at > to, scores[:chunk, inside], 0.0).astype(bf16)
            attend_ref[h, rows, inside] = jnp.where(
                at >= to, scores[chunk:, inside], 0.0
            ).astype(bf16)

    for i, piece in enumerate(pieces):
        streams[i].wait()
        project(2, piece, value_weight[:, piece])

    at, to = row[:block, :block], col[:block, :block]
    eye = jnp.where(at == to, 1.0, 0.0).astype(bf16)
    base = math.gcd(block, BASE)
    near = jnp.where(at // base == to // base, -1.0, 0.0).astype(bf16)
    corners = [(h, slice(d * block, (d + 1) * block)) for h in range(heads) for d in range(blocks)]
    powers = [mixing[h, d, d] * near for h, d in corners]
    totals = [power + eye for power in powers]
    steps = (base - 1).bit_length() - 1
    if steps:
        powers = [dot(power, power).astype(bf16) for power in powers]
    for step in range(steps):
        for n in range(len(corners)):
            power, total = powers[n], totals[n]
            if step < steps - 1:
                both = dot(jnp.concatenate([power, total], axis=0), power)
                powers[n], more = both[:block].astype(bf16), both[block:]
            else:
                more = dot(total, power)
            totals[n] = (total.astype(f32) + more).astype(bf16)
    for (h, d), total in zip(corners, totals):
        inverse[h, d, :] = total
    width = base
    while width < block:
        odd = range(width, block, 2 * width)
        pair_mask = (at // width % 2 == 1) & (to // width == at // width - 1)
        pair_mask = jnp.where(pair_mask, 1.0, 0.0).astype(bf16)
        halves = []
        for h, d in corners:
            parts = [inverse[h, d.start + i : d.start + i + width, :] for i in odd]
            chosen = jnp.concatenate(parts, axis=0)
            halves.append((chosen, dot(chosen, mixing[h, d, d] * pair_mask).astype(bf16)))
        for (h, d), (chosen, half) in zip(corners, halves):
            new = (chosen.astype(f32) - dot(half, inverse[h, d, :])).astype(bf16)
            for n, i in enumerate(odd):
                inverse[h, d.start + i : d.start + i + width, :] = new[n * width : (n + 1) * width]
        width *= 2

    for h in range(heads):
        for rows in tiles:
            sides[h, rows, size:] = convolved(2, rows, h).astype(bf16)
    for d in range(blocks):
        rows = slice(d * block, (d + 1) * block)
        for h in range(heads):
            side = sides[h, rows, :]
            if d:
                done = solved_ref[h, : d * block, :]
                side = (side.astype(f32) - dot(mixing[h, rows, : d * block], done)).astype(bf16)
            solved_ref[h, rows, :] = dot(inverse[h, rows, :], side).astype(bf16)
    pairs = []
    unit = row[:size, :size] == col[:size, :size]
    for h in range(heads):
        stop, fade = stops[h]
        moved = dot(stop, solved_ref[h], ((0,), (0,)))
        diagonal = jnp.where(unit, jnp.broadcast_to(fade, (size, size)), 0.0)
        pairs.append(jnp.concatenate([diagonal - moved[:, :size], moved[:, size:]], axis=1))
    upper = place("seq", 1) == 1
    for h in range(heads // 2):
        low, high = pairs[h], pairs[heads // 2 + h]
        group, at = divmod(h, own_refs[0].shape[0])
        own_refs[group][at] = jnp.where(upper, high, low).astype(bf16)
        other_refs[group][at] = jnp.where(upper, low, high).astype(bf16)


def front(rims, slabs, fetched, loaded, weight, size):
    slab_count, slab_rows = 1 + len(slabs), slabs[0].shape[0]
    count = slab_count * slab_rows
    _, width, channels = weight.shape
    heads, block = channels // size, math.gcd(count, 128)
    buffers = [pltpu.SMEM(loaded[0].shape, f32)]
    buffers += [pltpu.VMEM(part.shape, part.dtype) for part in loaded[1:]]
    return vmem_call(
        functools.partial(front_body, slab_count),
        (
            *[jax.ShapeDtypeStruct((heads // 2 // GROUPS, size, 2 * size), bf16)] * (2 * GROUPS),
            jax.ShapeDtypeStruct((heads, count, 2 * size), bf16),
            jax.ShapeDtypeStruct((heads, count, count), bf16),
            jax.ShapeDtypeStruct((heads, count, size), bf16),
            jax.ShapeDtypeStruct((count, fetched[2].shape[1] // 2), bf16),
        ),
        (*rims, *slabs, *fetched, *loaded, weight),
        scratch=[
            *buffers,
            pltpu.VMEM((width, channels), bf16),
            pltpu.VMEM((RIM + count, width), bf16),
            pltpu.VMEM((3 * heads, RIM + count, size), f32),
            pltpu.VMEM((count, channels), f32),
            pltpu.VMEM((2 * count, channels), bf16),
            pltpu.VMEM((heads, count, count), bf16),
            pltpu.VMEM((heads, count, block), bf16),
            pltpu.VMEM((heads, count, 2 * size), bf16),
            pltpu.SemaphoreType.DMA((4 + len(column_pieces(channels)),)),
        ],
        hbm=1 + len(loaded),
        grant=24,
        flops=2 * count * width * channels * 4,
        moved=2 * 4 * width * channels,
    )


def rows_body(attend_ref, solved_ref, start_ref, low_ref, up_ref, raised_ref, output_ref, gate_ref):
    heads, _, size = start_ref.shape
    gate_ref[...] = jax.nn.sigmoid(dot(low_ref[...], up_ref[...]))
    count = attend_ref.shape[1]
    block = math.gcd(count, 128)
    for h in range(heads):
        for begin in range(0, count, block):
            rows, reach = slice(begin, begin + block), slice(0, begin + block)
            both = dot(attend_ref[h, rows, reach], solved_ref[h, reach, :])
            raised_ref[h, rows, :] = (start_ref[h, rows, :].astype(f32) - both[:, :size]).astype(bf16)
            output_ref[rows, h * size : (h + 1) * size] = both[:, size:]


def composed(later, first, size):
    both = dot(later[:, :size], first)
    return both[:, :size], both[:, size:] + later[:, size:].astype(f32)


def put(ref, h, pair):
    size = ref.shape[1]
    if ref.shape[2] > size:
        ref[h, :, :size] = pair[0].astype(bf16)
    ref[h, :, ref.shape[2] - size :] = pair[1].astype(bf16)


def join_body(bit, own_ref, far_ref, total_ref):
    heads, size, _ = own_ref.shape
    for h in range(heads):
        own, far = own_ref[h], far_ref[h]
        upper = place("seq", bit) == 1
        later, first = jnp.where(upper, own, far), jnp.where(upper, far, own)
        put(total_ref, h, composed(later, first, size))


def join(bit, own, far, last):
    heads, size, width = own.shape
    return vmem_call(
        functools.partial(join_body, bit),
        jax.ShapeDtypeStruct((heads, size, size if last else width), bf16),
        (own, far),
        flops=2 * heads * size * size * width,
        moved=6 * heads * size * width,
    )


def before_body(bit, far_ref, *refs):
    *near_refs, out_ref = refs
    heads, size, width = far_ref.shape
    row = lax.broadcasted_iota(jnp.int32, (size, width), 0)
    col = lax.broadcasted_iota(jnp.int32, (size, width), 1)
    for h in range(heads):
        if near_refs:
            near = near_refs[0][h]
            pair = jnp.concatenate(composed(near, far_ref[h], size), axis=1)
            near = near.astype(f32)
        else:
            near, pair = jnp.where(row == col, 1.0, 0.0), far_ref[h].astype(f32)
        out_ref[h] = jnp.where(place("seq", bit) == 1, pair, near).astype(bf16)


def before(bit, near, far):
    return vmem_call(
        functools.partial(before_body, bit),
        jax.ShapeDtypeStruct(far.shape, bf16),
        (far, *near),
        flops=2 * math.prod(far.shape) * far.shape[1],
        moved=6 * math.prod(far.shape),
    )


def entry_body(bit, near_ref, far_ref, own_ref, partner_ref, keep_ref, send_ref):
    heads, size, _ = near_ref.shape
    arrived, upper = place("seq", bit) == 1, place("seq", 1) == 1
    for h in range(heads):
        state = dot(near_ref[h, :, :size], far_ref[h])
        state = jnp.where(arrived, state, 0.0) + near_ref[h, :, size:].astype(f32)
        first = jnp.where(upper, partner_ref[h], own_ref[h])
        state = state.astype(bf16)
        later = dot(first[:, :size], state) + first[:, size:].astype(f32)
        later = later.astype(bf16)
        keep_ref[h] = jnp.where(upper, later, state)
        send_ref[h] = jnp.where(upper, state, later)


def entry_states(own, other):
    heads, size, width = own.shape
    bits = bits_of(lax.axis_size("seq"))
    partner = swapped(other, "seq", 1)
    total = join(1, own, partner, len(bits) == 2)
    near = ()
    assert len(bits) > 2
    for bit in bits[1:-1]:
        far = swapped(total, "seq", bit)
        total = join(bit, total, far, 2 * bit == bits[-1])
        near = (before(bit, near, far),)
    far = swapped(total, "seq", bits[-1])
    state = jax.ShapeDtypeStruct((heads, size, size), bf16)
    keep, send = vmem_call(
        functools.partial(entry_body, bits[-1]),
        (state, state),
        (*near, far, own, partner),
        flops=4 * heads * size * size * size,
        moved=14 * heads * size * size,
    )
    return keep, swapped(send, "seq", 1)


def back_body(places, *refs):
    own_refs, other_refs, refs = refs[:GROUPS], refs[GROUPS : 2 * GROUPS], refs[2 * GROUPS :]
    raised_ref, output_ref, gate_ref, gain_ref, weight_ref, keep_ref, *rest = refs
    normed = rest[-1]
    size = gain_ref.shape[1]
    slab_rows = keep_ref.shape[0]
    share = own_refs[0].shape[0]
    half = GROUPS * share
    upper = place("seq", 1) == 1
    for k, away in enumerate(places):
        rows = pl.ds(pl.multiple_of((place("head") ^ away) * slab_rows, 16), slab_rows)
        for h in range(raised_ref.shape[0]):
            lanes = slice(h * size, (h + 1) * size)
            group, at = divmod(h % half, share)
            own, other = own_refs[group][at], other_refs[group][at]
            state = jnp.where(upper, other, own) if h < half else jnp.where(upper, own, other)
            attended = dot(raised_ref[h, rows, :], state) + output_ref[rows, lanes]
            power = jnp.sum(attended * attended, -1, keepdims=True) * (1.0 / size)
            normed[k * slab_rows : (k + 1) * slab_rows, lanes] = (
                attended * lax.rsqrt(power + 1e-05) * gain_ref[...] * gate_ref[rows, lanes]
            ).astype(bf16)
    total = dot(normed[...], weight_ref[...])
    keep_ref[...] = total[:slab_rows]
    if len(rest) > 1:
        rest[0][...] = total[slab_rows:].astype(bf16)


def back(places, states, raised, output_rows, out_gate, gain, weight, slab_rows):
    slab_count, width = len(places), weight.shape[1]
    shapes = [jax.ShapeDtypeStruct((slab_rows, width), f32)]
    if slab_count > 1:
        shapes.append(jax.ShapeDtypeStruct((slab_rows, width), bf16))
    return vmem_call(
        functools.partial(back_body, places),
        shapes,
        (*states, raised, output_rows, out_gate, gain, weight),
        scratch=[pltpu.VMEM((slab_count * slab_rows, weight.shape[0]), bf16)],
        grant=10,
        flops=2 * slab_count * slab_rows * weight.shape[0] * width,
        moved=2 * weight.shape[0] * width,
    )


def shards(
    hidden_in,
    qkv_weight,
    conv_weight,
    decay_log,
    dt_bias,
    decay_down,
    decay_up,
    beta_weight,
    gate_down,
    gate_up,
    norm_gain,
    out_weight,
):
    heads, size = decay_log.shape[0], norm_gain.shape[0]
    channels = heads * size
    devices = lax.axis_size("head")
    weight = qkv_weight.transpose(1, 0, 2)
    fetched = load(hidden_in, decay_down, gate_down, beta_weight.T, weight)
    slabs, rims, fetched = gathered(hidden_in, fetched)
    *pairs, solved, attend, start, gate_low = front(
        rims, slabs, fetched, (decay_log, decay_up, dt_bias[None], conv_weight), weight, size
    )
    count = start.shape[1]
    raised, output_rows, out_gate = vmem_call(
        rows_body,
        (
            jax.ShapeDtypeStruct((heads, count, size), bf16),
            jax.ShapeDtypeStruct((count, channels), f32),
            jax.ShapeDtypeStruct((count, channels), f32),
        ),
        (attend, solved, start, gate_low, gate_up),
        grant=8,
        flops=2 * heads * count * count * 2 * size,
        moved=4 * heads * count * count,
    )
    states = [entry_states(*both) for both in zip(pairs[:GROUPS], pairs[GROUPS:])]
    states = [own for own, _ in states] + [other for _, other in states]
    slab_rows = count // devices
    sums = {}
    for g in reversed(range(max(devices // 2, 1))):
        places = [2 * g, 2 * g + 1][:devices]
        keep, *send = back(
            places, states, raised, output_rows, out_gate, norm_gain[None], out_weight, slab_rows
        )
        sums[g] = [keep] + [swapped(part, "head", 1).astype(f32) for part in send]
    for bit in bits_of(devices)[1:]:
        for g in sorted(sums):
            if 2 * g & bit:
                arrived = swapped(sum(sums.pop(g)).astype(bf16), "head", bit)
                sums[g ^ bit // 2].append(arrived.astype(f32))
    return sum(sums[0]).astype(bf16)


def solution(mesh):
    return jax.shard_map(
        shards,
        mesh=mesh,
        in_specs=(
            P(("seq", "head"), None),
            P(None, None, "head"),
            P(None, None, "head"),
            P("head"),
            P("head"),
            P(),
            P(None, "head"),
            P(None, "head"),
            P(),
            P(None, "head"),
            P(),
            P("head", None),
        ),
        out_specs=P(("seq", "head"), None),
        check_vma=False,
    )
```

```python
import functools
import math

import jax
import jax.numpy as jnp
from jax import lax
from jax.experimental import pallas as pl
from jax.experimental.pallas import tpu as pltpu
from jax.sharding import PartitionSpec as P

RIM = 16
BASE = 16
GROUPS = 2
MIB = 1024 * 1024
f32 = jnp.float32
bf16 = jnp.bfloat16


def dot(left, right, contract=((1,), (0,))):
    return lax.dot_general(left, right, (contract, ((), ())), preferred_element_type=f32)


def swapped(block, axis, bit):
    return lax.ppermute(block, axis, [(i, i ^ bit) for i in range(lax.axis_size(axis))])


def bits_of(size):
    assert size & (size - 1) == 0
    return [1 << i for i in range(size.bit_length() - 1)]


def rim_route(target):
    heads, seqs = lax.axis_size("head"), lax.axis_size("seq")
    return [(s * heads + heads - 1, (s + 1) * heads + target) for s in range(seqs - 1)]


def pick_body(targets, *refs):
    *tail_refs, rim_ref = refs
    rim = jnp.zeros(rim_ref.shape, f32)
    for target, ref in zip(targets, tail_refs):
        rim = jnp.where(place("head") == target, ref[...].astype(f32), rim)
    rim_ref[...] = rim.astype(rim_ref.dtype)


def gathered(own, loaded):
    heads = lax.axis_size("head")
    bits = bits_of(heads)
    assert bits
    slabs = {0: own}
    for bit in reversed(bits[1:]):
        for k in sorted(slabs):
            slabs[k ^ bit] = swapped(slabs[k], "head", bit)
    tail = own[own.shape[0] - RIM :]
    targets = [first if first == heads - 2 else first + 1 for first in range(0, heads, 2)][::-1]
    tails = [lax.ppermute(tail, ("seq", "head"), rim_route(target)) for target in targets]
    slabs[1] = swapped(own, "head", 1)
    arrived = [k for k in sorted(slabs) if k > 1]
    moved, tails, loaded = lax.optimization_barrier(
        ([slabs[k] for k in arrived], tails, loaded)
    )
    for k, slab in zip(arrived, moved):
        slabs[k], slabs[k ^ 1] = slab, swapped(slab, "head", 1)
    rim = vmem_call(
        functools.partial(pick_body, targets), jax.ShapeDtypeStruct(tail.shape, bf16), tails
    )
    return [slabs[k] for k in range(1, heads)], [rim, swapped(rim, "head", 1)], loaded


def vmem_call(body, out_shape, args, scratch=(), hbm=0, grant=4, flops=0, moved=0):
    here = len(args) - hbm
    args = [pltpu.with_memory_space_constraint(a, pltpu.HBM) if i >= here else a for i, a in enumerate(args)]
    spaces = [pltpu.VMEM] * here + [pltpu.HBM] * hbm
    return pl.pallas_call(
        body,
        out_shape=out_shape,
        in_specs=[pl.BlockSpec(memory_space=space) for space in spaces],
        out_specs=jax.tree.map(lambda _: pl.BlockSpec(memory_space=pltpu.VMEM), out_shape),
        scratch_shapes=list(scratch),
        compiler_params=pltpu.CompilerParams(vmem_limit_bytes=grant * MIB),
        cost_estimate=pl.CostEstimate(flops=flops, bytes_accessed=moved, transcendentals=0),
    )(*args)


def place(axis, bit=None):
    here = lax.axis_index(axis)
    return here if bit is None else here // bit % 2


def column_pieces(width):
    step = math.gcd(width, 256)
    return [slice(i, i + step) for i in range(0, width, step)]


def load_body(
    hidden_ref, decay_down_ref, gate_down_ref, beta_ref, weight_ref,
    own_ref, weights, downs, betas, sems,
):
    rank = decay_down_ref.shape[1]
    copies = [
        pltpu.make_async_copy(hidden_ref, own_ref, sems.at[0]),
        pltpu.make_async_copy(decay_down_ref, downs.at[:, pl.ds(0, rank)], sems.at[1]),
        pltpu.make_async_copy(gate_down_ref, downs.at[:, pl.ds(rank, rank)], sems.at[2]),
        pltpu.make_async_copy(beta_ref, betas, sems.at[3]),
    ]
    for c in range(2):
        copies.append(pltpu.make_async_copy(weight_ref.at[c], weights.at[c], sems.at[4 + c]))
    for copy in copies:
        copy.start()
    for copy in copies:
        copy.wait()


def load(own, decay_down, gate_down, beta, weight):
    width, rank = decay_down.shape
    return vmem_call(
        load_body,
        (
            jax.ShapeDtypeStruct(own.shape, bf16),
            jax.ShapeDtypeStruct((2, *weight.shape[1:]), bf16),
            jax.ShapeDtypeStruct((width, 2 * rank), bf16),
            jax.ShapeDtypeStruct(beta.shape, bf16),
        ),
        (own, decay_down, gate_down, beta, weight),
        scratch=[pltpu.SemaphoreType.DMA((6,))],
        hbm=5,
        grant=8,
    )


def front_body(slab_count, *refs):
    (one_ref, two_ref, *slab_refs), refs = refs[: slab_count + 1], refs[slab_count + 1 :]
    (own_rows_ref, weights, downs, betas), refs = refs[:4], refs[4:]
    hbm_refs, refs = refs[:5], refs[5:]
    (own_refs, other_refs), refs = (refs[:GROUPS], refs[GROUPS : 2 * GROUPS]), refs[2 * GROUPS :]
    (solved_ref, attend_ref, start_ref, gate_ref), refs = refs[:4], refs[4:]
    loaded, refs = refs[:5], refs[5:]
    rows_ref, projected, running_ref, parts_ref, mixing, inverse, sides, sems = refs
    rates, decay_up_ref, bias_ref, conv_ref, value_weight = loaded
    weight_ref = hbm_refs[-1]
    heads, count, size = start_ref.shape
    slab_rows = count // slab_count
    tap_count = conv_ref.shape[1]
    rank = decay_up_ref.shape[0]
    chunk = math.gcd(count, 64)
    chunks = count // chunk
    block = math.gcd(count, 128)
    blocks = count // block
    here = place("head")

    def rows_of(k):
        return pl.ds(pl.multiple_of(RIM + (here ^ k) * slab_rows, 16), slab_rows)

    small = [pltpu.make_async_copy(hbm_refs[i], loaded[i], sems.at[i]) for i in range(4)]
    pieces = column_pieces(heads * size)
    streams = []
    for i, piece in enumerate(pieces):
        streams.append(
            pltpu.make_async_copy(
                weight_ref.at[2, :, piece], value_weight.at[:, piece], sems.at[4 + i]
            )
        )
    for copy in small + streams:
        copy.start()
    rows_ref[:RIM, :] = (one_ref[...].astype(f32) + two_ref[...].astype(f32)).astype(bf16)
    for k, ref in enumerate([own_rows_ref, *slab_refs]):
        rows_ref[rows_of(k), :] = ref[...]

    def project(c, piece, weight):
        result = dot(rows_ref[...], weight)
        for begin in range(piece.start, piece.stop, size):
            at = begin - piece.start
            projected[c * heads + begin // size] = result[:, at : at + size]

    for c in range(2):
        for piece in pieces:
            project(c, piece, weights[c, :, piece])
    low = dot(rows_ref[RIM:, :], downs[...]).astype(bf16)
    gate_ref[...] = low[:, rank:]
    strength = jax.nn.sigmoid(dot(rows_ref[RIM:, :], betas[...], ((1,), (1,))))
    for copy in small:
        copy.wait()
    running_ref[...] = dot(low[:, :rank], decay_up_ref[...])
    tiles = [slice(a * chunk, (a + 1) * chunk) for a in range(chunks)]
    for h in range(heads):
        lanes = slice(h * size, (h + 1) * size)
        rate = jnp.exp(jnp.full((1, size), rates[h], f32))
        for rows in tiles:
            raw = running_ref[rows, lanes] + bias_ref[:, lanes]
            softplus = jnp.maximum(raw, 0.0) + jnp.log(1.0 + jnp.exp(-jnp.abs(raw)))
            log_decay = -rate * softplus
            high = log_decay.astype(bf16)
            parts_ref[rows, lanes] = high
            rest = (log_decay - high.astype(f32)).astype(bf16)
            parts_ref[count + rows.start : count + rows.stop, lanes] = rest
    row = lax.broadcasted_iota(jnp.int32, (count, count), 0)
    col = lax.broadcasted_iota(jnp.int32, (count, count), 1)
    lower = jnp.where(row >= col, 1.0, 0.0).astype(bf16)
    running_ref[...] = dot(jnp.concatenate([lower, lower], axis=1), parts_ref[...])

    def convolved(c, rows, h):
        taps = conv_ref[c].astype(f32)[:, h * size : (h + 1) * size]
        total = None
        for i in range(tap_count):
            first = RIM - tap_count + 1 + i + rows.start
            term = projected[c * heads + h, pl.ds(first, chunk), :] * taps[i : i + 1]
            total = term if total is None else total + term
        half = 0.5 * total
        return half + half * jnp.tanh(half)

    for i, piece in enumerate(pieces):
        streams[i].wait()
        project(2, piece, value_weight[:, piece])

    stops = []
    for h in range(heads):
        lanes = slice(h * size, (h + 1) * size)
        last = running_ref[count - 1 : count, lanes]
        middles, key_falls, stop, lefts = [], [], [], []
        for rows in tiles:
            running = running_ref[rows, lanes]
            middle = running[chunk // 2 : chunk // 2 + 1]
            above = running - middle
            rise, entry = jnp.exp(above), jnp.exp(middle)
            queries = convolved(0, rows, h)
            power = jnp.sum(queries * queries, -1, keepdims=True)
            queries = queries * (lax.rsqrt(power + 1e-06) * size ** (-0.5)) * rise
            start_ref[h, rows, :] = (queries * entry).astype(bf16)
            keys = convolved(1, rows, h)
            power = jnp.sum(keys * keys, -1, keepdims=True)
            keys = keys * lax.rsqrt(power + 1e-06)
            key_fall = keys * strength[rows, h : h + 1] * jnp.exp(-above)
            keys = keys * rise
            sides[h, rows, :size] = (keys * entry).astype(bf16)
            stop.append((key_fall * jnp.exp(last - middle)).astype(bf16))
            middles.append(middle)
            key_falls.append(key_fall)
            lefts.append(jnp.concatenate([keys.astype(bf16), queries.astype(bf16)], axis=0))
        stops.append((jnp.concatenate(stop, axis=0), jnp.exp(last)))
        for a in range(chunks):
            rows = tiles[a]
            reach = (a * chunk // block + 1) * block
            falls = []
            for b in range(reach // chunk):
                if b < a:
                    falls.append(key_falls[b] * jnp.exp(middles[a] - middles[b]))
                elif b == a:
                    falls.append(key_falls[b])
                else:
                    falls.append(jnp.zeros((chunk, size), f32))
            right = jnp.concatenate(falls, axis=0).astype(bf16)
            scores = dot(lefts[a], right, ((1,), (1,)))
            inside = slice(reach - block, reach)
            if reach > block:
                before = slice(0, reach - block)
                mixing[h, rows, before] = scores[:chunk, before].astype(bf16)
                attend_ref[h, rows, before] = scores[chunk:, before].astype(bf16)
            at, to = row[rows, inside], col[rows, inside]
            mixing[h, rows, inside] = jnp.where(at > to, scores[:chunk, inside], 0.0).astype(bf16)
            attend_ref[h, rows, inside] = jnp.where(
                at >= to, scores[chunk:, inside], 0.0
            ).astype(bf16)

    at, to = row[:block, :block], col[:block, :block]
    eye = jnp.where(at == to, 1.0, 0.0).astype(bf16)
    base = math.gcd(block, BASE)
    near = jnp.where(at // base == to // base, -1.0, 0.0).astype(bf16)
    corners = [(h, slice(d * block, (d + 1) * block)) for h in range(heads) for d in range(blocks)]
    powers = [mixing[h, d, d] * near for h, d in corners]
    totals = [power + eye for power in powers]
    steps = (base - 1).bit_length() - 1
    if steps:
        powers = [dot(power, power).astype(bf16) for power in powers]
    for step in range(steps):
        for n in range(len(corners)):
            power, total = powers[n], totals[n]
            if step < steps - 1:
                both = dot(jnp.concatenate([power, total], axis=0), power)
                powers[n], more = both[:block].astype(bf16), both[block:]
            else:
                more = dot(total, power)
            totals[n] = (total.astype(f32) + more).astype(bf16)
    for (h, d), total in zip(corners, totals):
        inverse[h, d, :] = total
    width = base
    while width < block:
        odd = range(width, block, 2 * width)
        pair_mask = (at // width % 2 == 1) & (to // width == at // width - 1)
        pair_mask = jnp.where(pair_mask, 1.0, 0.0).astype(bf16)
        halves = []
        for h, d in corners:
            parts = [inverse[h, d.start + i : d.start + i + width, :] for i in odd]
            chosen = jnp.concatenate(parts, axis=0)
            halves.append((chosen, dot(chosen, mixing[h, d, d] * pair_mask).astype(bf16)))
        for (h, d), (chosen, half) in zip(corners, halves):
            new = (chosen.astype(f32) - dot(half, inverse[h, d, :])).astype(bf16)
            for n, i in enumerate(odd):
                inverse[h, d.start + i : d.start + i + width, :] = new[n * width : (n + 1) * width]
        width *= 2

    for h in range(heads):
        for rows in tiles:
            sides[h, rows, size:] = convolved(2, rows, h).astype(bf16)
    for d in range(blocks):
        rows = slice(d * block, (d + 1) * block)
        for h in range(heads):
            side = sides[h, rows, :]
            if d:
                done = solved_ref[h, : d * block, :]
                side = (side.astype(f32) - dot(mixing[h, rows, : d * block], done)).astype(bf16)
            solved_ref[h, rows, :] = dot(inverse[h, rows, :], side).astype(bf16)
    pairs = []
    unit = row[:size, :size] == col[:size, :size]
    for h in range(heads):
        stop, fade = stops[h]
        moved = dot(stop, solved_ref[h], ((0,), (0,)))
        diagonal = jnp.where(unit, jnp.broadcast_to(fade, (size, size)), 0.0)
        pairs.append(jnp.concatenate([diagonal - moved[:, :size], moved[:, size:]], axis=1))
    upper = place("seq", 1) == 1
    for h in range(heads // 2):
        low, high = pairs[h], pairs[heads // 2 + h]
        group, at = divmod(h, own_refs[0].shape[0])
        own_refs[group][at] = jnp.where(upper, high, low).astype(bf16)
        other_refs[group][at] = jnp.where(upper, low, high).astype(bf16)


def front(rims, slabs, fetched, loaded, weight, size):
    slab_count, slab_rows = 1 + len(slabs), slabs[0].shape[0]
    count = slab_count * slab_rows
    _, width, channels = weight.shape
    heads, block = channels // size, math.gcd(count, 128)
    buffers = [pltpu.SMEM(loaded[0].shape, f32)]
    buffers += [pltpu.VMEM(part.shape, part.dtype) for part in loaded[1:]]
    return vmem_call(
        functools.partial(front_body, slab_count),
        (
            *[jax.ShapeDtypeStruct((heads // 2 // GROUPS, size, 2 * size), bf16)] * (2 * GROUPS),
            jax.ShapeDtypeStruct((heads, count, 2 * size), bf16),
            jax.ShapeDtypeStruct((heads, count, count), bf16),
            jax.ShapeDtypeStruct((heads, count, size), bf16),
            jax.ShapeDtypeStruct((count, fetched[2].shape[1] // 2), bf16),
        ),
        (*rims, *slabs, *fetched, *loaded, weight),
        scratch=[
            *buffers,
            pltpu.VMEM((width, channels), bf16),
            pltpu.VMEM((RIM + count, width), bf16),
            pltpu.VMEM((3 * heads, RIM + count, size), f32),
            pltpu.VMEM((count, channels), f32),
            pltpu.VMEM((2 * count, channels), bf16),
            pltpu.VMEM((heads, count, count), bf16),
            pltpu.VMEM((heads, count, block), bf16),
            pltpu.VMEM((heads, count, 2 * size), bf16),
            pltpu.SemaphoreType.DMA((4 + len(column_pieces(channels)),)),
        ],
        hbm=1 + len(loaded),
        grant=24,
        flops=2 * count * width * channels * 4,
        moved=2 * 4 * width * channels,
    )


def rows_body(attend_ref, solved_ref, start_ref, low_ref, up_ref, raised_ref, output_ref, gate_ref):
    heads, _, size = start_ref.shape
    gate_ref[...] = jax.nn.sigmoid(dot(low_ref[...], up_ref[...]))
    count = attend_ref.shape[1]
    block = math.gcd(count, 128)
    for h in range(heads):
        for begin in range(0, count, block):
            rows, reach = slice(begin, begin + block), slice(0, begin + block)
            both = dot(attend_ref[h, rows, reach], solved_ref[h, reach, :])
            raised_ref[h, rows, :] = (start_ref[h, rows, :].astype(f32) - both[:, :size]).astype(bf16)
            output_ref[rows, h * size : (h + 1) * size] = both[:, size:]


def composed(later, first, size):
    both = dot(later[:, :size], first)
    return both[:, :size], both[:, size:] + later[:, size:].astype(f32)


def put(ref, h, pair):
    size = ref.shape[1]
    if ref.shape[2] > size:
        ref[h, :, :size] = pair[0].astype(bf16)
    ref[h, :, ref.shape[2] - size :] = pair[1].astype(bf16)


def join_body(bit, own_ref, far_ref, total_ref):
    heads, size, _ = own_ref.shape
    for h in range(heads):
        own, far = own_ref[h], far_ref[h]
        upper = place("seq", bit) == 1
        later, first = jnp.where(upper, own, far), jnp.where(upper, far, own)
        put(total_ref, h, composed(later, first, size))


def join(bit, own, far, last):
    heads, size, width = own.shape
    return vmem_call(
        functools.partial(join_body, bit),
        jax.ShapeDtypeStruct((heads, size, size if last else width), bf16),
        (own, far),
        flops=2 * heads * size * size * width,
        moved=6 * heads * size * width,
    )


def before_body(bit, far_ref, *refs):
    *near_refs, out_ref = refs
    heads, size, width = far_ref.shape
    row = lax.broadcasted_iota(jnp.int32, (size, width), 0)
    col = lax.broadcasted_iota(jnp.int32, (size, width), 1)
    for h in range(heads):
        if near_refs:
            near = near_refs[0][h]
            pair = jnp.concatenate(composed(near, far_ref[h], size), axis=1)
            near = near.astype(f32)
        else:
            near, pair = jnp.where(row == col, 1.0, 0.0), far_ref[h].astype(f32)
        out_ref[h] = jnp.where(place("seq", bit) == 1, pair, near).astype(bf16)


def before(bit, near, far):
    return vmem_call(
        functools.partial(before_body, bit),
        jax.ShapeDtypeStruct(far.shape, bf16),
        (far, *near),
        flops=2 * math.prod(far.shape) * far.shape[1],
        moved=6 * math.prod(far.shape),
    )


def entry_body(bit, near_ref, far_ref, own_ref, partner_ref, keep_ref, send_ref):
    heads, size, _ = near_ref.shape
    arrived, upper = place("seq", bit) == 1, place("seq", 1) == 1
    for h in range(heads):
        state = dot(near_ref[h, :, :size], far_ref[h])
        state = jnp.where(arrived, state, 0.0) + near_ref[h, :, size:].astype(f32)
        first = jnp.where(upper, partner_ref[h], own_ref[h])
        state = state.astype(bf16)
        later = dot(first[:, :size], state) + first[:, size:].astype(f32)
        later = later.astype(bf16)
        keep_ref[h] = jnp.where(upper, later, state)
        send_ref[h] = jnp.where(upper, state, later)


def entry_states(own, other):
    heads, size, width = own.shape
    bits = bits_of(lax.axis_size("seq"))
    partner = swapped(other, "seq", 1)
    total = join(1, own, partner, len(bits) == 2)
    near = ()
    assert len(bits) > 2
    for bit in bits[1:-1]:
        far = swapped(total, "seq", bit)
        total = join(bit, total, far, 2 * bit == bits[-1])
        near = (before(bit, near, far),)
    far = swapped(total, "seq", bits[-1])
    state = jax.ShapeDtypeStruct((heads, size, size), bf16)
    keep, send = vmem_call(
        functools.partial(entry_body, bits[-1]),
        (state, state),
        (*near, far, own, partner),
        flops=4 * heads * size * size * size,
        moved=14 * heads * size * size,
    )
    return keep, swapped(send, "seq", 1)


def back_body(places, *refs):
    own_refs, other_refs, refs = refs[:GROUPS], refs[GROUPS : 2 * GROUPS], refs[2 * GROUPS :]
    raised_ref, output_ref, gate_ref, gain_ref, weight_ref, keep_ref, *rest = refs
    normed = rest[-1]
    size = gain_ref.shape[1]
    slab_rows = keep_ref.shape[0]
    share = own_refs[0].shape[0]
    half = GROUPS * share
    upper = place("seq", 1) == 1
    for k, away in enumerate(places):
        rows = pl.ds(pl.multiple_of((place("head") ^ away) * slab_rows, 16), slab_rows)
        for h in range(raised_ref.shape[0]):
            lanes = slice(h * size, (h + 1) * size)
            group, at = divmod(h % half, share)
            own, other = own_refs[group][at], other_refs[group][at]
            state = jnp.where(upper, other, own) if h < half else jnp.where(upper, own, other)
            attended = dot(raised_ref[h, rows, :], state) + output_ref[rows, lanes]
            power = jnp.sum(attended * attended, -1, keepdims=True) * (1.0 / size)
            normed[k * slab_rows : (k + 1) * slab_rows, lanes] = (
                attended * lax.rsqrt(power + 1e-05) * gain_ref[...] * gate_ref[rows, lanes]
            ).astype(bf16)
    total = dot(normed[...], weight_ref[...])
    keep_ref[...] = total[:slab_rows]
    if len(rest) > 1:
        rest[0][...] = total[slab_rows:].astype(bf16)


def back(places, states, raised, output_rows, out_gate, gain, weight, slab_rows):
    slab_count, width = len(places), weight.shape[1]
    shapes = [jax.ShapeDtypeStruct((slab_rows, width), f32)]
    if slab_count > 1:
        shapes.append(jax.ShapeDtypeStruct((slab_rows, width), bf16))
    return vmem_call(
        functools.partial(back_body, places),
        shapes,
        (*states, raised, output_rows, out_gate, gain, weight),
        scratch=[pltpu.VMEM((slab_count * slab_rows, weight.shape[0]), bf16)],
        grant=10,
        flops=2 * slab_count * slab_rows * weight.shape[0] * width,
        moved=2 * weight.shape[0] * width,
    )


def shards(
    hidden_in,
    qkv_weight,
    conv_weight,
    decay_log,
    dt_bias,
    decay_down,
    decay_up,
    beta_weight,
    gate_down,
    gate_up,
    norm_gain,
    out_weight,
):
    heads, size = decay_log.shape[0], norm_gain.shape[0]
    channels = heads * size
    devices = lax.axis_size("head")
    weight = qkv_weight.transpose(1, 0, 2)
    fetched = load(hidden_in, decay_down, gate_down, beta_weight.T, weight)
    slabs, rims, fetched = gathered(hidden_in, fetched)
    *pairs, solved, attend, start, gate_low = front(
        rims, slabs, fetched, (decay_log, decay_up, dt_bias[None], conv_weight), weight, size
    )
    count = start.shape[1]
    raised, output_rows, out_gate = vmem_call(
        rows_body,
        (
            jax.ShapeDtypeStruct((heads, count, size), bf16),
            jax.ShapeDtypeStruct((count, channels), f32),
            jax.ShapeDtypeStruct((count, channels), f32),
        ),
        (attend, solved, start, gate_low, gate_up),
        grant=8,
        flops=2 * heads * count * count * 2 * size,
        moved=4 * heads * count * count,
    )
    states = [entry_states(*both) for both in zip(pairs[:GROUPS], pairs[GROUPS:])]
    states = [own for own, _ in states] + [other for _, other in states]
    slab_rows = count // devices
    sums = {}
    for g in reversed(range(max(devices // 2, 1))):
        places = [2 * g, 2 * g + 1][:devices]
        keep, *send = back(
            places, states, raised, output_rows, out_gate, norm_gain[None], out_weight, slab_rows
        )
        near = [swapped(part, "head", 1).astype(f32) for part in send]
        sums[g] = [lax.optimization_barrier(sum([keep] + near))]
    for bit in bits_of(devices)[1:]:
        for g in sorted(sums):
            if 2 * g & bit:
                arrived = swapped(sum(sums.pop(g)).astype(bf16), "head", bit)
                sums[g ^ bit // 2].append(arrived.astype(f32))
    return sum(sums[0]).astype(bf16)


def solution(mesh):
    return jax.shard_map(
        shards,
        mesh=mesh,
        in_specs=(
            P(("seq", "head"), None),
            P(None, None, "head"),
            P(None, None, "head"),
            P("head"),
            P("head"),
            P(),
            P(None, "head"),
            P(None, "head"),
            P(),
            P(None, "head"),
            P(),
            P("head", None),
        ),
        out_specs=P(("seq", "head"), None),
        check_vma=False,
    )
```

```python
import functools
import math

import jax
import jax.numpy as jnp
from jax import lax
from jax.experimental import pallas as pl
from jax.experimental.pallas import tpu as pltpu
from jax.sharding import PartitionSpec as P

RIM = 16
BASE = 16
GROUPS = 2
MIB = 1024 * 1024
f32 = jnp.float32
bf16 = jnp.bfloat16


def dot(left, right, contract=((1,), (0,))):
    return lax.dot_general(left, right, (contract, ((), ())), preferred_element_type=f32)


def swapped(block, axis, bit):
    return lax.ppermute(block, axis, [(i, i ^ bit) for i in range(lax.axis_size(axis))])


def bits_of(size):
    assert size & (size - 1) == 0
    return [1 << i for i in range(size.bit_length() - 1)]


def rim_route(target):
    heads, seqs = lax.axis_size("head"), lax.axis_size("seq")
    return [(s * heads + heads - 1, (s + 1) * heads + target) for s in range(seqs - 1)]


def pick_body(targets, *refs):
    *tail_refs, rim_ref = refs
    rim = jnp.zeros(tail_refs[0].shape, f32)
    above = jnp.zeros((rim_ref.shape[0] - rim.shape[0], rim.shape[1]), f32)
    for target, ref in zip(targets, tail_refs):
        rim = jnp.where(place("head") == target, ref[...].astype(f32), rim)
    rim_ref[...] = jnp.concatenate([above, rim], axis=0).astype(rim_ref.dtype)


def gathered(own, loaded):
    heads = lax.axis_size("head")
    bits = bits_of(heads)
    assert bits
    slabs = {0: own}
    for bit in reversed(bits[1:]):
        for k in sorted(slabs):
            slabs[k ^ bit] = swapped(slabs[k], "head", bit)
    tail = own[own.shape[0] - RIM // 2 :]
    targets = [first if first == heads - 2 else first + 1 for first in range(0, heads, 2)][::-1]
    tails = [lax.ppermute(tail, ("seq", "head"), rim_route(target)) for target in targets]
    slabs[1] = swapped(own, "head", 1)
    arrived = [k for k in sorted(slabs) if k > 1]
    moved, tails, loaded = lax.optimization_barrier(
        ([slabs[k] for k in arrived], tails, loaded)
    )
    for k, slab in zip(arrived, moved):
        slabs[k], slabs[k ^ 1] = slab, swapped(slab, "head", 1)
    rim = vmem_call(
        functools.partial(pick_body, targets), jax.ShapeDtypeStruct((RIM, own.shape[1]), bf16), tails
    )
    return [slabs[k] for k in range(1, heads)], [rim, swapped(rim, "head", 1)], loaded


def vmem_call(body, out_shape, args, scratch=(), hbm=0, grant=4, flops=0, moved=0):
    here = len(args) - hbm
    args = [pltpu.with_memory_space_constraint(a, pltpu.HBM) if i >= here else a for i, a in enumerate(args)]
    spaces = [pltpu.VMEM] * here + [pltpu.HBM] * hbm
    return pl.pallas_call(
        body,
        out_shape=out_shape,
        in_specs=[pl.BlockSpec(memory_space=space) for space in spaces],
        out_specs=jax.tree.map(lambda _: pl.BlockSpec(memory_space=pltpu.VMEM), out_shape),
        scratch_shapes=list(scratch),
        compiler_params=pltpu.CompilerParams(vmem_limit_bytes=grant * MIB),
        cost_estimate=pl.CostEstimate(flops=flops, bytes_accessed=moved, transcendentals=0),
    )(*args)


def place(axis, bit=None):
    here = lax.axis_index(axis)
    return here if bit is None else here // bit % 2


def column_pieces(width):
    step = math.gcd(width, 256)
    return [slice(i, i + step) for i in range(0, width, step)]


def load_body(
    hidden_ref, decay_down_ref, gate_down_ref, beta_ref, weight_ref,
    own_ref, weights, downs, betas, sems,
):
    rank = decay_down_ref.shape[1]
    copies = [
        pltpu.make_async_copy(hidden_ref, own_ref, sems.at[0]),
        pltpu.make_async_copy(decay_down_ref, downs.at[:, pl.ds(0, rank)], sems.at[1]),
        pltpu.make_async_copy(gate_down_ref, downs.at[:, pl.ds(rank, rank)], sems.at[2]),
        pltpu.make_async_copy(beta_ref, betas, sems.at[3]),
    ]
    for c in range(2):
        copies.append(pltpu.make_async_copy(weight_ref.at[c], weights.at[c], sems.at[4 + c]))
    for copy in copies:
        copy.start()
    for copy in copies:
        copy.wait()


def load(own, decay_down, gate_down, beta, weight):
    width, rank = decay_down.shape
    return vmem_call(
        load_body,
        (
            jax.ShapeDtypeStruct(own.shape, bf16),
            jax.ShapeDtypeStruct((2, *weight.shape[1:]), bf16),
            jax.ShapeDtypeStruct((width, 2 * rank), bf16),
            jax.ShapeDtypeStruct(beta.shape, bf16),
        ),
        (own, decay_down, gate_down, beta, weight),
        scratch=[pltpu.SemaphoreType.DMA((6,))],
        hbm=5,
        grant=8,
    )


def front_body(slab_count, *refs):
    (one_ref, two_ref, *slab_refs), refs = refs[: slab_count + 1], refs[slab_count + 1 :]
    (own_rows_ref, weights, downs, betas), refs = refs[:4], refs[4:]
    hbm_refs, refs = refs[:5], refs[5:]
    (own_refs, other_refs), refs = (refs[:GROUPS], refs[GROUPS : 2 * GROUPS]), refs[2 * GROUPS :]
    (solved_ref, attend_ref, start_ref, gate_ref), refs = refs[:4], refs[4:]
    loaded, refs = refs[:5], refs[5:]
    rows_ref, projected, running_ref, parts_ref, mixing, inverse, sides, sems = refs
    rates, decay_up_ref, bias_ref, conv_ref, value_weight = loaded
    weight_ref = hbm_refs[-1]
    heads, count, size = start_ref.shape
    slab_rows = count // slab_count
    tap_count = conv_ref.shape[1]
    rank = decay_up_ref.shape[0]
    chunk = math.gcd(count, 64)
    chunks = count // chunk
    block = math.gcd(count, 128)
    blocks = count // block
    here = place("head")

    def rows_of(k):
        return pl.ds(pl.multiple_of(RIM + (here ^ k) * slab_rows, 16), slab_rows)

    small = [pltpu.make_async_copy(hbm_refs[i], loaded[i], sems.at[i]) for i in range(4)]
    pieces = column_pieces(heads * size)
    streams = []
    for i, piece in enumerate(pieces):
        streams.append(
            pltpu.make_async_copy(
                weight_ref.at[2, :, piece], value_weight.at[:, piece], sems.at[4 + i]
            )
        )
    for copy in small + streams:
        copy.start()
    rows_ref[:RIM, :] = (one_ref[...].astype(f32) + two_ref[...].astype(f32)).astype(bf16)
    for k, ref in enumerate([own_rows_ref, *slab_refs]):
        rows_ref[rows_of(k), :] = ref[...]

    def project(c, piece, weight):
        result = dot(rows_ref[...], weight)
        for begin in range(piece.start, piece.stop, size):
            at = begin - piece.start
            projected[c * heads + begin // size] = result[:, at : at + size]

    pending = [(c, piece) for piece in pieces for c in range(2)]
    share = (pieces[0].stop - pieces[0].start) // size

    def project_next(number):
        for c, piece in pending[:number]:
            project(c, piece, weights[c, :, piece])
        del pending[:number]

    project_next(2)
    low = dot(rows_ref[RIM:, :], downs[...]).astype(bf16)
    gate_ref[...] = low[:, rank:]
    strength = jax.nn.sigmoid(dot(rows_ref[RIM:, :], betas[...], ((1,), (1,))))
    for copy in small:
        copy.wait()
    running_ref[...] = dot(low[:, :rank], decay_up_ref[...])
    tiles = [slice(a * chunk, (a + 1) * chunk) for a in range(chunks)]
    for h in range(heads):
        lanes = slice(h * size, (h + 1) * size)
        rate = jnp.exp(jnp.full((1, size), rates[h], f32))
        for rows in tiles:
            raw = running_ref[rows, lanes] + bias_ref[:, lanes]
            softplus = jnp.maximum(raw, 0.0) + jnp.log(1.0 + jnp.exp(-jnp.abs(raw)))
            log_decay = -rate * softplus
            high = log_decay.astype(bf16)
            parts_ref[rows, lanes] = high
            rest = (log_decay - high.astype(f32)).astype(bf16)
            parts_ref[count + rows.start : count + rows.stop, lanes] = rest
    row = lax.broadcasted_iota(jnp.int32, (count, count), 0)
    col = lax.broadcasted_iota(jnp.int32, (count, count), 1)
    lower = jnp.where(row >= col, 1.0, 0.0).astype(bf16)
    running_ref[...] = dot(jnp.concatenate([lower, lower], axis=1), parts_ref[...])

    def convolved(c, rows, h):
        taps = conv_ref[c].astype(f32)[:, h * size : (h + 1) * size]
        total = None
        for i in range(tap_count):
            first = RIM - tap_count + 1 + i + rows.start
            term = projected[c * heads + h, pl.ds(first, chunk), :] * taps[i : i + 1]
            total = term if total is None else total + term
        half = 0.5 * total
        return half + half * jnp.tanh(half)

    for copy in streams:
        copy.wait()
    stops = []
    for h in range(heads):
        lanes = slice(h * size, (h + 1) * size)
        last = running_ref[count - 1 : count, lanes]
        middles, key_falls, stop, lefts = [], [], [], []
        for rows in tiles:
            running = running_ref[rows, lanes]
            middle = running[chunk // 2 : chunk // 2 + 1]
            above = running - middle
            rise, entry = jnp.exp(above), jnp.exp(middle)
            queries = convolved(0, rows, h)
            power = jnp.sum(queries * queries, -1, keepdims=True)
            queries = queries * (lax.rsqrt(power + 1e-06) * size ** (-0.5)) * rise
            start_ref[h, rows, :] = (queries * entry).astype(bf16)
            keys = convolved(1, rows, h)
            power = jnp.sum(keys * keys, -1, keepdims=True)
            keys = keys * lax.rsqrt(power + 1e-06)
            key_fall = keys * strength[rows, h : h + 1] * jnp.exp(-above)
            keys = keys * rise
            sides[h, rows, :size] = (keys * entry).astype(bf16)
            stop.append((key_fall * jnp.exp(last - middle)).astype(bf16))
            middles.append(middle)
            key_falls.append(key_fall)
            lefts.append(jnp.concatenate([keys.astype(bf16), queries.astype(bf16)], axis=0))
        stops.append((jnp.concatenate(stop, axis=0), jnp.exp(last)))
        project_next(pl.cdiv(2, share))
        for a in range(chunks):
            rows = tiles[a]
            reach = (a * chunk // block + 1) * block
            falls = []
            for b in range(reach // chunk):
                if b < a:
                    falls.append(key_falls[b] * jnp.exp(middles[a] - middles[b]))
                elif b == a:
                    falls.append(key_falls[b])
                else:
                    falls.append(jnp.zeros((chunk, size), f32))
            right = jnp.concatenate(falls, axis=0).astype(bf16)
            scores = dot(lefts[a], right, ((1,), (1,)))
            inside = slice(reach - block, reach)
            if reach > block:
                before = slice(0, reach - block)
                mixing[h, rows, before] = scores[:chunk, before].astype(bf16)
                attend_ref[h, rows, before] = scores[chunk:, before].astype(bf16)
            at, to = row[rows, inside], col[rows, inside]
            mixing[h, rows, inside] = jnp.where(at > to, scores[:chunk, inside], 0.0).astype(bf16)
            attend_ref[h, rows, inside] = jnp.where(
                at >= to, scores[chunk:, inside], 0.0
            ).astype(bf16)

    def value_side(h):
        for rows in tiles:
            sides[h, rows, size:] = convolved(2, rows, h).astype(bf16)

    between = [functools.partial(project, 2, p, value_weight[:, p]) for p in pieces]
    between += [functools.partial(value_side, h) for h in range(heads)]

    at, to = row[:block, :block], col[:block, :block]
    eye = jnp.where(at == to, 1.0, 0.0).astype(bf16)
    base = math.gcd(block, BASE)
    near = jnp.where(at // base == to // base, -1.0, 0.0).astype(bf16)
    corners = [(h, slice(d * block, (d + 1) * block)) for h in range(heads) for d in range(blocks)]
    powers = [mixing[h, d, d] * near for h, d in corners]
    totals = [power + eye for power in powers]
    steps = (base - 1).bit_length() - 1
    if steps:
        powers = [dot(power, power).astype(bf16) for power in powers]
    for step in range(steps):
        for n in range(len(corners)):
            power, total = powers[n], totals[n]
            if step < steps - 1:
                both = dot(jnp.concatenate([power, total], axis=0), power)
                powers[n], more = both[:block].astype(bf16), both[block:]
            else:
                more = dot(total, power)
            totals[n] = (total.astype(f32) + more).astype(bf16)
        if between:
            between.pop(0)()
    for (h, d), total in zip(corners, totals):
        inverse[h, d, :] = total
    width = base
    while width < block:
        odd = range(width, block, 2 * width)
        pair_mask = (at // width % 2 == 1) & (to // width == at // width - 1)
        pair_mask = jnp.where(pair_mask, 1.0, 0.0).astype(bf16)
        halves = []
        for h, d in corners:
            parts = [inverse[h, d.start + i : d.start + i + width, :] for i in odd]
            chosen = jnp.concatenate(parts, axis=0)
            halves.append((chosen, dot(chosen, mixing[h, d, d] * pair_mask).astype(bf16)))
        for (h, d), (chosen, half) in zip(corners, halves):
            new = (chosen.astype(f32) - dot(half, inverse[h, d, :])).astype(bf16)
            for n, i in enumerate(odd):
                inverse[h, d.start + i : d.start + i + width, :] = new[n * width : (n + 1) * width]
        if between:
            between.pop(0)()
        width *= 2
    for work in between:
        work()

    for d in range(blocks):
        rows = slice(d * block, (d + 1) * block)
        for h in range(heads):
            side = sides[h, rows, :]
            if d:
                done = solved_ref[h, : d * block, :]
                side = (side.astype(f32) - dot(mixing[h, rows, : d * block], done)).astype(bf16)
            solved_ref[h, rows, :] = dot(inverse[h, rows, :], side).astype(bf16)
    pairs = []
    unit = row[:size, :size] == col[:size, :size]
    for h in range(heads):
        stop, fade = stops[h]
        moved = dot(stop, solved_ref[h], ((0,), (0,)))
        diagonal = jnp.where(unit, jnp.broadcast_to(fade, (size, size)), 0.0)
        pairs.append(jnp.concatenate([diagonal - moved[:, :size], moved[:, size:]], axis=1))
    upper = place("seq", 1) == 1
    for h in range(heads // 2):
        low, high = pairs[h], pairs[heads // 2 + h]
        group, at = divmod(h, own_refs[0].shape[0])
        own_refs[group][at] = jnp.where(upper, high, low).astype(bf16)
        other_refs[group][at] = jnp.where(upper, low, high).astype(bf16)


def front(rims, slabs, fetched, loaded, weight, size):
    slab_count, slab_rows = 1 + len(slabs), slabs[0].shape[0]
    count = slab_count * slab_rows
    _, width, channels = weight.shape
    heads, block = channels // size, math.gcd(count, 128)
    buffers = [pltpu.SMEM(loaded[0].shape, f32)]
    buffers += [pltpu.VMEM(part.shape, part.dtype) for part in loaded[1:]]
    return vmem_call(
        functools.partial(front_body, slab_count),
        (
            *[jax.ShapeDtypeStruct((heads // 2 // GROUPS, size, 2 * size), bf16)] * (2 * GROUPS),
            jax.ShapeDtypeStruct((heads, count, 2 * size), bf16),
            jax.ShapeDtypeStruct((heads, count, count), bf16),
            jax.ShapeDtypeStruct((heads, count, size), bf16),
            jax.ShapeDtypeStruct((count, fetched[2].shape[1] // 2), bf16),
        ),
        (*rims, *slabs, *fetched, *loaded, weight),
        scratch=[
            *buffers,
            pltpu.VMEM((width, channels), bf16),
            pltpu.VMEM((RIM + count, width), bf16),
            pltpu.VMEM((3 * heads, RIM + count, size), f32),
            pltpu.VMEM((count, channels), f32),
            pltpu.VMEM((2 * count, channels), bf16),
            pltpu.VMEM((heads, count, count), bf16),
            pltpu.VMEM((heads, count, block), bf16),
            pltpu.VMEM((heads, count, 2 * size), bf16),
            pltpu.SemaphoreType.DMA((4 + len(column_pieces(channels)),)),
        ],
        hbm=1 + len(loaded),
        grant=24,
        flops=2 * count * width * channels * 4,
        moved=2 * 4 * width * channels,
    )


def rows_body(attend_ref, solved_ref, start_ref, low_ref, up_ref, raised_ref, output_ref, gate_ref):
    heads, _, size = start_ref.shape
    gate_ref[...] = jax.nn.sigmoid(dot(low_ref[...], up_ref[...]))
    count = attend_ref.shape[1]
    block = math.gcd(count, 128)
    for h in range(heads):
        for begin in range(0, count, block):
            rows, reach = slice(begin, begin + block), slice(0, begin + block)
            both = dot(attend_ref[h, rows, reach], solved_ref[h, reach, :])
            raised_ref[h, rows, :] = (start_ref[h, rows, :].astype(f32) - both[:, :size]).astype(bf16)
            output_ref[rows, h * size : (h + 1) * size] = both[:, size:]


def composed(later, first, size):
    both = dot(later[:, :size], first)
    return both[:, :size], both[:, size:] + later[:, size:].astype(f32)


def put(ref, h, pair):
    size = ref.shape[1]
    if ref.shape[2] > size:
        ref[h, :, :size] = pair[0].astype(bf16)
    ref[h, :, ref.shape[2] - size :] = pair[1].astype(bf16)


def join_body(bit, own_ref, far_ref, total_ref):
    heads, size, _ = own_ref.shape
    for h in range(heads):
        own, far = own_ref[h], far_ref[h]
        upper = place("seq", bit) == 1
        later, first = jnp.where(upper, own, far), jnp.where(upper, far, own)
        put(total_ref, h, composed(later, first, size))


def join(bit, own, far, last):
    heads, size, width = own.shape
    return vmem_call(
        functools.partial(join_body, bit),
        jax.ShapeDtypeStruct((heads, size, size if last else width), bf16),
        (own, far),
        flops=2 * heads * size * size * width,
        moved=6 * heads * size * width,
    )


def before_body(bit, far_ref, *refs):
    *near_refs, out_ref = refs
    heads, size, width = far_ref.shape
    row = lax.broadcasted_iota(jnp.int32, (size, width), 0)
    col = lax.broadcasted_iota(jnp.int32, (size, width), 1)
    for h in range(heads):
        if near_refs:
            near = near_refs[0][h]
            pair = jnp.concatenate(composed(near, far_ref[h], size), axis=1)
            near = near.astype(f32)
        else:
            near, pair = jnp.where(row == col, 1.0, 0.0), far_ref[h].astype(f32)
        out_ref[h] = jnp.where(place("seq", bit) == 1, pair, near).astype(bf16)


def before(bit, near, far):
    return vmem_call(
        functools.partial(before_body, bit),
        jax.ShapeDtypeStruct(far.shape, bf16),
        (far, *near),
        flops=2 * math.prod(far.shape) * far.shape[1],
        moved=6 * math.prod(far.shape),
    )


def entry_body(bit, near_ref, far_ref, own_ref, partner_ref, keep_ref, send_ref):
    heads, size, _ = near_ref.shape
    arrived, upper = place("seq", bit) == 1, place("seq", 1) == 1
    for h in range(heads):
        state = dot(near_ref[h, :, :size], far_ref[h])
        state = jnp.where(arrived, state, 0.0) + near_ref[h, :, size:].astype(f32)
        first = jnp.where(upper, partner_ref[h], own_ref[h])
        state = state.astype(bf16)
        later = dot(first[:, :size], state) + first[:, size:].astype(f32)
        later = later.astype(bf16)
        keep_ref[h] = jnp.where(upper, later, state)
        send_ref[h] = jnp.where(upper, state, later)


def entry_states(own, other):
    heads, size, width = own.shape
    bits = bits_of(lax.axis_size("seq"))
    partner = swapped(other, "seq", 1)
    total = join(1, own, partner, len(bits) == 2)
    near = ()
    assert len(bits) > 2
    for bit in bits[1:-1]:
        far = swapped(total, "seq", bit)
        total = join(bit, total, far, 2 * bit == bits[-1])
        near = (before(bit, near, far),)
    far = swapped(total, "seq", bits[-1])
    state = jax.ShapeDtypeStruct((heads, size, size), bf16)
    keep, send = vmem_call(
        functools.partial(entry_body, bits[-1]),
        (state, state),
        (*near, far, own, partner),
        flops=4 * heads * size * size * size,
        moved=14 * heads * size * size,
    )
    return keep, swapped(send, "seq", 1)


def back_body(places, *refs):
    own_refs, other_refs, refs = refs[:GROUPS], refs[GROUPS : 2 * GROUPS], refs[2 * GROUPS :]
    raised_ref, output_ref, gate_ref, gain_ref, weight_ref, keep_ref, *rest = refs
    normed = rest[-1]
    size = gain_ref.shape[1]
    slab_rows = keep_ref.shape[0]
    share = own_refs[0].shape[0]
    half = GROUPS * share
    upper = place("seq", 1) == 1
    for k, away in enumerate(places):
        rows = pl.ds(pl.multiple_of((place("head") ^ away) * slab_rows, 16), slab_rows)
        for h in range(raised_ref.shape[0]):
            lanes = slice(h * size, (h + 1) * size)
            group, at = divmod(h % half, share)
            own, other = own_refs[group][at], other_refs[group][at]
            state = jnp.where(upper, other, own) if h < half else jnp.where(upper, own, other)
            attended = dot(raised_ref[h, rows, :], state) + output_ref[rows, lanes]
            power = jnp.sum(attended * attended, -1, keepdims=True) * (1.0 / size)
            normed[k * slab_rows : (k + 1) * slab_rows, lanes] = (
                attended * lax.rsqrt(power + 1e-05) * gain_ref[...] * gate_ref[rows, lanes]
            ).astype(bf16)
    total = dot(normed[...], weight_ref[...])
    keep_ref[...] = total[:slab_rows]
    if len(rest) > 1:
        rest[0][...] = total[slab_rows:].astype(bf16)


def back(places, states, raised, output_rows, out_gate, gain, weight, slab_rows):
    slab_count, width = len(places), weight.shape[1]
    shapes = [jax.ShapeDtypeStruct((slab_rows, width), f32)]
    if slab_count > 1:
        shapes.append(jax.ShapeDtypeStruct((slab_rows, width), bf16))
    return vmem_call(
        functools.partial(back_body, places),
        shapes,
        (*states, raised, output_rows, out_gate, gain, weight),
        scratch=[pltpu.VMEM((slab_count * slab_rows, weight.shape[0]), bf16)],
        grant=10,
        flops=2 * slab_count * slab_rows * weight.shape[0] * width,
        moved=2 * weight.shape[0] * width,
    )


def shards(
    hidden_in,
    qkv_weight,
    conv_weight,
    decay_log,
    dt_bias,
    decay_down,
    decay_up,
    beta_weight,
    gate_down,
    gate_up,
    norm_gain,
    out_weight,
):
    heads, size = decay_log.shape[0], norm_gain.shape[0]
    channels = heads * size
    devices = lax.axis_size("head")
    weight = qkv_weight.transpose(1, 0, 2)
    fetched = load(hidden_in, decay_down, gate_down, beta_weight.T, weight)
    slabs, rims, fetched = gathered(hidden_in, fetched)
    *pairs, solved, attend, start, gate_low = front(
        rims, slabs, fetched, (decay_log, decay_up, dt_bias[None], conv_weight), weight, size
    )
    count = start.shape[1]
    raised, output_rows, out_gate = vmem_call(
        rows_body,
        (
            jax.ShapeDtypeStruct((heads, count, size), bf16),
            jax.ShapeDtypeStruct((count, channels), f32),
            jax.ShapeDtypeStruct((count, channels), f32),
        ),
        (attend, solved, start, gate_low, gate_up),
        grant=8,
        flops=2 * heads * count * count * 2 * size,
        moved=4 * heads * count * count,
    )
    states = [entry_states(*both) for both in zip(pairs[:GROUPS], pairs[GROUPS:])]
    states = [own for own, _ in states] + [other for _, other in states]
    slab_rows = count // devices
    sums = {}
    for g in reversed(range(max(devices // 2, 1))):
        places = [2 * g, 2 * g + 1][:devices]
        keep, *send = back(
            places, states, raised, output_rows, out_gate, norm_gain[None], out_weight, slab_rows
        )
        near = [swapped(part, "head", 1).astype(f32) for part in send]
        sums[g] = [lax.optimization_barrier(sum([keep] + near))]
    for bit in bits_of(devices)[1:]:
        for g in sorted(sums):
            if 2 * g & bit:
                arrived = swapped(sum(sums.pop(g)).astype(bf16), "head", bit)
                sums[g ^ bit // 2].append(arrived.astype(f32))
    return sum(sums[0]).astype(bf16)


def solution(mesh):
    return jax.shard_map(
        shards,
        mesh=mesh,
        in_specs=(
            P(("seq", "head"), None),
            P(None, None, "head"),
            P(None, None, "head"),
            P("head"),
            P("head"),
            P(),
            P(None, "head"),
            P(None, "head"),
            P(),
            P(None, "head"),
            P(),
            P("head", None),
        ),
        out_specs=P(("seq", "head"), None),
        check_vma=False,
    )
```

```python
import functools
import itertools
import math

import jax
import jax.numpy as jnp
from jax import lax
from jax.experimental import pallas as pl
from jax.experimental.pallas import tpu as pltpu
from jax.sharding import PartitionSpec as P

RIM = 16
BASE = 16
GROUPS = 2
MIB = 1024 * 1024
f32 = jnp.float32
bf16 = jnp.bfloat16


def dot(left, right, contract=((1,), (0,))):
    return lax.dot_general(left, right, (contract, ((), ())), preferred_element_type=f32)


def swapped(block, axis, bit):
    return lax.ppermute(block, axis, [(i, i ^ bit) for i in range(lax.axis_size(axis))])


def bits_of(size):
    assert size & (size - 1) == 0
    return [1 << i for i in range(size.bit_length() - 1)]


def rim_route(target):
    heads, seqs = lax.axis_size("head"), lax.axis_size("seq")
    return [(s * heads + heads - 1, (s + 1) * heads + target) for s in range(seqs - 1)]


def pick_body(targets, *refs):
    *tail_refs, rim_ref = refs
    rim = jnp.zeros(tail_refs[0].shape, f32)
    above = jnp.zeros((rim_ref.shape[0] - rim.shape[0], rim.shape[1]), f32)
    for target, ref in zip(targets, tail_refs):
        rim = jnp.where(place("head") == target, ref[...].astype(f32), rim)
    rim_ref[...] = jnp.concatenate([above, rim], axis=0).astype(rim_ref.dtype)


def gathered(own, loaded):
    heads = lax.axis_size("head")
    bits = bits_of(heads)
    assert bits
    slabs = {0: own}
    for bit in reversed(bits[1:]):
        for k in sorted(slabs):
            slabs[k ^ bit] = swapped(slabs[k], "head", bit)
    tail = own[own.shape[0] - RIM // 2 :]
    targets = [first if first == heads - 2 else first + 1 for first in range(0, heads, 2)][::-1]
    tails = [lax.ppermute(tail, ("seq", "head"), rim_route(target)) for target in targets]
    slabs[1] = swapped(own, "head", 1)
    arrived = [k for k in sorted(slabs) if k > 1]
    moved, tails, loaded = lax.optimization_barrier(
        ([slabs[k] for k in arrived], tails, loaded)
    )
    for k, slab in zip(arrived, moved):
        slabs[k], slabs[k ^ 1] = slab, swapped(slab, "head", 1)
    rim = vmem_call(
        functools.partial(pick_body, targets), jax.ShapeDtypeStruct((RIM, own.shape[1]), bf16), tails
    )
    return [slabs[k] for k in range(1, heads)], [rim, swapped(rim, "head", 1)], loaded


def vmem_call(body, out_shape, args, scratch=(), hbm=0, grant=4, flops=0, moved=0):
    here = len(args) - hbm
    args = [pltpu.with_memory_space_constraint(a, pltpu.HBM) if i >= here else a for i, a in enumerate(args)]
    spaces = [pltpu.VMEM] * here + [pltpu.HBM] * hbm
    return pl.pallas_call(
        body,
        out_shape=out_shape,
        in_specs=[pl.BlockSpec(memory_space=space) for space in spaces],
        out_specs=jax.tree.map(lambda _: pl.BlockSpec(memory_space=pltpu.VMEM), out_shape),
        scratch_shapes=list(scratch),
        compiler_params=pltpu.CompilerParams(vmem_limit_bytes=grant * MIB),
        cost_estimate=pl.CostEstimate(flops=flops, bytes_accessed=moved, transcendentals=0),
    )(*args)


def place(axis, bit=None):
    here = lax.axis_index(axis)
    return here if bit is None else here // bit % 2


def column_pieces(width):
    step = math.gcd(width, 256)
    return [slice(i, i + step) for i in range(0, width, step)]


def load_body(*refs):
    (down_refs, whole_refs, weight_ref), refs = (refs[:2], refs[2:8], refs[8]), refs[9:]
    downs, whole, weights, sems = refs[0], refs[1:7], refs[7], refs[8]
    rank = down_refs[0].shape[1]
    pairs = [(ref, downs.at[:, pl.ds(i * rank, rank)]) for i, ref in enumerate(down_refs)]
    pairs += list(zip(whole_refs, whole))
    pairs += [(weight_ref.at[c], weights.at[c]) for c in range(2)]
    copies = [pltpu.make_async_copy(*pair, sems.at[i]) for i, pair in enumerate(pairs)]
    for copy in copies:
        copy.start()
    for copy in copies:
        copy.wait()


def load(downs, whole, weight):
    width, rank = downs[0].shape
    return vmem_call(
        load_body,
        (
            jax.ShapeDtypeStruct((width, 2 * rank), bf16),
            *[jax.ShapeDtypeStruct(part.shape, part.dtype) for part in whole],
            jax.ShapeDtypeStruct((2, *weight.shape[1:]), bf16),
        ),
        (*downs, *whole, weight),
        scratch=[pltpu.SemaphoreType.DMA((4 + len(whole),))],
        hbm=3 + len(whole),
        grant=8,
    )


def weave(main, *others):
    for _ in main:
        for other in others:
            next(other, None)


def drain(*steps):
    for each in steps:
        for _ in each:
            pass


def front_body(slab_count, *refs):
    (one_ref, two_ref, *slab_refs), refs = refs[: slab_count + 1], refs[slab_count + 1 :]
    (downs, own_rows_ref, betas, rates, decay_up_ref, bias_ref, conv_ref), refs = refs[:7], refs[7:]
    (weights, weight_ref), refs = refs[:2], refs[2:]
    (own_refs, other_refs), refs = (refs[:GROUPS], refs[GROUPS : 2 * GROUPS]), refs[2 * GROUPS :]
    (solved_ref, attend_ref, start_ref, gate_ref), refs = refs[:4], refs[4:]
    value_weight, rows_ref, projected, running_ref, parts_ref, *refs = refs
    mixing, inverse, sides, sems = refs
    heads, count, size = start_ref.shape
    slab_rows = count // slab_count
    tap_count = conv_ref.shape[1]
    rank = decay_up_ref.shape[0]
    chunk = math.gcd(count, 64)
    chunks = count // chunk
    block = math.gcd(count, 128)
    blocks = count // block
    half = heads // 2
    here = place("head")
    lanes_of = [slice(h * size, (h + 1) * size) for h in range(heads)]
    tiles = [slice(a * chunk, (a + 1) * chunk) for a in range(chunks)]
    pieces = column_pieces(heads * size)

    def rows_of(k):
        return pl.ds(pl.multiple_of(RIM + (here ^ k) * slab_rows, 16), slab_rows)

    streams = []
    for i, piece in enumerate(pieces):
        streams.append(
            pltpu.make_async_copy(weight_ref.at[2, :, piece], value_weight.at[:, piece], sems.at[i])
        )
    for copy in streams:
        copy.start()
    rows_ref[:RIM, :] = (one_ref[...].astype(f32) + two_ref[...].astype(f32)).astype(bf16)
    for k, ref in enumerate([own_rows_ref, *slab_refs]):
        rows_ref[rows_of(k), :] = ref[...]

    def project(c, piece):
        weight = value_weight[:, piece] if c == 2 else weights[c, :, piece]
        result = dot(rows_ref[...], weight)
        for begin in range(piece.start, piece.stop, size):
            at = begin - piece.start
            projected[c * heads + begin // size] = result[:, at : at + size]

    def projections(chosen):
        for c, piece in chosen:
            project(c, piece)
            yield

    def decays():
        for h, lanes in enumerate(lanes_of):
            rate = jnp.exp(jnp.broadcast_to(rates[:, h : h + 1], (1, size)))
            for rows in tiles:
                raw = running_ref[rows, lanes] + bias_ref[:, lanes]
                softplus = jnp.maximum(raw, 0.0) + jnp.log(1.0 + jnp.exp(-jnp.abs(raw)))
                log_decay = -rate * softplus
                high = log_decay.astype(bf16)
                parts_ref[rows, lanes] = high
                rest = (log_decay - high.astype(f32)).astype(bf16)
                parts_ref[count + rows.start : count + rows.stop, lanes] = rest
            yield

    low = dot(rows_ref[RIM:, :], downs[...]).astype(bf16)
    running_ref[...] = dot(low[:, :rank], decay_up_ref[...])
    gate_ref[...] = low[:, rank:]
    strength = jax.nn.sigmoid(dot(rows_ref[RIM:, :], betas[...], ((1,), (1,))))
    first = [(c, pieces[0]) for c in range(2)]
    weave(decays(), projections(first))
    row = lax.broadcasted_iota(jnp.int32, (count, count), 0)
    col = lax.broadcasted_iota(jnp.int32, (count, count), 1)
    lower = jnp.where(row >= col, 1.0, 0.0).astype(bf16)
    running_ref[...] = dot(jnp.concatenate([lower, lower], axis=1), parts_ref[...])
    for copy in streams:
        copy.wait()

    def convolved(c, rows, h):
        taps = conv_ref[c].astype(f32)[:, lanes_of[h]]
        total = None
        for i in range(tap_count):
            begin = RIM - tap_count + 1 + i + rows.start
            term = projected[c * heads + h, pl.ds(begin, chunk), :] * taps[i : i + 1]
            total = term if total is None else total + term
        part = 0.5 * total
        return part + part * jnp.tanh(part)

    middles, key_falls, stops, lefts = ([[] for _ in range(heads)] for _ in range(4))

    def tiles_of(h):
        lanes = lanes_of[h]
        last = running_ref[count - 1 : count, lanes]
        for rows in tiles:
            running = running_ref[rows, lanes]
            middle = running[chunk // 2 : chunk // 2 + 1]
            above = running - middle
            rise, entry = jnp.exp(above), jnp.exp(middle)
            queries = convolved(0, rows, h)
            power = jnp.sum(queries * queries, -1, keepdims=True)
            queries = queries * (lax.rsqrt(power + 1e-06) * size ** (-0.5)) * rise
            start_ref[h, rows, :] = (queries * entry).astype(bf16)
            keys = convolved(1, rows, h)
            power = jnp.sum(keys * keys, -1, keepdims=True)
            keys = keys * lax.rsqrt(power + 1e-06)
            key_fall = keys * strength[rows, h : h + 1] * jnp.exp(-above)
            keys = keys * rise
            sides[h, rows, :size] = (keys * entry).astype(bf16)
            stops[h].append((key_fall * jnp.exp(last - middle)).astype(bf16))
            middles[h].append(middle)
            key_falls[h].append(key_fall)
            lefts[h].append(jnp.concatenate([keys.astype(bf16), queries.astype(bf16)], axis=0))
            yield

    def scores_of(h):
        for a, rows in enumerate(tiles):
            reach = (a * chunk // block + 1) * block
            falls = []
            for b in range(reach // chunk):
                if b < a:
                    falls.append(key_falls[h][b] * jnp.exp(middles[h][a] - middles[h][b]))
                elif b == a:
                    falls.append(key_falls[h][b])
                else:
                    falls.append(jnp.zeros((chunk, size), f32))
            right = jnp.concatenate(falls, axis=0).astype(bf16)
            scores = dot(lefts[h][a], right, ((1,), (1,)))
            inside = slice(reach - block, reach)
            if reach > block:
                before = slice(0, reach - block)
                mixing[h, rows, before] = scores[:chunk, before].astype(bf16)
                attend_ref[h, rows, before] = scores[chunk:, before].astype(bf16)
            at, to = row[rows, inside], col[rows, inside]
            mixing[h, rows, inside] = jnp.where(at > to, scores[:chunk, inside], 0.0).astype(bf16)
            attend_ref[h, rows, inside] = jnp.where(
                at >= to, scores[chunk:, inside], 0.0
            ).astype(bf16)
            yield

    at, to = row[:block, :block], col[:block, :block]
    eye = jnp.where(at == to, 1.0, 0.0).astype(bf16)
    base = math.gcd(block, BASE)
    near = jnp.where(at // base == to // base, -1.0, 0.0).astype(bf16)

    def inverse_of(chosen):
        corners = [(h, slice(d * block, (d + 1) * block)) for h in chosen for d in range(blocks)]
        powers = [mixing[h, d, d] * near for h, d in corners]
        totals = [power + eye for power in powers]
        steps = (base - 1).bit_length() - 1
        if steps:
            powers = [dot(power, power).astype(bf16) for power in powers]
        yield
        for step in range(steps):
            for n in range(len(corners)):
                power, total = powers[n], totals[n]
                if step < steps - 1:
                    both = dot(jnp.concatenate([power, total], axis=0), power)
                    powers[n], more = both[:block].astype(bf16), both[block:]
                else:
                    more = dot(total, power)
                totals[n] = (total.astype(f32) + more).astype(bf16)
            yield
        for (h, d), total in zip(corners, totals):
            inverse[h, d, :] = total
        width = base
        while width < block:
            odd = range(width, block, 2 * width)
            pair_mask = (at // width % 2 == 1) & (to // width == at // width - 1)
            pair_mask = jnp.where(pair_mask, 1.0, 0.0).astype(bf16)
            halves = []
            for h, d in corners:
                parts = [inverse[h, d.start + i : d.start + i + width, :] for i in odd]
                picked = jnp.concatenate(parts, axis=0)
                halves.append((picked, dot(picked, mixing[h, d, d] * pair_mask).astype(bf16)))
            yield
            for (h, d), (picked, part) in zip(corners, halves):
                new = (picked.astype(f32) - dot(part, inverse[h, d, :])).astype(bf16)
                for n, i in enumerate(odd):
                    inverse[h, d.start + i : d.start + i + width, :] = new[
                        n * width : (n + 1) * width
                    ]
            yield
            width *= 2

    def values():
        for piece in pieces:
            project(2, piece)
            yield
            for h in range(piece.start // size, piece.stop // size):
                for rows in tiles:
                    sides[h, rows, size:] = convolved(2, rows, h).astype(bf16)
                yield

    pairs = [None] * heads
    unit = row[:size, :size] == col[:size, :size]

    def solve(chosen):
        for d in range(blocks):
            rows = slice(d * block, (d + 1) * block)
            for h in chosen:
                side = sides[h, rows, :]
                if d:
                    done = solved_ref[h, : d * block, :]
                    side = side.astype(f32) - dot(mixing[h, rows, : d * block], done)
                    side = side.astype(bf16)
                solved_ref[h, rows, :] = dot(inverse[h, rows, :], side).astype(bf16)
            yield
        for h in chosen:
            moved = dot(jnp.concatenate(stops[h], axis=0), solved_ref[h], ((0,), (0,)))
            fade = jnp.exp(running_ref[count - 1 : count, lanes_of[h]])
            diagonal = jnp.where(unit, jnp.broadcast_to(fade, (size, size)), 0.0)
            pairs[h] = jnp.concatenate([diagonal - moved[:, :size], moved[:, size:]], axis=1)
        yield

    ready, last = range(half), range(half, heads)
    early, late, value_steps, solving = inverse_of(ready), inverse_of(last), values(), solve(ready)
    weave(tiles_of(0), projections([(c, piece) for piece in pieces[1:] for c in range(2)]))
    for h in range(1, heads):
        scores = scores_of(h - 1)
        weave(tiles_of(h), scores, *([early] if h > half else []))
        drain(scores)
    weave(scores_of(heads - 1), early, value_steps)
    weave(early, value_steps)
    drain(early)
    weave(late, itertools.chain(value_steps, solving))
    drain(value_steps, solving, solve(last))
    upper = place("seq", 1) == 1
    for h in range(half):
        low, high = pairs[h], pairs[half + h]
        group, at = divmod(h, own_refs[0].shape[0])
        own_refs[group][at] = jnp.where(upper, high, low).astype(bf16)
        other_refs[group][at] = jnp.where(upper, low, high).astype(bf16)


def front(rims, slabs, loaded, weight, size):
    slab_count, slab_rows = 1 + len(slabs), slabs[0].shape[0]
    count = slab_count * slab_rows
    _, width, channels = weight.shape
    heads, block = channels // size, math.gcd(count, 128)
    return vmem_call(
        functools.partial(front_body, slab_count),
        (
            *[jax.ShapeDtypeStruct((heads // 2 // GROUPS, size, 2 * size), bf16)] * (2 * GROUPS),
            jax.ShapeDtypeStruct((heads, count, 2 * size), bf16),
            jax.ShapeDtypeStruct((heads, count, count), bf16),
            jax.ShapeDtypeStruct((heads, count, size), bf16),
            jax.ShapeDtypeStruct((count, loaded[0].shape[1] // 2), bf16),
        ),
        (*rims, *slabs, *loaded, weight),
        scratch=[
            pltpu.VMEM((width, channels), bf16),
            pltpu.VMEM((RIM + count, width), bf16),
            pltpu.VMEM((3 * heads, RIM + count, size), f32),
            pltpu.VMEM((count, channels), f32),
            pltpu.VMEM((2 * count, channels), bf16),
            pltpu.VMEM((heads, count, count), bf16),
            pltpu.VMEM((heads, count, block), bf16),
            pltpu.VMEM((heads, count, 2 * size), bf16),
            pltpu.SemaphoreType.DMA((len(column_pieces(channels)),)),
        ],
        hbm=1,
        grant=24,
        flops=2 * count * width * channels * 4,
        moved=2 * 4 * width * channels,
    )


def rows_body(attend_ref, solved_ref, start_ref, low_ref, up_ref, raised_ref, output_ref, gate_ref):
    heads, _, size = start_ref.shape
    gate_ref[...] = jax.nn.sigmoid(dot(low_ref[...], up_ref[...]))
    count = attend_ref.shape[1]
    block = math.gcd(count, 128)
    for h in range(heads):
        for begin in range(0, count, block):
            rows, reach = slice(begin, begin + block), slice(0, begin + block)
            both = dot(attend_ref[h, rows, reach], solved_ref[h, reach, :])
            raised_ref[h, rows, :] = (start_ref[h, rows, :].astype(f32) - both[:, :size]).astype(bf16)
            output_ref[rows, h * size : (h + 1) * size] = both[:, size:]


def composed(later, first, size):
    both = dot(later[:, :size], first)
    return both[:, :size], both[:, size:] + later[:, size:].astype(f32)


def put(ref, h, pair):
    size = ref.shape[1]
    if ref.shape[2] > size:
        ref[h, :, :size] = pair[0].astype(bf16)
    ref[h, :, ref.shape[2] - size :] = pair[1].astype(bf16)


def join_body(bit, own_ref, far_ref, total_ref):
    heads, size, _ = own_ref.shape
    for h in range(heads):
        own, far = own_ref[h], far_ref[h]
        upper = place("seq", bit) == 1
        later, first = jnp.where(upper, own, far), jnp.where(upper, far, own)
        put(total_ref, h, composed(later, first, size))


def join(bit, own, far, last):
    heads, size, width = own.shape
    return vmem_call(
        functools.partial(join_body, bit),
        jax.ShapeDtypeStruct((heads, size, size if last else width), bf16),
        (own, far),
        flops=2 * heads * size * size * width,
        moved=6 * heads * size * width,
    )


def before_body(bit, far_ref, *refs):
    *near_refs, out_ref = refs
    heads, size, width = far_ref.shape
    row = lax.broadcasted_iota(jnp.int32, (size, width), 0)
    col = lax.broadcasted_iota(jnp.int32, (size, width), 1)
    for h in range(heads):
        if near_refs:
            near = near_refs[0][h]
            pair = jnp.concatenate(composed(near, far_ref[h], size), axis=1)
            near = near.astype(f32)
        else:
            near, pair = jnp.where(row == col, 1.0, 0.0), far_ref[h].astype(f32)
        out_ref[h] = jnp.where(place("seq", bit) == 1, pair, near).astype(bf16)


def before(bit, near, far):
    return vmem_call(
        functools.partial(before_body, bit),
        jax.ShapeDtypeStruct(far.shape, bf16),
        (far, *near),
        flops=2 * math.prod(far.shape) * far.shape[1],
        moved=6 * math.prod(far.shape),
    )


def entry_body(bit, near_ref, far_ref, own_ref, partner_ref, keep_ref, send_ref):
    heads, size, _ = near_ref.shape
    arrived, upper = place("seq", bit) == 1, place("seq", 1) == 1
    for h in range(heads):
        state = dot(near_ref[h, :, :size], far_ref[h])
        state = jnp.where(arrived, state, 0.0) + near_ref[h, :, size:].astype(f32)
        first = jnp.where(upper, partner_ref[h], own_ref[h])
        state = state.astype(bf16)
        later = dot(first[:, :size], state) + first[:, size:].astype(f32)
        later = later.astype(bf16)
        keep_ref[h] = jnp.where(upper, later, state)
        send_ref[h] = jnp.where(upper, state, later)


def entry_states(own, other):
    heads, size, width = own.shape
    bits = bits_of(lax.axis_size("seq"))
    partner = swapped(other, "seq", 1)
    total = join(1, own, partner, len(bits) == 2)
    near = ()
    assert len(bits) > 2
    for bit in bits[1:-1]:
        far = swapped(total, "seq", bit)
        total = join(bit, total, far, 2 * bit == bits[-1])
        near = (before(bit, near, far),)
    far = swapped(total, "seq", bits[-1])
    state = jax.ShapeDtypeStruct((heads, size, size), bf16)
    keep, send = vmem_call(
        functools.partial(entry_body, bits[-1]),
        (state, state),
        (*near, far, own, partner),
        flops=4 * heads * size * size * size,
        moved=14 * heads * size * size,
    )
    return keep, swapped(send, "seq", 1)


def back_body(places, *refs):
    own_refs, other_refs, refs = refs[:GROUPS], refs[GROUPS : 2 * GROUPS], refs[2 * GROUPS :]
    raised_ref, output_ref, gate_ref, gain_ref, weight_ref, keep_ref, *rest = refs
    normed = rest[-1]
    size = gain_ref.shape[1]
    slab_rows = keep_ref.shape[0]
    share = own_refs[0].shape[0]
    half = GROUPS * share
    upper = place("seq", 1) == 1
    for k, away in enumerate(places):
        rows = pl.ds(pl.multiple_of((place("head") ^ away) * slab_rows, 16), slab_rows)
        for h in range(raised_ref.shape[0]):
            lanes = slice(h * size, (h + 1) * size)
            group, at = divmod(h % half, share)
            own, other = own_refs[group][at], other_refs[group][at]
            state = jnp.where(upper, other, own) if h < half else jnp.where(upper, own, other)
            attended = dot(raised_ref[h, rows, :], state) + output_ref[rows, lanes]
            power = jnp.sum(attended * attended, -1, keepdims=True) * (1.0 / size)
            normed[k * slab_rows : (k + 1) * slab_rows, lanes] = (
                attended * lax.rsqrt(power + 1e-05) * gain_ref[...] * gate_ref[rows, lanes]
            ).astype(bf16)
    total = dot(normed[...], weight_ref[...])
    keep_ref[...] = total[:slab_rows]
    if len(rest) > 1:
        rest[0][...] = total[slab_rows:].astype(bf16)


def back(places, states, raised, output_rows, out_gate, gain, weight, slab_rows):
    slab_count, width = len(places), weight.shape[1]
    shapes = [jax.ShapeDtypeStruct((slab_rows, width), f32)]
    if slab_count > 1:
        shapes.append(jax.ShapeDtypeStruct((slab_rows, width), bf16))
    return vmem_call(
        functools.partial(back_body, places),
        shapes,
        (*states, raised, output_rows, out_gate, gain, weight),
        scratch=[pltpu.VMEM((slab_count * slab_rows, weight.shape[0]), bf16)],
        grant=10,
        flops=2 * slab_count * slab_rows * weight.shape[0] * width,
        moved=2 * weight.shape[0] * width,
    )


def shards(
    hidden_in,
    qkv_weight,
    conv_weight,
    decay_log,
    dt_bias,
    decay_down,
    decay_up,
    beta_weight,
    gate_down,
    gate_up,
    norm_gain,
    out_weight,
):
    heads, size = decay_log.shape[0], norm_gain.shape[0]
    channels = heads * size
    devices = lax.axis_size("head")
    weight = qkv_weight.transpose(1, 0, 2)
    loaded = load(
        (decay_down, gate_down),
        (hidden_in, beta_weight.T, decay_log[None], decay_up, dt_bias[None], conv_weight),
        weight,
    )
    slabs, rims, loaded = gathered(hidden_in, loaded)
    *pairs, solved, attend, start, gate_low = front(rims, slabs, loaded, weight, size)
    count = start.shape[1]
    raised, output_rows, out_gate = vmem_call(
        rows_body,
        (
            jax.ShapeDtypeStruct((heads, count, size), bf16),
            jax.ShapeDtypeStruct((count, channels), f32),
            jax.ShapeDtypeStruct((count, channels), f32),
        ),
        (attend, solved, start, gate_low, gate_up),
        grant=8,
        flops=2 * heads * count * count * 2 * size,
        moved=4 * heads * count * count,
    )
    states = [entry_states(*both) for both in zip(pairs[:GROUPS], pairs[GROUPS:])]
    states = [own for own, _ in states] + [other for _, other in states]
    slab_rows = count // devices
    sums = {}
    for g in reversed(range(max(devices // 2, 1))):
        places = [2 * g, 2 * g + 1][:devices]
        keep, *send = back(
            places, states, raised, output_rows, out_gate, norm_gain[None], out_weight, slab_rows
        )
        near = [swapped(part, "head", 1).astype(f32) for part in send]
        sums[g] = [lax.optimization_barrier(sum([keep] + near))]
    for bit in bits_of(devices)[1:]:
        for g in sorted(sums):
            if 2 * g & bit:
                arrived = swapped(sum(sums.pop(g)).astype(bf16), "head", bit)
                sums[g ^ bit // 2].append(arrived.astype(f32))
    return sum(sums[0]).astype(bf16)


def solution(mesh):
    return jax.shard_map(
        shards,
        mesh=mesh,
        in_specs=(
            P(("seq", "head"), None),
            P(None, None, "head"),
            P(None, None, "head"),
            P("head"),
            P("head"),
            P(),
            P(None, "head"),
            P(None, "head"),
            P(),
            P(None, "head"),
            P(),
            P("head", None),
        ),
        out_specs=P(("seq", "head"), None),
        check_vma=False,
    )
```

```python
import functools
import math

import jax
import jax.numpy as jnp
from jax import lax
from jax.experimental import pallas as pl
from jax.experimental.pallas import tpu as pltpu
from jax.sharding import PartitionSpec as P

RIM = 16
BASE = 16
GROUPS = 2
MIB = 1024 * 1024
f32 = jnp.float32
bf16 = jnp.bfloat16


def dot(left, right, contract=((1,), (0,))):
    return lax.dot_general(left, right, (contract, ((), ())), preferred_element_type=f32)


def swapped(block, axis, bit):
    return lax.ppermute(block, axis, [(i, i ^ bit) for i in range(lax.axis_size(axis))])


def bits_of(size):
    assert size & (size - 1) == 0
    return [1 << i for i in range(size.bit_length() - 1)]


def rim_route(target):
    heads, seqs = lax.axis_size("head"), lax.axis_size("seq")
    return [(s * heads + heads - 1, (s + 1) * heads + target) for s in range(seqs - 1)]


def pick_body(targets, *refs):
    *tail_refs, rim_ref = refs
    rim = jnp.zeros(tail_refs[0].shape, f32)
    above = jnp.zeros((rim_ref.shape[0] - rim.shape[0], rim.shape[1]), f32)
    for target, ref in zip(targets, tail_refs):
        rim = jnp.where(place("head") == target, ref[...].astype(f32), rim)
    rim_ref[...] = jnp.concatenate([above, rim], axis=0).astype(rim_ref.dtype)


def gathered(own, loaded):
    heads = lax.axis_size("head")
    bits = bits_of(heads)
    assert bits
    slabs = {0: own}
    for bit in reversed(bits[1:]):
        for k in sorted(slabs):
            slabs[k ^ bit] = swapped(slabs[k], "head", bit)
    tail = own[own.shape[0] - RIM // 2 :]
    targets = [first if first == heads - 2 else first + 1 for first in range(0, heads, 2)][::-1]
    tails = [lax.ppermute(tail, ("seq", "head"), rim_route(target)) for target in targets]
    slabs[1] = swapped(own, "head", 1)
    arrived = [k for k in sorted(slabs) if k > 1]
    moved, tails, loaded = lax.optimization_barrier(
        ([slabs[k] for k in arrived], tails, loaded)
    )
    for k, slab in zip(arrived, moved):
        slabs[k], slabs[k ^ 1] = slab, swapped(slab, "head", 1)
    rim = vmem_call(
        functools.partial(pick_body, targets), jax.ShapeDtypeStruct((RIM, own.shape[1]), bf16), tails
    )
    return [slabs[k] for k in range(1, heads)], [rim, swapped(rim, "head", 1)], loaded


def vmem_call(body, out_shape, args, scratch=(), hbm=0, grant=4, flops=0, moved=0):
    here = len(args) - hbm
    args = [pltpu.with_memory_space_constraint(a, pltpu.HBM) if i >= here else a for i, a in enumerate(args)]
    spaces = [pltpu.VMEM] * here + [pltpu.HBM] * hbm
    return pl.pallas_call(
        body,
        out_shape=out_shape,
        in_specs=[pl.BlockSpec(memory_space=space) for space in spaces],
        out_specs=jax.tree.map(lambda _: pl.BlockSpec(memory_space=pltpu.VMEM), out_shape),
        scratch_shapes=list(scratch),
        compiler_params=pltpu.CompilerParams(vmem_limit_bytes=grant * MIB),
        cost_estimate=pl.CostEstimate(flops=flops, bytes_accessed=moved, transcendentals=0),
    )(*args)


def place(axis, bit=None):
    here = lax.axis_index(axis)
    return here if bit is None else here // bit % 2


def column_pieces(width):
    step = math.gcd(width, 256)
    return [slice(i, i + step) for i in range(0, width, step)]


def load_body(
    hidden_ref, decay_down_ref, gate_down_ref, beta_ref, weight_ref,
    own_ref, weights, downs, betas, sems,
):
    rank = decay_down_ref.shape[1]
    copies = [
        pltpu.make_async_copy(hidden_ref, own_ref, sems.at[0]),
        pltpu.make_async_copy(decay_down_ref, downs.at[:, pl.ds(0, rank)], sems.at[1]),
        pltpu.make_async_copy(gate_down_ref, downs.at[:, pl.ds(rank, rank)], sems.at[2]),
        pltpu.make_async_copy(beta_ref, betas, sems.at[3]),
    ]
    for c in range(2):
        copies.append(pltpu.make_async_copy(weight_ref.at[c], weights.at[c], sems.at[4 + c]))
    for copy in copies:
        copy.start()
    for copy in copies:
        copy.wait()


def load(own, decay_down, gate_down, beta, weight):
    width, rank = decay_down.shape
    return vmem_call(
        load_body,
        (
            jax.ShapeDtypeStruct(own.shape, bf16),
            jax.ShapeDtypeStruct((2, *weight.shape[1:]), bf16),
            jax.ShapeDtypeStruct((width, 2 * rank), bf16),
            jax.ShapeDtypeStruct(beta.shape, bf16),
        ),
        (own, decay_down, gate_down, beta, weight),
        scratch=[pltpu.SemaphoreType.DMA((6,))],
        hbm=5,
        grant=8,
    )


def front_body(slab_count, *refs):
    (one_ref, two_ref, *slab_refs), refs = refs[: slab_count + 1], refs[slab_count + 1 :]
    (own_rows_ref, weights, downs, betas), refs = refs[:4], refs[4:]
    hbm_refs, refs = refs[:5], refs[5:]
    (own_refs, other_refs), refs = (refs[:GROUPS], refs[GROUPS : 2 * GROUPS]), refs[2 * GROUPS :]
    (solved_ref, attend_ref, start_ref, gate_ref), refs = refs[:4], refs[4:]
    loaded, refs = refs[:5], refs[5:]
    rows_ref, projected, running_ref, parts_ref, mixing, inverse, sides, sems = refs
    rates, decay_up_ref, bias_ref, conv_ref, value_weight = loaded
    weight_ref = hbm_refs[-1]
    heads, count, size = start_ref.shape
    slab_rows = count // slab_count
    tap_count = conv_ref.shape[1]
    rank = decay_up_ref.shape[0]
    chunk = math.gcd(count, 64)
    chunks = count // chunk
    block = math.gcd(count, 128)
    blocks = count // block
    here = place("head")

    def rows_of(k):
        return pl.ds(pl.multiple_of(RIM + (here ^ k) * slab_rows, 16), slab_rows)

    small = [pltpu.make_async_copy(hbm_refs[i], loaded[i], sems.at[i]) for i in range(4)]
    pieces = column_pieces(heads * size)
    streams = []
    for i, piece in enumerate(pieces):
        streams.append(
            pltpu.make_async_copy(
                weight_ref.at[2, :, piece], value_weight.at[:, piece], sems.at[4 + i]
            )
        )
    for copy in small + streams:
        copy.start()
    rows_ref[:RIM, :] = (one_ref[...].astype(f32) + two_ref[...].astype(f32)).astype(bf16)
    for k, ref in enumerate([own_rows_ref, *slab_refs]):
        rows_ref[rows_of(k), :] = ref[...]

    def project(c, piece, weight):
        result = dot(rows_ref[...], weight)
        for begin in range(piece.start, piece.stop, size):
            at = begin - piece.start
            projected[c * heads + begin // size] = result[:, at : at + size]

    pending = [(c, piece) for piece in pieces for c in range(2)]
    share = (pieces[0].stop - pieces[0].start) // size

    def project_next(number):
        for c, piece in pending[:number]:
            project(c, piece, weights[c, :, piece])
        del pending[:number]

    project_next(2)
    low = dot(rows_ref[RIM:, :], downs[...]).astype(bf16)
    gate_ref[...] = low[:, rank:]
    strength = jax.nn.sigmoid(dot(rows_ref[RIM:, :], betas[...], ((1,), (1,))))
    for copy in small:
        copy.wait()
    running_ref[...] = dot(low[:, :rank], decay_up_ref[...])
    tiles = [slice(a * chunk, (a + 1) * chunk) for a in range(chunks)]
    for h in range(heads):
        lanes = slice(h * size, (h + 1) * size)
        rate = jnp.exp(jnp.full((1, size), rates[h], f32))
        for rows in tiles:
            raw = running_ref[rows, lanes] + bias_ref[:, lanes]
            softplus = jnp.maximum(raw, 0.0) + jnp.log(1.0 + jnp.exp(-jnp.abs(raw)))
            log_decay = -rate * softplus
            high = log_decay.astype(bf16)
            parts_ref[rows, lanes] = high
            rest = (log_decay - high.astype(f32)).astype(bf16)
            parts_ref[count + rows.start : count + rows.stop, lanes] = rest
    row = lax.broadcasted_iota(jnp.int32, (count, count), 0)
    col = lax.broadcasted_iota(jnp.int32, (count, count), 1)
    lower = jnp.where(row >= col, 1.0, 0.0).astype(bf16)
    running_ref[...] = dot(jnp.concatenate([lower, lower], axis=1), parts_ref[...])

    def convolved(c, rows, h):
        taps = conv_ref[c].astype(f32)[:, h * size : (h + 1) * size]
        total = None
        for i in range(tap_count):
            first = RIM - tap_count + 1 + i + rows.start
            term = projected[c * heads + h, pl.ds(first, chunk), :] * taps[i : i + 1]
            total = term if total is None else total + term
        half = 0.5 * total
        return half + half * jnp.tanh(half)

    for copy in streams:
        copy.wait()
    stops = []
    for h in range(heads):
        lanes = slice(h * size, (h + 1) * size)
        last = running_ref[count - 1 : count, lanes]
        middles, key_falls, stop, lefts = [], [], [], []
        for rows in tiles:
            running = running_ref[rows, lanes]
            middle = running[chunk // 2 : chunk // 2 + 1]
            above = running - middle
            rise, entry = jnp.exp(above), jnp.exp(middle)
            queries = convolved(0, rows, h)
            power = jnp.sum(queries * queries, -1, keepdims=True)
            queries = queries * (lax.rsqrt(power + 1e-06) * size ** (-0.5)) * rise
            start_ref[h, rows, :] = (queries * entry).astype(bf16)
            keys = convolved(1, rows, h)
            power = jnp.sum(keys * keys, -1, keepdims=True)
            keys = keys * lax.rsqrt(power + 1e-06)
            key_fall = keys * strength[rows, h : h + 1] * jnp.exp(-above)
            keys = keys * rise
            sides[h, rows, :size] = (keys * entry).astype(bf16)
            stop.append((key_fall * jnp.exp(last - middle)).astype(bf16))
            middles.append(middle)
            key_falls.append(key_fall)
            lefts.append(jnp.concatenate([keys.astype(bf16), queries.astype(bf16)], axis=0))
        stops.append((jnp.concatenate(stop, axis=0), jnp.exp(last)))
        project_next(pl.cdiv(2, share))
        for a in range(chunks):
            rows = tiles[a]
            reach = (a * chunk // block + 1) * block
            falls = []
            for b in range(reach // chunk):
                if b < a:
                    falls.append(key_falls[b] * jnp.exp(middles[a] - middles[b]))
                elif b == a:
                    falls.append(key_falls[b])
                else:
                    falls.append(jnp.zeros((chunk, size), f32))
            right = jnp.concatenate(falls, axis=0).astype(bf16)
            scores = dot(lefts[a], right, ((1,), (1,)))
            inside = slice(reach - block, reach)
            if reach > block:
                before = slice(0, reach - block)
                mixing[h, rows, before] = scores[:chunk, before].astype(bf16)
                attend_ref[h, rows, before] = scores[chunk:, before].astype(bf16)
            at, to = row[rows, inside], col[rows, inside]
            mixing[h, rows, inside] = jnp.where(at > to, scores[:chunk, inside], 0.0).astype(bf16)
            attend_ref[h, rows, inside] = jnp.where(
                at >= to, scores[chunk:, inside], 0.0
            ).astype(bf16)

    def value_side(h):
        for rows in tiles:
            sides[h, rows, size:] = convolved(2, rows, h).astype(bf16)

    between = [functools.partial(project, 2, p, value_weight[:, p]) for p in pieces]
    between += [functools.partial(value_side, h) for h in range(heads)]

    at, to = row[:block, :block], col[:block, :block]
    eye = jnp.where(at == to, 1.0, 0.0).astype(bf16)
    base = math.gcd(block, BASE)
    near = jnp.where(at // base == to // base, -1.0, 0.0).astype(bf16)
    corners = [(h, slice(d * block, (d + 1) * block)) for h in range(heads) for d in range(blocks)]
    powers = [mixing[h, d, d] * near for h, d in corners]
    totals = [power + eye for power in powers]
    steps = (base - 1).bit_length() - 1
    if steps:
        powers = [dot(power, power).astype(bf16) for power in powers]
    for step in range(steps):
        for n in range(len(corners)):
            power, total = powers[n], totals[n]
            if step < steps - 1:
                both = dot(jnp.concatenate([power, total], axis=0), power)
                powers[n], more = both[:block].astype(bf16), both[block:]
            else:
                more = dot(total, power)
            totals[n] = (total.astype(f32) + more).astype(bf16)
        if between:
            between.pop(0)()
    for (h, d), total in zip(corners, totals):
        inverse[h, d, :] = total
    width = base
    while width < block:
        odd = range(width, block, 2 * width)
        pair_mask = (at // width % 2 == 1) & (to // width == at // width - 1)
        pair_mask = jnp.where(pair_mask, 1.0, 0.0).astype(bf16)
        halves = []
        for h, d in corners:
            parts = [inverse[h, d.start + i : d.start + i + width, :] for i in odd]
            chosen = jnp.concatenate(parts, axis=0)
            halves.append((chosen, dot(chosen, mixing[h, d, d] * pair_mask).astype(bf16)))
        for (h, d), (chosen, half) in zip(corners, halves):
            new = (chosen.astype(f32) - dot(half, inverse[h, d, :])).astype(bf16)
            for n, i in enumerate(odd):
                inverse[h, d.start + i : d.start + i + width, :] = new[n * width : (n + 1) * width]
        if between:
            between.pop(0)()
        width *= 2
    for work in between:
        work()

    for d in range(blocks):
        rows = slice(d * block, (d + 1) * block)
        for h in range(heads):
            side = sides[h, rows, :]
            if d:
                done = solved_ref[h, : d * block, :]
                side = (side.astype(f32) - dot(mixing[h, rows, : d * block], done)).astype(bf16)
            solved_ref[h, rows, :] = dot(inverse[h, rows, :], side).astype(bf16)
    pairs = []
    unit = row[:size, :size] == col[:size, :size]
    for h in range(heads):
        stop, fade = stops[h]
        moved = dot(stop, solved_ref[h], ((0,), (0,)))
        diagonal = jnp.where(unit, jnp.broadcast_to(fade, (size, size)), 0.0)
        pairs.append(jnp.concatenate([diagonal - moved[:, :size], moved[:, size:]], axis=1))
    upper = place("seq", 1) == 1
    for h in range(heads // 2):
        low, high = pairs[h], pairs[heads // 2 + h]
        group, at = divmod(h, own_refs[0].shape[0])
        own_refs[group][at] = jnp.where(upper, high, low).astype(bf16)
        other_refs[group][at] = jnp.where(upper, low, high).astype(bf16)


def front(rims, slabs, fetched, loaded, weight, size):
    slab_count, slab_rows = 1 + len(slabs), slabs[0].shape[0]
    count = slab_count * slab_rows
    _, width, channels = weight.shape
    heads, block = channels // size, math.gcd(count, 128)
    buffers = [pltpu.SMEM(loaded[0].shape, f32)]
    buffers += [pltpu.VMEM(part.shape, part.dtype) for part in loaded[1:]]
    return vmem_call(
        functools.partial(front_body, slab_count),
        (
            *[jax.ShapeDtypeStruct((heads // 2 // GROUPS, size, 2 * size), bf16)] * (2 * GROUPS),
            jax.ShapeDtypeStruct((heads, count, 2 * size), bf16),
            jax.ShapeDtypeStruct((heads, count, count), bf16),
            jax.ShapeDtypeStruct((heads, count, size), bf16),
            jax.ShapeDtypeStruct((count, fetched[2].shape[1] // 2), bf16),
        ),
        (*rims, *slabs, *fetched, *loaded, weight),
        scratch=[
            *buffers,
            pltpu.VMEM((width, channels), bf16),
            pltpu.VMEM((RIM + count, width), bf16),
            pltpu.VMEM((3 * heads, RIM + count, size), f32),
            pltpu.VMEM((count, channels), f32),
            pltpu.VMEM((2 * count, channels), bf16),
            pltpu.VMEM((heads, count, count), bf16),
            pltpu.VMEM((heads, count, block), bf16),
            pltpu.VMEM((heads, count, 2 * size), bf16),
            pltpu.SemaphoreType.DMA((4 + len(column_pieces(channels)),)),
        ],
        hbm=1 + len(loaded),
        grant=24,
        flops=2 * count * width * channels * 4,
        moved=2 * 4 * width * channels,
    )


def rows_body(attend_ref, solved_ref, start_ref, low_ref, up_ref, raised_ref, output_ref, gate_ref):
    heads, _, size = start_ref.shape
    gate_ref[...] = jax.nn.sigmoid(dot(low_ref[...], up_ref[...]))
    count = attend_ref.shape[1]
    block = math.gcd(count, 128)
    for h in range(heads):
        for begin in range(0, count, block):
            rows, reach = slice(begin, begin + block), slice(0, begin + block)
            both = dot(attend_ref[h, rows, reach], solved_ref[h, reach, :])
            raised_ref[h, rows, :] = (start_ref[h, rows, :].astype(f32) - both[:, :size]).astype(bf16)
            output_ref[rows, h * size : (h + 1) * size] = both[:, size:]


def composed(later, first, size):
    both = dot(later[:, :size], first)
    return both[:, :size], both[:, size:] + later[:, size:].astype(f32)


def put(ref, h, pair):
    size = ref.shape[1]
    if ref.shape[2] > size:
        ref[h, :, :size] = pair[0].astype(bf16)
    ref[h, :, ref.shape[2] - size :] = pair[1].astype(bf16)


def join_body(bit, own_ref, far_ref, total_ref):
    heads, size, _ = own_ref.shape
    for h in range(heads):
        own, far = own_ref[h], far_ref[h]
        upper = place("seq", bit) == 1
        later, first = jnp.where(upper, own, far), jnp.where(upper, far, own)
        put(total_ref, h, composed(later, first, size))


def join(bit, own, far, last):
    heads, size, width = own.shape
    return vmem_call(
        functools.partial(join_body, bit),
        jax.ShapeDtypeStruct((heads, size, size if last else width), bf16),
        (own, far),
        flops=2 * heads * size * size * width,
        moved=6 * heads * size * width,
    )


def before_body(bit, far_ref, *refs):
    *near_refs, out_ref = refs
    heads, size, width = far_ref.shape
    row = lax.broadcasted_iota(jnp.int32, (size, width), 0)
    col = lax.broadcasted_iota(jnp.int32, (size, width), 1)
    for h in range(heads):
        if near_refs:
            near = near_refs[0][h]
            pair = jnp.concatenate(composed(near, far_ref[h], size), axis=1)
            near = near.astype(f32)
        else:
            near, pair = jnp.where(row == col, 1.0, 0.0), far_ref[h].astype(f32)
        out_ref[h] = jnp.where(place("seq", bit) == 1, pair, near).astype(bf16)


def before(bit, near, far):
    return vmem_call(
        functools.partial(before_body, bit),
        jax.ShapeDtypeStruct(far.shape, bf16),
        (far, *near),
        flops=2 * math.prod(far.shape) * far.shape[1],
        moved=6 * math.prod(far.shape),
    )


def entry_body(bit, near_ref, far_ref, own_ref, partner_ref, keep_ref, send_ref):
    heads, size, _ = near_ref.shape
    arrived, upper = place("seq", bit) == 1, place("seq", 1) == 1
    for h in range(heads):
        state = dot(near_ref[h, :, :size], far_ref[h])
        state = jnp.where(arrived, state, 0.0) + near_ref[h, :, size:].astype(f32)
        first = jnp.where(upper, partner_ref[h], own_ref[h])
        state = state.astype(bf16)
        later = dot(first[:, :size], state) + first[:, size:].astype(f32)
        later = later.astype(bf16)
        keep_ref[h] = jnp.where(upper, later, state)
        send_ref[h] = jnp.where(upper, state, later)


def entry_states(own, other):
    heads, size, width = own.shape
    bits = bits_of(lax.axis_size("seq"))
    partner = swapped(other, "seq", 1)
    total = join(1, own, partner, len(bits) == 2)
    near = ()
    assert len(bits) > 2
    for bit in bits[1:-1]:
        far = swapped(total, "seq", bit)
        total = join(bit, total, far, 2 * bit == bits[-1])
        near = (before(bit, near, far),)
    far = swapped(total, "seq", bits[-1])
    state = jax.ShapeDtypeStruct((heads, size, size), bf16)
    keep, send = vmem_call(
        functools.partial(entry_body, bits[-1]),
        (state, state),
        (*near, far, own, partner),
        flops=4 * heads * size * size * size,
        moved=14 * heads * size * size,
    )
    return keep, swapped(send, "seq", 1)


def norm_body(places, *refs):
    own_refs, other_refs, refs = refs[:GROUPS], refs[GROUPS : 2 * GROUPS], refs[2 * GROUPS :]
    raised_ref, output_ref, gate_ref, gain_ref, *normed_refs = refs
    size = gain_ref.shape[1]
    slab_rows = normed_refs[0].shape[0]
    share = own_refs[0].shape[0]
    half = GROUPS * share
    upper = place("seq", 1) == 1
    for h in range(raised_ref.shape[0]):
        lanes = slice(h * size, (h + 1) * size)
        group, at = divmod(h % half, share)
        own, other = own_refs[group][at], other_refs[group][at]
        state = jnp.where(upper, other, own) if h < half else jnp.where(upper, own, other)
        for away, normed_ref in zip(places, normed_refs):
            rows = pl.ds(pl.multiple_of((place("head") ^ away) * slab_rows, 16), slab_rows)
            attended = dot(raised_ref[h, rows, :], state) + output_ref[rows, lanes]
            power = jnp.sum(attended * attended, -1, keepdims=True) * (1.0 / size)
            normed_ref[:, lanes] = (
                attended * lax.rsqrt(power + 1e-05) * gain_ref[...] * gate_ref[rows, lanes]
            ).astype(bf16)


def normed_rows(places, states, raised, output_rows, out_gate, gain, slab_rows):
    shape = jax.ShapeDtypeStruct((slab_rows, output_rows.shape[1]), bf16)
    return vmem_call(
        functools.partial(norm_body, places),
        [shape] * len(places),
        (*states, raised, output_rows, out_gate, gain),
        grant=6,
        flops=2 * len(places) * slab_rows * output_rows.shape[1] * gain.shape[1],
        moved=8 * output_rows.size,
    )


def product_body(one_ref, two_ref, own_ref, other_ref, out_ref):
    total = dot(one_ref[...], own_ref[...]) + dot(two_ref[...], other_ref[...])
    out_ref[...] = total.astype(out_ref.dtype)


def product_rows(one, two, own_weight, other_weight, dtype):
    rows, width = one.shape[0], own_weight.shape[1]
    return vmem_call(
        product_body,
        jax.ShapeDtypeStruct((rows, width), dtype),
        (one, two, own_weight, other_weight),
        grant=8,
        flops=4 * rows * own_weight.size,
        moved=4 * own_weight.size,
    )


def shards(
    hidden_in,
    qkv_weight,
    conv_weight,
    decay_log,
    dt_bias,
    decay_down,
    decay_up,
    beta_weight,
    gate_down,
    gate_up,
    norm_gain,
    out_weight,
):
    heads, size = decay_log.shape[0], norm_gain.shape[0]
    channels = heads * size
    devices = lax.axis_size("head")
    weight = qkv_weight.transpose(1, 0, 2)
    fetched = load(hidden_in, decay_down, gate_down, beta_weight.T, weight)
    slabs, rims, fetched = gathered(hidden_in, fetched)
    rims, late_weight = lax.optimization_barrier((rims, out_weight))
    near_weight = swapped(late_weight, "head", 1)
    *pairs, solved, attend, start, gate_low = front(
        rims, slabs, fetched, (decay_log, decay_up, dt_bias[None], conv_weight), weight, size
    )
    count = start.shape[1]
    attend, near_weight = lax.optimization_barrier((attend, near_weight))
    raised, output_rows, out_gate = vmem_call(
        rows_body,
        (
            jax.ShapeDtypeStruct((heads, count, size), bf16),
            jax.ShapeDtypeStruct((count, channels), f32),
            jax.ShapeDtypeStruct((count, channels), f32),
        ),
        (attend, solved, start, gate_low, gate_up),
        grant=8,
        flops=2 * heads * count * count * 2 * size,
        moved=4 * heads * count * count,
    )
    states = [entry_states(*both) for both in zip(pairs[:GROUPS], pairs[GROUPS:])]
    states = [own for own, _ in states] + [other for _, other in states]
    slab_rows = count // devices
    sums = {}
    for g in reversed(range(devices // 2)):
        keep, send = normed_rows(
            [2 * g, 2 * g + 1], states, raised, output_rows, out_gate, norm_gain[None], slab_rows
        )
        received = swapped(send, "head", 1)
        sums[g] = [product_rows(keep, received, out_weight, near_weight, bf16 if g else f32)]
    for bit in bits_of(devices)[1:]:
        for g in sorted(sums):
            if 2 * g & bit:
                parts = sums.pop(g)
                parts = parts[0] if len(parts) == 1 else sum(p.astype(f32) for p in parts)
                arrived = swapped(parts.astype(bf16), "head", bit)
                sums[g ^ bit // 2].append(arrived.astype(f32))
    return sum(sums[0]).astype(bf16)


def solution(mesh):
    return jax.shard_map(
        shards,
        mesh=mesh,
        in_specs=(
            P(("seq", "head"), None),
            P(None, None, "head"),
            P(None, None, "head"),
            P("head"),
            P("head"),
            P(),
            P(None, "head"),
            P(None, "head"),
            P(),
            P(None, "head"),
            P(),
            P("head", None),
        ),
        out_specs=P(("seq", "head"), None),
        check_vma=False,
    )
```

```python
import functools
import math

import jax
import jax.numpy as jnp
from jax import lax
from jax.experimental import pallas as pl
from jax.experimental.pallas import tpu as pltpu
from jax.sharding import PartitionSpec as P

RIM = 16
BASE = 16
GROUPS = 2
MIB = 1024 * 1024
f32 = jnp.float32
bf16 = jnp.bfloat16


def dot(left, right, contract=((1,), (0,))):
    return lax.dot_general(left, right, (contract, ((), ())), preferred_element_type=f32)


def swapped(block, axis, bit):
    return lax.ppermute(block, axis, [(i, i ^ bit) for i in range(lax.axis_size(axis))])


def bits_of(size):
    assert size & (size - 1) == 0
    return [1 << i for i in range(size.bit_length() - 1)]


def rim_route(target):
    heads, seqs = lax.axis_size("head"), lax.axis_size("seq")
    return [(s * heads + heads - 1, (s + 1) * heads + target) for s in range(seqs - 1)]


def pick_body(targets, *refs):
    *tail_refs, rim_ref = refs
    rim = jnp.zeros(tail_refs[0].shape, f32)
    above = jnp.zeros((rim_ref.shape[0] - rim.shape[0], rim.shape[1]), f32)
    for target, ref in zip(targets, tail_refs):
        rim = jnp.where(place("head") == target, ref[...].astype(f32), rim)
    rim_ref[...] = jnp.concatenate([above, rim], axis=0).astype(rim_ref.dtype)


def gathered(own, loaded):
    heads = lax.axis_size("head")
    bits = bits_of(heads)
    assert bits
    slabs = {0: own}
    for bit in reversed(bits[1:]):
        for k in sorted(slabs):
            slabs[k ^ bit] = swapped(slabs[k], "head", bit)
    tail = own[own.shape[0] - RIM // 2 :]
    targets = [first if first == heads - 2 else first + 1 for first in range(0, heads, 2)][::-1]
    tails = [lax.ppermute(tail, ("seq", "head"), rim_route(target)) for target in targets]
    slabs[1] = swapped(own, "head", 1)
    arrived = [k for k in sorted(slabs) if k > 1]
    moved, tails, loaded = lax.optimization_barrier(
        ([slabs[k] for k in arrived], tails, loaded)
    )
    for k, slab in zip(arrived, moved):
        slabs[k], slabs[k ^ 1] = slab, swapped(slab, "head", 1)
    rim = vmem_call(
        functools.partial(pick_body, targets), jax.ShapeDtypeStruct((RIM, own.shape[1]), bf16), tails
    )
    return [slabs[k] for k in range(1, heads)], [rim, swapped(rim, "head", 1)], loaded


def vmem_call(body, out_shape, args, scratch=(), hbm=0, grant=4, flops=0, moved=0):
    here = len(args) - hbm
    args = [pltpu.with_memory_space_constraint(a, pltpu.HBM) if i >= here else a for i, a in enumerate(args)]
    spaces = [pltpu.VMEM] * here + [pltpu.HBM] * hbm
    return pl.pallas_call(
        body,
        out_shape=out_shape,
        in_specs=[pl.BlockSpec(memory_space=space) for space in spaces],
        out_specs=jax.tree.map(lambda _: pl.BlockSpec(memory_space=pltpu.VMEM), out_shape),
        scratch_shapes=list(scratch),
        compiler_params=pltpu.CompilerParams(vmem_limit_bytes=grant * MIB),
        cost_estimate=pl.CostEstimate(flops=flops, bytes_accessed=moved, transcendentals=0),
    )(*args)


def place(axis, bit=None):
    here = lax.axis_index(axis)
    return here if bit is None else here // bit % 2


def column_pieces(width):
    step = math.gcd(width, 256)
    return [slice(i, i + step) for i in range(0, width, step)]


def load_body(
    hidden_ref, decay_down_ref, beta_ref, weight_ref, own_ref, weights, downs, betas, sems
):
    rank, heads = decay_down_ref.shape[1], beta_ref.shape[0]
    beta = pltpu.make_async_copy(beta_ref, betas, sems.at[0])
    copies = [
        pltpu.make_async_copy(hidden_ref, own_ref, sems.at[1]),
        pltpu.make_async_copy(decay_down_ref, downs.at[:, pl.ds(0, rank)], sems.at[2]),
    ]
    for c in range(2):
        copies.append(pltpu.make_async_copy(weight_ref.at[c], weights.at[c], sems.at[3 + c]))
    for copy in [beta] + copies:
        copy.start()
    beta.wait()
    below = jnp.zeros((rank - heads, betas.shape[1]), f32)
    wide = jnp.concatenate([betas[...].astype(f32), below], axis=0)
    downs[:, rank:] = wide.T.astype(bf16)
    for copy in copies:
        copy.wait()


def load(own, decay_down, beta, weight):
    width, rank = decay_down.shape
    return vmem_call(
        load_body,
        (
            jax.ShapeDtypeStruct(own.shape, bf16),
            jax.ShapeDtypeStruct((2, *weight.shape[1:]), bf16),
            jax.ShapeDtypeStruct((width, 2 * rank), bf16),
        ),
        (own, decay_down, beta, weight),
        scratch=[pltpu.VMEM(beta.shape, bf16), pltpu.SemaphoreType.DMA((5,))],
        hbm=4,
        grant=12,
    )


def front_body(slab_count, *refs):
    (one_ref, two_ref, *slab_refs), refs = refs[: slab_count + 1], refs[slab_count + 1 :]
    (own_rows_ref, weights, downs), refs = refs[:3], refs[3:]
    hbm_refs, refs = refs[:5], refs[5:]
    (own_refs, other_refs), refs = (refs[:GROUPS], refs[GROUPS : 2 * GROUPS]), refs[2 * GROUPS :]
    (solved_ref, attend_ref, start_ref, rows_ref), refs = refs[:4], refs[4:]
    loaded, refs = refs[:5], refs[5:]
    projected, running_ref, parts_ref, mixing, inverse, sides, sems = refs
    rates, decay_up_ref, bias_ref, conv_ref, value_weight = loaded
    weight_ref = hbm_refs[-1]
    heads, count, size = start_ref.shape
    slab_rows = count // slab_count
    tap_count = conv_ref.shape[1]
    rank = decay_up_ref.shape[0]
    chunk = math.gcd(count, 64)
    chunks = count // chunk
    block = math.gcd(count, 128)
    blocks = count // block
    here = place("head")

    def rows_of(k):
        return pl.ds(pl.multiple_of(RIM + (here ^ k) * slab_rows, 16), slab_rows)

    small = [pltpu.make_async_copy(hbm_refs[i], loaded[i], sems.at[i]) for i in range(4)]
    pieces = column_pieces(heads * size)
    streams = []
    for i, piece in enumerate(pieces):
        streams.append(
            pltpu.make_async_copy(
                weight_ref.at[2, :, piece], value_weight.at[:, piece], sems.at[4 + i]
            )
        )
    for copy in small + streams:
        copy.start()
    rows_ref[:RIM, :] = (one_ref[...].astype(f32) + two_ref[...].astype(f32)).astype(bf16)
    for k, ref in enumerate([own_rows_ref, *slab_refs]):
        rows_ref[rows_of(k), :] = ref[...]

    def project(c, piece, weight):
        result = dot(rows_ref[...], weight)
        for begin in range(piece.start, piece.stop, size):
            at = begin - piece.start
            projected[c * heads + begin // size] = result[:, at : at + size]

    pending = [(c, piece) for piece in pieces for c in range(2)]
    share = (pieces[0].stop - pieces[0].start) // size

    def project_next(number):
        for c, piece in pending[:number]:
            project(c, piece, weights[c, :, piece])
        del pending[:number]

    project_next(2)
    low = dot(rows_ref[RIM:, :], downs[...])
    strength = jax.nn.sigmoid(low[:, rank:])
    for copy in small:
        copy.wait()
    running_ref[...] = dot(low[:, :rank].astype(bf16), decay_up_ref[...])
    tiles = [slice(a * chunk, (a + 1) * chunk) for a in range(chunks)]
    for h in range(heads):
        lanes = slice(h * size, (h + 1) * size)
        rate = jnp.exp(jnp.full((1, size), rates[h], f32))
        for rows in tiles:
            raw = running_ref[rows, lanes] + bias_ref[:, lanes]
            softplus = jnp.maximum(raw, 0.0) + jnp.log(1.0 + jnp.exp(-jnp.abs(raw)))
            log_decay = -rate * softplus
            high = log_decay.astype(bf16)
            parts_ref[rows, lanes] = high
            rest = (log_decay - high.astype(f32)).astype(bf16)
            parts_ref[count + rows.start : count + rows.stop, lanes] = rest
    row = lax.broadcasted_iota(jnp.int32, (count, count), 0)
    col = lax.broadcasted_iota(jnp.int32, (count, count), 1)
    lower = jnp.where(row >= col, 1.0, 0.0).astype(bf16)
    running_ref[...] = dot(jnp.concatenate([lower, lower], axis=1), parts_ref[...])

    def convolved(c, rows, h):
        taps = conv_ref[c].astype(f32)[:, h * size : (h + 1) * size]
        total = None
        for i in range(tap_count):
            first = RIM - tap_count + 1 + i + rows.start
            term = projected[c * heads + h, pl.ds(first, chunk), :] * taps[i : i + 1]
            total = term if total is None else total + term
        half = 0.5 * total
        return half + half * jnp.tanh(half)

    for copy in streams:
        copy.wait()
    stops = []
    for h in range(heads):
        lanes = slice(h * size, (h + 1) * size)
        last = running_ref[count - 1 : count, lanes]
        middles, key_falls, stop, lefts = [], [], [], []
        for rows in tiles:
            running = running_ref[rows, lanes]
            middle = running[chunk // 2 : chunk // 2 + 1]
            above = running - middle
            rise, entry = jnp.exp(above), jnp.exp(middle)
            queries = convolved(0, rows, h)
            power = jnp.sum(queries * queries, -1, keepdims=True)
            queries = queries * (lax.rsqrt(power + 1e-06) * size ** (-0.5)) * rise
            start_ref[h, rows, :] = (queries * entry).astype(bf16)
            keys = convolved(1, rows, h)
            power = jnp.sum(keys * keys, -1, keepdims=True)
            keys = keys * lax.rsqrt(power + 1e-06)
            key_fall = keys * strength[rows, h : h + 1] * jnp.exp(-above)
            keys = keys * rise
            sides[h, rows, :size] = (keys * entry).astype(bf16)
            stop.append((key_fall * jnp.exp(last - middle)).astype(bf16))
            middles.append(middle)
            key_falls.append(key_fall)
            lefts.append(jnp.concatenate([keys.astype(bf16), queries.astype(bf16)], axis=0))
        stops.append((jnp.concatenate(stop, axis=0), jnp.exp(last)))
        project_next(pl.cdiv(2, share))
        for a in range(chunks):
            rows = tiles[a]
            reach = (a * chunk // block + 1) * block
            falls = []
            for b in range(reach // chunk):
                if b < a:
                    falls.append(key_falls[b] * jnp.exp(middles[a] - middles[b]))
                elif b == a:
                    falls.append(key_falls[b])
                else:
                    falls.append(jnp.zeros((chunk, size), f32))
            right = jnp.concatenate(falls, axis=0).astype(bf16)
            scores = dot(lefts[a], right, ((1,), (1,)))
            inside = slice(reach - block, reach)
            if reach > block:
                before = slice(0, reach - block)
                mixing[h, rows, before] = scores[:chunk, before].astype(bf16)
                attend_ref[h, rows, before] = scores[chunk:, before].astype(bf16)
            at, to = row[rows, inside], col[rows, inside]
            mixing[h, rows, inside] = jnp.where(at > to, scores[:chunk, inside], 0.0).astype(bf16)
            attend_ref[h, rows, inside] = jnp.where(
                at >= to, scores[chunk:, inside], 0.0
            ).astype(bf16)

    def value_side(h):
        for rows in tiles:
            sides[h, rows, size:] = convolved(2, rows, h).astype(bf16)

    between = [functools.partial(project, 2, p, value_weight[:, p]) for p in pieces]
    between += [functools.partial(value_side, h) for h in range(heads)]

    at, to = row[:block, :block], col[:block, :block]
    eye = jnp.where(at == to, 1.0, 0.0).astype(bf16)
    base = math.gcd(block, BASE)
    near = jnp.where(at // base == to // base, -1.0, 0.0).astype(bf16)
    corners = [(h, slice(d * block, (d + 1) * block)) for h in range(heads) for d in range(blocks)]
    powers = [mixing[h, d, d] * near for h, d in corners]
    totals = [power + eye for power in powers]
    steps = (base - 1).bit_length() - 1
    if steps:
        powers = [dot(power, power).astype(bf16) for power in powers]
    for step in range(steps):
        for n in range(len(corners)):
            power, total = powers[n], totals[n]
            if step < steps - 1:
                both = dot(jnp.concatenate([power, total], axis=0), power)
                powers[n], more = both[:block].astype(bf16), both[block:]
            else:
                more = dot(total, power)
            totals[n] = (total.astype(f32) + more).astype(bf16)
        if between:
            between.pop(0)()
    for (h, d), total in zip(corners, totals):
        inverse[h, d, :] = total
    width = base
    while width < block:
        odd = range(width, block, 2 * width)
        pair_mask = (at // width % 2 == 1) & (to // width == at // width - 1)
        pair_mask = jnp.where(pair_mask, 1.0, 0.0).astype(bf16)
        halves = []
        for h, d in corners:
            parts = [inverse[h, d.start + i : d.start + i + width, :] for i in odd]
            chosen = jnp.concatenate(parts, axis=0)
            halves.append((chosen, dot(chosen, mixing[h, d, d] * pair_mask).astype(bf16)))
        for (h, d), (chosen, half) in zip(corners, halves):
            new = (chosen.astype(f32) - dot(half, inverse[h, d, :])).astype(bf16)
            for n, i in enumerate(odd):
                inverse[h, d.start + i : d.start + i + width, :] = new[n * width : (n + 1) * width]
        if between:
            between.pop(0)()
        width *= 2
    for work in between:
        work()

    for d in range(blocks):
        rows = slice(d * block, (d + 1) * block)
        for h in range(heads):
            side = sides[h, rows, :]
            if d:
                done = solved_ref[h, : d * block, :]
                side = (side.astype(f32) - dot(mixing[h, rows, : d * block], done)).astype(bf16)
            solved_ref[h, rows, :] = dot(inverse[h, rows, :], side).astype(bf16)
    pairs = []
    unit = row[:size, :size] == col[:size, :size]
    for h in range(heads):
        stop, fade = stops[h]
        moved = dot(stop, solved_ref[h], ((0,), (0,)))
        diagonal = jnp.where(unit, jnp.broadcast_to(fade, (size, size)), 0.0)
        pairs.append(jnp.concatenate([diagonal - moved[:, :size], moved[:, size:]], axis=1))
    upper = place("seq", 1) == 1
    for h in range(heads // 2):
        low, high = pairs[h], pairs[heads // 2 + h]
        group, at = divmod(h, own_refs[0].shape[0])
        own_refs[group][at] = jnp.where(upper, high, low).astype(bf16)
        other_refs[group][at] = jnp.where(upper, low, high).astype(bf16)


def front(rims, slabs, fetched, loaded, weight, size):
    slab_count, slab_rows = 1 + len(slabs), slabs[0].shape[0]
    count = slab_count * slab_rows
    _, width, channels = weight.shape
    heads, block = channels // size, math.gcd(count, 128)
    buffers = [pltpu.SMEM(loaded[0].shape, f32)]
    buffers += [pltpu.VMEM(part.shape, part.dtype) for part in loaded[1:]]
    return vmem_call(
        functools.partial(front_body, slab_count),
        (
            *[jax.ShapeDtypeStruct((heads // 2 // GROUPS, size, 2 * size), bf16)] * (2 * GROUPS),
            jax.ShapeDtypeStruct((heads, count, 2 * size), bf16),
            jax.ShapeDtypeStruct((heads, count, count), bf16),
            jax.ShapeDtypeStruct((heads, count, size), bf16),
            jax.ShapeDtypeStruct((RIM + count, width), bf16),
        ),
        (*rims, *slabs, *fetched, *loaded, weight),
        scratch=[
            *buffers,
            pltpu.VMEM((width, channels), bf16),
            pltpu.VMEM((3 * heads, RIM + count, size), f32),
            pltpu.VMEM((count, channels), f32),
            pltpu.VMEM((2 * count, channels), bf16),
            pltpu.VMEM((heads, count, count), bf16),
            pltpu.VMEM((heads, count, block), bf16),
            pltpu.VMEM((heads, count, 2 * size), bf16),
            pltpu.SemaphoreType.DMA((4 + len(column_pieces(channels)),)),
        ],
        hbm=1 + len(loaded),
        grant=24,
        flops=2 * count * width * channels * 4,
        moved=2 * 4 * width * channels,
    )


def rows_body(
    attend_ref, solved_ref, start_ref, rows_ref, down_ref, up_ref, raised_ref, output_ref, gate_ref
):
    heads, _, size = start_ref.shape
    low = dot(rows_ref[RIM:, :], down_ref[...]).astype(bf16)
    gate_ref[...] = jax.nn.sigmoid(dot(low, up_ref[...]))
    count = attend_ref.shape[1]
    block = math.gcd(count, 128)
    for h in range(heads):
        for begin in range(0, count, block):
            rows, reach = slice(begin, begin + block), slice(0, begin + block)
            both = dot(attend_ref[h, rows, reach], solved_ref[h, reach, :])
            raised_ref[h, rows, :] = (start_ref[h, rows, :].astype(f32) - both[:, :size]).astype(bf16)
            output_ref[rows, h * size : (h + 1) * size] = both[:, size:]


def composed(later, first, size):
    both = dot(later[:, :size], first)
    return both[:, :size], both[:, size:] + later[:, size:].astype(f32)


def put(ref, h, pair):
    size = ref.shape[1]
    if ref.shape[2] > size:
        ref[h, :, :size] = pair[0].astype(bf16)
    ref[h, :, ref.shape[2] - size :] = pair[1].astype(bf16)


def join_body(bit, own_ref, far_ref, total_ref):
    heads, size, _ = own_ref.shape
    for h in range(heads):
        own, far = own_ref[h], far_ref[h]
        upper = place("seq", bit) == 1
        later, first = jnp.where(upper, own, far), jnp.where(upper, far, own)
        put(total_ref, h, composed(later, first, size))


def join(bit, own, far, last):
    heads, size, width = own.shape
    return vmem_call(
        functools.partial(join_body, bit),
        jax.ShapeDtypeStruct((heads, size, size if last else width), bf16),
        (own, far),
        flops=2 * heads * size * size * width,
        moved=6 * heads * size * width,
    )


def before_body(bit, far_ref, *refs):
    *near_refs, out_ref = refs
    heads, size, width = far_ref.shape
    row = lax.broadcasted_iota(jnp.int32, (size, width), 0)
    col = lax.broadcasted_iota(jnp.int32, (size, width), 1)
    for h in range(heads):
        if near_refs:
            near = near_refs[0][h]
            pair = jnp.concatenate(composed(near, far_ref[h], size), axis=1)
            near = near.astype(f32)
        else:
            near, pair = jnp.where(row == col, 1.0, 0.0), far_ref[h].astype(f32)
        out_ref[h] = jnp.where(place("seq", bit) == 1, pair, near).astype(bf16)


def before(bit, near, far):
    return vmem_call(
        functools.partial(before_body, bit),
        jax.ShapeDtypeStruct(far.shape, bf16),
        (far, *near),
        flops=2 * math.prod(far.shape) * far.shape[1],
        moved=6 * math.prod(far.shape),
    )


def entry_body(bit, near_ref, far_ref, own_ref, partner_ref, keep_ref, send_ref):
    heads, size, _ = near_ref.shape
    arrived, upper = place("seq", bit) == 1, place("seq", 1) == 1
    for h in range(heads):
        state = dot(near_ref[h, :, :size], far_ref[h])
        state = jnp.where(arrived, state, 0.0) + near_ref[h, :, size:].astype(f32)
        first = jnp.where(upper, partner_ref[h], own_ref[h])
        state = state.astype(bf16)
        later = dot(first[:, :size], state) + first[:, size:].astype(f32)
        later = later.astype(bf16)
        keep_ref[h] = jnp.where(upper, later, state)
        send_ref[h] = jnp.where(upper, state, later)


def entry_states(own, other):
    heads, size, width = own.shape
    bits = bits_of(lax.axis_size("seq"))
    partner = swapped(other, "seq", 1)
    total = join(1, own, partner, len(bits) == 2)
    near = ()
    assert len(bits) > 2
    for bit in bits[1:-1]:
        far = swapped(total, "seq", bit)
        total = join(bit, total, far, 2 * bit == bits[-1])
        near = (before(bit, near, far),)
    far = swapped(total, "seq", bits[-1])
    state = jax.ShapeDtypeStruct((heads, size, size), bf16)
    keep, send = vmem_call(
        functools.partial(entry_body, bits[-1]),
        (state, state),
        (*near, far, own, partner),
        flops=4 * heads * size * size * size,
        moved=14 * heads * size * size,
    )
    return keep, swapped(send, "seq", 1)


def back_body(away, *refs):
    own_refs, other_refs, refs = refs[:GROUPS], refs[GROUPS : 2 * GROUPS], refs[2 * GROUPS :]
    raised_ref, output_ref, gate_ref, gain_ref, weight_ref, out_ref, normed = refs
    size = gain_ref.shape[1]
    slab_rows = out_ref.shape[0]
    share = own_refs[0].shape[0]
    half = GROUPS * share
    upper = place("seq", 1) == 1
    rows = pl.ds(pl.multiple_of((place("head") ^ away) * slab_rows, 16), slab_rows)
    for h in range(raised_ref.shape[0]):
        lanes = slice(h * size, (h + 1) * size)
        group, at = divmod(h % half, share)
        own, other = own_refs[group][at], other_refs[group][at]
        state = jnp.where(upper, other, own) if h < half else jnp.where(upper, own, other)
        attended = dot(raised_ref[h, rows, :], state) + output_ref[rows, lanes]
        power = jnp.sum(attended * attended, -1, keepdims=True) * (1.0 / size)
        normed[:, lanes] = (
            attended * lax.rsqrt(power + 1e-05) * gain_ref[...] * gate_ref[rows, lanes]
        ).astype(bf16)
    out_ref[...] = dot(normed[...], weight_ref[...]).astype(out_ref.dtype)


def back(away, states, raised, output_rows, out_gate, gain, weight, slab_rows, dtype):
    width = weight.shape[1]
    return vmem_call(
        functools.partial(back_body, away),
        jax.ShapeDtypeStruct((slab_rows, width), dtype),
        (*states, raised, output_rows, out_gate, gain, weight),
        scratch=[pltpu.VMEM((slab_rows, weight.shape[0]), bf16)],
        grant=10,
        flops=2 * slab_rows * weight.shape[0] * width,
        moved=2 * weight.shape[0] * width,
    )


def shards(
    hidden_in,
    qkv_weight,
    conv_weight,
    decay_log,
    dt_bias,
    decay_down,
    decay_up,
    beta_weight,
    gate_down,
    gate_up,
    norm_gain,
    out_weight,
):
    heads, size = decay_log.shape[0], norm_gain.shape[0]
    channels = heads * size
    devices = lax.axis_size("head")
    weight = qkv_weight.transpose(1, 0, 2)
    fetched = load(hidden_in, decay_down, beta_weight.T, weight)
    slabs, rims, fetched = gathered(hidden_in, fetched)
    *pairs, solved, attend, start, rows = front(
        rims, slabs, fetched, (decay_log, decay_up, dt_bias[None], conv_weight), weight, size
    )
    count = start.shape[1]
    raised, output_rows, out_gate = vmem_call(
        rows_body,
        (
            jax.ShapeDtypeStruct((heads, count, size), bf16),
            jax.ShapeDtypeStruct((count, channels), f32),
            jax.ShapeDtypeStruct((count, channels), f32),
        ),
        (attend, solved, start, rows, gate_down, gate_up),
        grant=8,
        flops=2 * heads * count * count * 2 * size,
        moved=4 * heads * count * count,
    )
    states = [entry_states(*both) for both in zip(pairs[:GROUPS], pairs[GROUPS:])]
    states = [own for own, _ in states] + [other for _, other in states]
    slab_rows = count // devices
    sums = {}
    for g in reversed(range(devices // 2)):
        rest = (states, raised, output_rows, out_gate, norm_gain[None], out_weight, slab_rows)
        near = swapped(back(2 * g + 1, *rest, bf16), "head", 1).astype(f32)
        sums[g] = [lax.optimization_barrier(back(2 * g, *rest, f32) + near)]
    for bit in bits_of(devices)[1:]:
        for g in sorted(sums):
            if 2 * g & bit:
                arrived = swapped(sum(sums.pop(g)).astype(bf16), "head", bit)
                sums[g ^ bit // 2].append(arrived.astype(f32))
    return sum(sums[0]).astype(bf16)


def solution(mesh):
    return jax.shard_map(
        shards,
        mesh=mesh,
        in_specs=(
            P(("seq", "head"), None),
            P(None, None, "head"),
            P(None, None, "head"),
            P("head"),
            P("head"),
            P(),
            P(None, "head"),
            P(None, "head"),
            P(),
            P(None, "head"),
            P(),
            P("head", None),
        ),
        out_specs=P(("seq", "head"), None),
        check_vma=False,
    )
```

```python
import functools
import math

import jax
import jax.numpy as jnp
from jax import lax
from jax.experimental import pallas as pl
from jax.experimental.pallas import tpu as pltpu
from jax.sharding import PartitionSpec as P

RIM = 16
BASE = 16
GROUPS = 2
MIB = 1024 * 1024
f32 = jnp.float32
bf16 = jnp.bfloat16


def dot(left, right, contract=((1,), (0,))):
    return lax.dot_general(left, right, (contract, ((), ())), preferred_element_type=f32)


def swapped(block, axis, bit):
    return lax.ppermute(block, axis, [(i, i ^ bit) for i in range(lax.axis_size(axis))])


def bits_of(size):
    assert size & (size - 1) == 0
    return [1 << i for i in range(size.bit_length() - 1)]


def rim_route(target):
    heads, seqs = lax.axis_size("head"), lax.axis_size("seq")
    return [(s * heads + heads - 1, (s + 1) * heads + target) for s in range(seqs - 1)]


def pick_body(targets, *refs):
    *tail_refs, rim_ref = refs
    rim = jnp.zeros(tail_refs[0].shape, f32)
    above = jnp.zeros((rim_ref.shape[0] - rim.shape[0], rim.shape[1]), f32)
    for target, ref in zip(targets, tail_refs):
        rim = jnp.where(place("head") == target, ref[...].astype(f32), rim)
    rim_ref[...] = jnp.concatenate([above, rim], axis=0).astype(rim_ref.dtype)


def gathered(own, loaded):
    heads = lax.axis_size("head")
    bits = bits_of(heads)
    assert bits
    slabs = {0: own}
    for bit in reversed(bits[1:]):
        for k in sorted(slabs):
            slabs[k ^ bit] = swapped(slabs[k], "head", bit)
    tail = own[own.shape[0] - RIM // 2 :]
    targets = [first if first == heads - 2 else first + 1 for first in range(0, heads, 2)][::-1]
    tails = [lax.ppermute(tail, ("seq", "head"), rim_route(target)) for target in targets]
    slabs[1] = swapped(own, "head", 1)
    arrived = [k for k in sorted(slabs) if k > 1]
    moved, tails, loaded = lax.optimization_barrier(
        ([slabs[k] for k in arrived], tails, loaded)
    )
    for k, slab in zip(arrived, moved):
        slabs[k], slabs[k ^ 1] = slab, swapped(slab, "head", 1)
    rim = vmem_call(
        functools.partial(pick_body, targets), jax.ShapeDtypeStruct((RIM, own.shape[1]), bf16), tails
    )
    return [slabs[k] for k in range(1, heads)], [rim, swapped(rim, "head", 1)], loaded


def vmem_call(body, out_shape, args, scratch=(), hbm=0, grant=4, flops=0, moved=0):
    here = len(args) - hbm
    args = [pltpu.with_memory_space_constraint(a, pltpu.HBM) if i >= here else a for i, a in enumerate(args)]
    spaces = [pltpu.VMEM] * here + [pltpu.HBM] * hbm
    return pl.pallas_call(
        body,
        out_shape=out_shape,
        in_specs=[pl.BlockSpec(memory_space=space) for space in spaces],
        out_specs=jax.tree.map(lambda _: pl.BlockSpec(memory_space=pltpu.VMEM), out_shape),
        scratch_shapes=list(scratch),
        compiler_params=pltpu.CompilerParams(vmem_limit_bytes=grant * MIB),
        cost_estimate=pl.CostEstimate(flops=flops, bytes_accessed=moved, transcendentals=0),
    )(*args)


def place(axis, bit=None):
    here = lax.axis_index(axis)
    return here if bit is None else here // bit % 2


def column_pieces(width):
    step = math.gcd(width, 256)
    return [slice(i, i + step) for i in range(0, width, step)]


def load_body(
    hidden_ref, decay_down_ref, beta_ref, weight_ref, own_ref, weights, downs, betas, sems
):
    rank, heads = decay_down_ref.shape[1], beta_ref.shape[0]
    beta = pltpu.make_async_copy(beta_ref, betas, sems.at[0])
    copies = [
        pltpu.make_async_copy(hidden_ref, own_ref, sems.at[1]),
        pltpu.make_async_copy(decay_down_ref, downs.at[:, pl.ds(0, rank)], sems.at[2]),
    ]
    for c in range(2):
        copies.append(pltpu.make_async_copy(weight_ref.at[c], weights.at[c], sems.at[3 + c]))
    for copy in [beta] + copies:
        copy.start()
    beta.wait()
    below = jnp.zeros((rank - heads, betas.shape[1]), f32)
    wide = jnp.concatenate([betas[...].astype(f32), below], axis=0)
    downs[:, rank:] = wide.T.astype(bf16)
    for copy in copies:
        copy.wait()


def load(own, decay_down, beta, weight):
    width, rank = decay_down.shape
    return vmem_call(
        load_body,
        (
            jax.ShapeDtypeStruct(own.shape, bf16),
            jax.ShapeDtypeStruct((2, *weight.shape[1:]), bf16),
            jax.ShapeDtypeStruct((width, 2 * rank), bf16),
        ),
        (own, decay_down, beta, weight),
        scratch=[pltpu.VMEM(beta.shape, bf16), pltpu.SemaphoreType.DMA((5,))],
        hbm=4,
        grant=12,
    )


def front_body(slab_count, *refs):
    (one_ref, two_ref, *slab_refs), refs = refs[: slab_count + 1], refs[slab_count + 1 :]
    (own_rows_ref, weights, downs), refs = refs[:3], refs[3:]
    hbm_refs, refs = refs[:5], refs[5:]
    (own_refs, other_refs), refs = (refs[:GROUPS], refs[GROUPS : 2 * GROUPS]), refs[2 * GROUPS :]
    (solved_ref, attend_ref, start_ref, rows_ref), refs = refs[:4], refs[4:]
    loaded, refs = refs[:5], refs[5:]
    projected, running_ref, parts_ref, mixing, inverse, sides, sems = refs
    rates, decay_up_ref, bias_ref, conv_ref, value_weight = loaded
    weight_ref = hbm_refs[-1]
    heads, count, size = start_ref.shape
    slab_rows = count // slab_count
    tap_count = conv_ref.shape[1]
    rank = decay_up_ref.shape[0]
    chunk = math.gcd(count, 64)
    chunks = count // chunk
    block = math.gcd(count, 128)
    blocks = count // block
    here = place("head")

    def rows_of(k):
        return pl.ds(pl.multiple_of(RIM + (here ^ k) * slab_rows, 16), slab_rows)

    small = [pltpu.make_async_copy(hbm_refs[i], loaded[i], sems.at[i]) for i in range(4)]
    pieces = column_pieces(heads * size)
    streams = []
    for i, piece in enumerate(pieces):
        streams.append(
            pltpu.make_async_copy(
                weight_ref.at[2, :, piece], value_weight.at[:, piece], sems.at[4 + i]
            )
        )
    for copy in small + streams:
        copy.start()
    rows_ref[:RIM, :] = (one_ref[...].astype(f32) + two_ref[...].astype(f32)).astype(bf16)
    for k, ref in enumerate([own_rows_ref, *slab_refs]):
        rows_ref[rows_of(k), :] = ref[...]

    def project(c, piece, weight):
        result = dot(rows_ref[...], weight)
        for begin in range(piece.start, piece.stop, size):
            at = begin - piece.start
            projected[c * heads + begin // size] = result[:, at : at + size]

    pending = [(c, piece) for piece in pieces for c in range(2)]
    share = (pieces[0].stop - pieces[0].start) // size

    def project_next(number):
        for c, piece in pending[:number]:
            project(c, piece, weights[c, :, piece])
        del pending[:number]

    project_next(2)
    low = dot(rows_ref[RIM:, :], downs[...])
    strength = jax.nn.sigmoid(low[:, rank:])
    for copy in small:
        copy.wait()
    running_ref[...] = dot(low[:, :rank].astype(bf16), decay_up_ref[...])
    tiles = [slice(a * chunk, (a + 1) * chunk) for a in range(chunks)]
    for h in range(heads):
        lanes = slice(h * size, (h + 1) * size)
        rate = jnp.exp(jnp.full((1, size), rates[h], f32))
        for rows in tiles:
            raw = running_ref[rows, lanes] + bias_ref[:, lanes]
            softplus = jnp.maximum(raw, 0.0) + jnp.log(1.0 + jnp.exp(-jnp.abs(raw)))
            log_decay = -rate * softplus
            high = log_decay.astype(bf16)
            parts_ref[rows, lanes] = high
            rest = (log_decay - high.astype(f32)).astype(bf16)
            parts_ref[count + rows.start : count + rows.stop, lanes] = rest
    row = lax.broadcasted_iota(jnp.int32, (count, count), 0)
    col = lax.broadcasted_iota(jnp.int32, (count, count), 1)
    lower = jnp.where(row >= col, 1.0, 0.0).astype(bf16)
    running_ref[...] = dot(jnp.concatenate([lower, lower], axis=1), parts_ref[...])

    def convolved(c, rows, h):
        taps = conv_ref[c].astype(f32)[:, h * size : (h + 1) * size]
        total = None
        for i in range(tap_count):
            first = RIM - tap_count + 1 + i + rows.start
            term = projected[c * heads + h, pl.ds(first, chunk), :] * taps[i : i + 1]
            total = term if total is None else total + term
        half = 0.5 * total
        return half + half * jnp.tanh(half)

    for copy in streams:
        copy.wait()
    stops = []
    for h in range(heads):
        lanes = slice(h * size, (h + 1) * size)
        last = running_ref[count - 1 : count, lanes]
        middles, key_falls, stop, lefts = [], [], [], []
        for rows in tiles:
            running = running_ref[rows, lanes]
            middle = running[chunk // 2 : chunk // 2 + 1]
            above = running - middle
            rise, entry = jnp.exp(above), jnp.exp(middle)
            queries = convolved(0, rows, h)
            power = jnp.sum(queries * queries, -1, keepdims=True)
            queries = queries * (lax.rsqrt(power + 1e-06) * size ** (-0.5)) * rise
            start_ref[h, rows, :] = (queries * entry).astype(bf16)
            keys = convolved(1, rows, h)
            power = jnp.sum(keys * keys, -1, keepdims=True)
            keys = keys * lax.rsqrt(power + 1e-06)
            key_fall = keys * strength[rows, h : h + 1] * jnp.exp(-above)
            keys = keys * rise
            sides[h, rows, :size] = (keys * entry).astype(bf16)
            stop.append((key_fall * jnp.exp(last - middle)).astype(bf16))
            middles.append(middle)
            key_falls.append(key_fall)
            lefts.append(jnp.concatenate([keys.astype(bf16), queries.astype(bf16)], axis=0))
        stops.append((jnp.concatenate(stop, axis=0), jnp.exp(last)))
        project_next(pl.cdiv(2, share))
        for a in range(chunks):
            rows = tiles[a]
            reach = (a * chunk // block + 1) * block
            falls = []
            for b in range(reach // chunk):
                if b < a:
                    falls.append(key_falls[b] * jnp.exp(middles[a] - middles[b]))
                elif b == a:
                    falls.append(key_falls[b])
                else:
                    falls.append(jnp.zeros((chunk, size), f32))
            right = jnp.concatenate(falls, axis=0).astype(bf16)
            scores = dot(lefts[a], right, ((1,), (1,)))
            inside = slice(reach - block, reach)
            if reach > block:
                before = slice(0, reach - block)
                mixing[h, rows, before] = scores[:chunk, before].astype(bf16)
                attend_ref[h, rows, before] = scores[chunk:, before].astype(bf16)
            at, to = row[rows, inside], col[rows, inside]
            mixing[h, rows, inside] = jnp.where(at > to, scores[:chunk, inside], 0.0).astype(bf16)
            attend_ref[h, rows, inside] = jnp.where(
                at >= to, scores[chunk:, inside], 0.0
            ).astype(bf16)

    def value_side(h):
        for rows in tiles:
            sides[h, rows, size:] = convolved(2, rows, h).astype(bf16)

    between = [functools.partial(project, 2, p, value_weight[:, p]) for p in pieces]
    between += [functools.partial(value_side, h) for h in range(heads)]

    at, to = row[:block, :block], col[:block, :block]
    eye = jnp.where(at == to, 1.0, 0.0).astype(bf16)
    base = math.gcd(block, BASE)
    near = jnp.where(at // base == to // base, -1.0, 0.0).astype(bf16)
    corners = [(h, slice(d * block, (d + 1) * block)) for h in range(heads) for d in range(blocks)]
    powers = [mixing[h, d, d] * near for h, d in corners]
    totals = [power + eye for power in powers]
    steps = (base - 1).bit_length() - 1
    if steps:
        powers = [dot(power, power).astype(bf16) for power in powers]
    for step in range(steps):
        for n in range(len(corners)):
            power, total = powers[n], totals[n]
            if step < steps - 1:
                both = dot(jnp.concatenate([power, total], axis=0), power)
                powers[n], more = both[:block].astype(bf16), both[block:]
            else:
                more = dot(total, power)
            totals[n] = (total.astype(f32) + more).astype(bf16)
        if between:
            between.pop(0)()
    for (h, d), total in zip(corners, totals):
        inverse[h, d, :] = total
    width = base
    while width < block:
        odd = range(width, block, 2 * width)
        pair_mask = (at // width % 2 == 1) & (to // width == at // width - 1)
        pair_mask = jnp.where(pair_mask, 1.0, 0.0).astype(bf16)
        halves = []
        for h, d in corners:
            parts = [inverse[h, d.start + i : d.start + i + width, :] for i in odd]
            chosen = jnp.concatenate(parts, axis=0)
            halves.append((chosen, dot(chosen, mixing[h, d, d] * pair_mask).astype(bf16)))
        for (h, d), (chosen, half) in zip(corners, halves):
            new = (chosen.astype(f32) - dot(half, inverse[h, d, :])).astype(bf16)
            for n, i in enumerate(odd):
                inverse[h, d.start + i : d.start + i + width, :] = new[n * width : (n + 1) * width]
        if between:
            between.pop(0)()
        width *= 2
    for work in between:
        work()

    for d in range(blocks):
        rows = slice(d * block, (d + 1) * block)
        for h in range(heads):
            side = sides[h, rows, :]
            if d:
                done = solved_ref[h, : d * block, :]
                side = (side.astype(f32) - dot(mixing[h, rows, : d * block], done)).astype(bf16)
            solved_ref[h, rows, :] = dot(inverse[h, rows, :], side).astype(bf16)
    pairs = []
    unit = row[:size, :size] == col[:size, :size]
    for h in range(heads):
        stop, fade = stops[h]
        moved = dot(stop, solved_ref[h], ((0,), (0,)))
        diagonal = jnp.where(unit, jnp.broadcast_to(fade, (size, size)), 0.0)
        pairs.append(jnp.concatenate([diagonal - moved[:, :size], moved[:, size:]], axis=1))
    upper = place("seq", 1) == 1
    for h in range(heads // 2):
        low, high = pairs[h], pairs[heads // 2 + h]
        group, at = divmod(h, own_refs[0].shape[0])
        own_refs[group][at] = jnp.where(upper, high, low).astype(bf16)
        other_refs[group][at] = jnp.where(upper, low, high).astype(bf16)


def front(rims, slabs, fetched, loaded, weight, size):
    slab_count, slab_rows = 1 + len(slabs), slabs[0].shape[0]
    count = slab_count * slab_rows
    _, width, channels = weight.shape
    heads, block = channels // size, math.gcd(count, 128)
    buffers = [pltpu.SMEM(loaded[0].shape, f32)]
    buffers += [pltpu.VMEM(part.shape, part.dtype) for part in loaded[1:]]
    return vmem_call(
        functools.partial(front_body, slab_count),
        (
            *[jax.ShapeDtypeStruct((heads // 2 // GROUPS, size, 2 * size), bf16)] * (2 * GROUPS),
            jax.ShapeDtypeStruct((heads, count, 2 * size), bf16),
            jax.ShapeDtypeStruct((heads, count, count), bf16),
            jax.ShapeDtypeStruct((heads, count, size), bf16),
            jax.ShapeDtypeStruct((RIM + count, width), bf16),
        ),
        (*rims, *slabs, *fetched, *loaded, weight),
        scratch=[
            *buffers,
            pltpu.VMEM((width, channels), bf16),
            pltpu.VMEM((3 * heads, RIM + count, size), f32),
            pltpu.VMEM((count, channels), f32),
            pltpu.VMEM((2 * count, channels), bf16),
            pltpu.VMEM((heads, count, count), bf16),
            pltpu.VMEM((heads, count, block), bf16),
            pltpu.VMEM((heads, count, 2 * size), bf16),
            pltpu.SemaphoreType.DMA((4 + len(column_pieces(channels)),)),
        ],
        hbm=1 + len(loaded),
        grant=24,
        flops=2 * count * width * channels * 4,
        moved=2 * 4 * width * channels,
    )


def rows_body(
    attend_ref, solved_ref, start_ref, rows_ref, down_ref, up_ref, raised_ref, output_ref, gate_ref
):
    heads, _, size = start_ref.shape
    low = dot(rows_ref[RIM:, :], down_ref[...]).astype(bf16)
    gate_ref[...] = jax.nn.sigmoid(dot(low, up_ref[...]))
    count = attend_ref.shape[1]
    block = math.gcd(count, 128)
    for h in range(heads):
        for begin in range(0, count, block):
            rows, reach = slice(begin, begin + block), slice(0, begin + block)
            both = dot(attend_ref[h, rows, reach], solved_ref[h, reach, :])
            raised_ref[h, rows, :] = (start_ref[h, rows, :].astype(f32) - both[:, :size]).astype(bf16)
            output_ref[rows, h * size : (h + 1) * size] = both[:, size:]


def composed(later, first, size):
    both = dot(later[:, :size], first)
    return both[:, :size], both[:, size:] + later[:, size:].astype(f32)


def put(ref, h, pair):
    size = ref.shape[1]
    if ref.shape[2] > size:
        ref[h, :, :size] = pair[0].astype(bf16)
    ref[h, :, ref.shape[2] - size :] = pair[1].astype(bf16)


def join_body(bit, own_ref, far_ref, total_ref):
    heads, size, _ = own_ref.shape
    for h in range(heads):
        own, far = own_ref[h], far_ref[h]
        upper = place("seq", bit) == 1
        later, first = jnp.where(upper, own, far), jnp.where(upper, far, own)
        put(total_ref, h, composed(later, first, size))


def join(bit, own, far, last):
    heads, size, width = own.shape
    return vmem_call(
        functools.partial(join_body, bit),
        jax.ShapeDtypeStruct((heads, size, size if last else width), bf16),
        (own, far),
        flops=2 * heads * size * size * width,
        moved=6 * heads * size * width,
    )


def before_body(bit, far_ref, *refs):
    *near_refs, out_ref = refs
    heads, size, width = far_ref.shape
    row = lax.broadcasted_iota(jnp.int32, (size, width), 0)
    col = lax.broadcasted_iota(jnp.int32, (size, width), 1)
    for h in range(heads):
        if near_refs:
            near = near_refs[0][h]
            pair = jnp.concatenate(composed(near, far_ref[h], size), axis=1)
            near = near.astype(f32)
        else:
            near, pair = jnp.where(row == col, 1.0, 0.0), far_ref[h].astype(f32)
        out_ref[h] = jnp.where(place("seq", bit) == 1, pair, near).astype(bf16)


def before(bit, near, far):
    return vmem_call(
        functools.partial(before_body, bit),
        jax.ShapeDtypeStruct(far.shape, bf16),
        (far, *near),
        flops=2 * math.prod(far.shape) * far.shape[1],
        moved=6 * math.prod(far.shape),
    )


def entry_body(bit, near_ref, far_ref, own_ref, partner_ref, keep_ref, send_ref):
    heads, size, _ = near_ref.shape
    arrived, upper = place("seq", bit) == 1, place("seq", 1) == 1
    for h in range(heads):
        state = dot(near_ref[h, :, :size], far_ref[h])
        state = jnp.where(arrived, state, 0.0) + near_ref[h, :, size:].astype(f32)
        first = jnp.where(upper, partner_ref[h], own_ref[h])
        state = state.astype(bf16)
        later = dot(first[:, :size], state) + first[:, size:].astype(f32)
        later = later.astype(bf16)
        keep_ref[h] = jnp.where(upper, later, state)
        send_ref[h] = jnp.where(upper, state, later)


def entry_states(own, other):
    heads, size, width = own.shape
    bits = bits_of(lax.axis_size("seq"))
    partner = swapped(other, "seq", 1)
    total = join(1, own, partner, len(bits) == 2)
    near = ()
    assert len(bits) > 2
    for bit in bits[1:-1]:
        far = swapped(total, "seq", bit)
        total = join(bit, total, far, 2 * bit == bits[-1])
        near = (before(bit, near, far),)
    far = swapped(total, "seq", bits[-1])
    state = jax.ShapeDtypeStruct((heads, size, size), bf16)
    keep, send = vmem_call(
        functools.partial(entry_body, bits[-1]),
        (state, state),
        (*near, far, own, partner),
        flops=4 * heads * size * size * size,
        moved=14 * heads * size * size,
    )
    return keep, swapped(send, "seq", 1)


def back_body(places, *refs):
    own_refs, other_refs, refs = refs[:GROUPS], refs[GROUPS : 2 * GROUPS], refs[2 * GROUPS :]
    raised_ref, output_ref, gate_ref, gain_ref, weight_ref, keep_ref, *rest = refs
    normed = rest[-1]
    size = gain_ref.shape[1]
    slab_rows = keep_ref.shape[0]
    share = own_refs[0].shape[0]
    half = GROUPS * share
    upper = place("seq", 1) == 1
    for k, away in enumerate(places):
        rows = pl.ds(pl.multiple_of((place("head") ^ away) * slab_rows, 16), slab_rows)
        for h in range(raised_ref.shape[0]):
            lanes = slice(h * size, (h + 1) * size)
            group, at = divmod(h % half, share)
            own, other = own_refs[group][at], other_refs[group][at]
            state = jnp.where(upper, other, own) if h < half else jnp.where(upper, own, other)
            attended = dot(raised_ref[h, rows, :], state) + output_ref[rows, lanes]
            power = jnp.sum(attended * attended, -1, keepdims=True) * (1.0 / size)
            normed[k * slab_rows : (k + 1) * slab_rows, lanes] = (
                attended * lax.rsqrt(power + 1e-05) * gain_ref[...] * gate_ref[rows, lanes]
            ).astype(bf16)
    total = dot(normed[...], weight_ref[...])
    keep_ref[...] = total[:slab_rows]
    if len(rest) > 1:
        rest[0][...] = total[slab_rows:].astype(bf16)


def back(places, states, raised, output_rows, out_gate, gain, weight, slab_rows):
    slab_count, width = len(places), weight.shape[1]
    shapes = [jax.ShapeDtypeStruct((slab_rows, width), f32)]
    if slab_count > 1:
        shapes.append(jax.ShapeDtypeStruct((slab_rows, width), bf16))
    return vmem_call(
        functools.partial(back_body, places),
        shapes,
        (*states, raised, output_rows, out_gate, gain, weight),
        scratch=[pltpu.VMEM((slab_count * slab_rows, weight.shape[0]), bf16)],
        grant=10,
        flops=2 * slab_count * slab_rows * weight.shape[0] * width,
        moved=2 * weight.shape[0] * width,
    )


def shards(
    hidden_in,
    qkv_weight,
    conv_weight,
    decay_log,
    dt_bias,
    decay_down,
    decay_up,
    beta_weight,
    gate_down,
    gate_up,
    norm_gain,
    out_weight,
):
    heads, size = decay_log.shape[0], norm_gain.shape[0]
    channels = heads * size
    devices = lax.axis_size("head")
    weight = qkv_weight.transpose(1, 0, 2)
    fetched = load(hidden_in, decay_down, beta_weight.T, weight)
    slabs, rims, fetched = gathered(hidden_in, fetched)
    *pairs, solved, attend, start, rows = front(
        rims, slabs, fetched, (decay_log, decay_up, dt_bias[None], conv_weight), weight, size
    )
    count = start.shape[1]
    raised, output_rows, out_gate = vmem_call(
        rows_body,
        (
            jax.ShapeDtypeStruct((heads, count, size), bf16),
            jax.ShapeDtypeStruct((count, channels), f32),
            jax.ShapeDtypeStruct((count, channels), f32),
        ),
        (attend, solved, start, rows, gate_down, gate_up),
        grant=8,
        flops=2 * heads * count * count * 2 * size,
        moved=4 * heads * count * count,
    )
    states = [entry_states(*both) for both in zip(pairs[:GROUPS], pairs[GROUPS:])]
    states = [own for own, _ in states] + [other for _, other in states]
    slab_rows = count // devices
    sums = {}
    for g in reversed(range(max(devices // 2, 1))):
        places = [2 * g, 2 * g + 1][:devices]
        keep, *send = back(
            places, states, raised, output_rows, out_gate, norm_gain[None], out_weight, slab_rows
        )
        near = [swapped(part, "head", 1).astype(f32) for part in send]
        sums[g] = [lax.optimization_barrier(sum([keep] + near))]
    for bit in bits_of(devices)[1:]:
        for g in sorted(sums):
            if 2 * g & bit:
                arrived = swapped(sum(sums.pop(g)).astype(bf16), "head", bit)
                sums[g ^ bit // 2].append(arrived.astype(f32))
    return sum(sums[0]).astype(bf16)


def solution(mesh):
    return jax.shard_map(
        shards,
        mesh=mesh,
        in_specs=(
            P(("seq", "head"), None),
            P(None, None, "head"),
            P(None, None, "head"),
            P("head"),
            P("head"),
            P(),
            P(None, "head"),
            P(None, "head"),
            P(),
            P(None, "head"),
            P(),
            P("head", None),
        ),
        out_specs=P(("seq", "head"), None),
        check_vma=False,
    )
```

```python
import functools
import math

import jax
import jax.numpy as jnp
from jax import lax
from jax.experimental import pallas as pl
from jax.experimental.pallas import tpu as pltpu
from jax.sharding import PartitionSpec as P

RIM = 16
BASE = 16
GROUPS = 1
MIB = 1024 * 1024
f32 = jnp.float32
bf16 = jnp.bfloat16


def dot(left, right, contract=((1,), (0,))):
    return lax.dot_general(left, right, (contract, ((), ())), preferred_element_type=f32)


def swapped(block, axis, bit):
    return lax.ppermute(block, axis, [(i, i ^ bit) for i in range(lax.axis_size(axis))])


def bits_of(size):
    assert size & (size - 1) == 0
    return [1 << i for i in range(size.bit_length() - 1)]


def rim_route(target):
    heads, seqs = lax.axis_size("head"), lax.axis_size("seq")
    return [(s * heads + heads - 1, (s + 1) * heads + target) for s in range(seqs - 1)]


def pick_body(targets, *refs):
    *tail_refs, rim_ref = refs
    rim = jnp.zeros(tail_refs[0].shape, f32)
    above = jnp.zeros((rim_ref.shape[0] - rim.shape[0], rim.shape[1]), f32)
    for target, ref in zip(targets, tail_refs):
        rim = jnp.where(place("head") == target, ref[...].astype(f32), rim)
    rim_ref[...] = jnp.concatenate([above, rim], axis=0).astype(rim_ref.dtype)


def gathered(own, loaded):
    heads = lax.axis_size("head")
    bits = bits_of(heads)
    assert bits
    slabs = {0: own}
    for bit in reversed(bits[1:]):
        for k in sorted(slabs):
            slabs[k ^ bit] = swapped(slabs[k], "head", bit)
    tail = own[own.shape[0] - RIM // 2 :]
    targets = [first if first == heads - 2 else first + 1 for first in range(0, heads, 2)][::-1]
    tails = [lax.ppermute(tail, ("seq", "head"), rim_route(target)) for target in targets]
    slabs[1] = swapped(own, "head", 1)
    arrived = [k for k in sorted(slabs) if k > 1]
    moved, tails, loaded = lax.optimization_barrier(
        ([slabs[k] for k in arrived], tails, loaded)
    )
    for k, slab in zip(arrived, moved):
        slabs[k], slabs[k ^ 1] = slab, swapped(slab, "head", 1)
    rim = vmem_call(
        functools.partial(pick_body, targets), jax.ShapeDtypeStruct((RIM, own.shape[1]), bf16), tails
    )
    return [slabs[k] for k in range(1, heads)], [rim, swapped(rim, "head", 1)], loaded


def vmem_call(body, out_shape, args, scratch=(), hbm=0, grant=4, flops=0, moved=0):
    here = len(args) - hbm
    args = [pltpu.with_memory_space_constraint(a, pltpu.HBM) if i >= here else a for i, a in enumerate(args)]
    spaces = [pltpu.VMEM] * here + [pltpu.HBM] * hbm
    return pl.pallas_call(
        body,
        out_shape=out_shape,
        in_specs=[pl.BlockSpec(memory_space=space) for space in spaces],
        out_specs=jax.tree.map(lambda _: pl.BlockSpec(memory_space=pltpu.VMEM), out_shape),
        scratch_shapes=list(scratch),
        compiler_params=pltpu.CompilerParams(vmem_limit_bytes=grant * MIB),
        cost_estimate=pl.CostEstimate(flops=flops, bytes_accessed=moved, transcendentals=0),
    )(*args)


def place(axis, bit=None):
    here = lax.axis_index(axis)
    return here if bit is None else here // bit % 2


def column_pieces(width):
    step = math.gcd(width, 256)
    return [slice(i, i + step) for i in range(0, width, step)]


def load_body(
    hidden_ref, decay_down_ref, beta_ref, weight_ref, own_ref, weights, downs, betas, sems
):
    rank, heads = decay_down_ref.shape[1], beta_ref.shape[0]
    beta = pltpu.make_async_copy(beta_ref, betas, sems.at[0])
    copies = [
        pltpu.make_async_copy(hidden_ref, own_ref, sems.at[1]),
        pltpu.make_async_copy(decay_down_ref, downs.at[:, pl.ds(0, rank)], sems.at[2]),
    ]
    for c in range(2):
        copies.append(pltpu.make_async_copy(weight_ref.at[c], weights.at[c], sems.at[3 + c]))
    for copy in [beta] + copies:
        copy.start()
    beta.wait()
    below = jnp.zeros((rank - heads, betas.shape[1]), f32)
    wide = jnp.concatenate([betas[...].astype(f32), below], axis=0)
    downs[:, rank:] = wide.T.astype(bf16)
    for copy in copies:
        copy.wait()


def load(own, decay_down, beta, weight):
    width, rank = decay_down.shape
    return vmem_call(
        load_body,
        (
            jax.ShapeDtypeStruct(own.shape, bf16),
            jax.ShapeDtypeStruct((2, *weight.shape[1:]), bf16),
            jax.ShapeDtypeStruct((width, 2 * rank), bf16),
        ),
        (own, decay_down, beta, weight),
        scratch=[pltpu.VMEM(beta.shape, bf16), pltpu.SemaphoreType.DMA((5,))],
        hbm=4,
        grant=12,
    )


def front_body(slab_count, *refs):
    (one_ref, two_ref, *slab_refs), refs = refs[: slab_count + 1], refs[slab_count + 1 :]
    (own_rows_ref, weights, downs), refs = refs[:3], refs[3:]
    hbm_refs, refs = refs[:5], refs[5:]
    (own_refs, other_refs), refs = (refs[:GROUPS], refs[GROUPS : 2 * GROUPS]), refs[2 * GROUPS :]
    (solved_ref, attend_ref, start_ref, rows_ref), refs = refs[:4], refs[4:]
    loaded, refs = refs[:5], refs[5:]
    projected, running_ref, parts_ref, mixing, inverse, sides, sems = refs
    rates, decay_up_ref, bias_ref, conv_ref, value_weight = loaded
    weight_ref = hbm_refs[-1]
    heads, count, size = start_ref.shape
    slab_rows = count // slab_count
    tap_count = conv_ref.shape[1]
    rank = decay_up_ref.shape[0]
    chunk = math.gcd(count, 64)
    chunks = count // chunk
    block = math.gcd(count, 128)
    blocks = count // block
    here = place("head")

    def rows_of(k):
        return pl.ds(pl.multiple_of(RIM + (here ^ k) * slab_rows, 16), slab_rows)

    small = [pltpu.make_async_copy(hbm_refs[i], loaded[i], sems.at[i]) for i in range(4)]
    pieces = column_pieces(heads * size)
    streams = []
    for i, piece in enumerate(pieces):
        streams.append(
            pltpu.make_async_copy(
                weight_ref.at[2, :, piece], value_weight.at[:, piece], sems.at[4 + i]
            )
        )
    for copy in small + streams:
        copy.start()
    rows_ref[:RIM, :] = (one_ref[...].astype(f32) + two_ref[...].astype(f32)).astype(bf16)
    for k, ref in enumerate([own_rows_ref, *slab_refs]):
        rows_ref[rows_of(k), :] = ref[...]

    def project(c, piece, weight):
        result = dot(rows_ref[...], weight)
        for begin in range(piece.start, piece.stop, size):
            at = begin - piece.start
            projected[c * heads + begin // size] = result[:, at : at + size]

    pending = [(c, piece) for piece in pieces for c in range(2)]
    share = (pieces[0].stop - pieces[0].start) // size

    def project_next(number):
        for c, piece in pending[:number]:
            project(c, piece, weights[c, :, piece])
        del pending[:number]

    project_next(2)
    low = dot(rows_ref[RIM:, :], downs[...])
    strength = jax.nn.sigmoid(low[:, rank:])
    for copy in small:
        copy.wait()
    running_ref[...] = dot(low[:, :rank].astype(bf16), decay_up_ref[...])
    tiles = [slice(a * chunk, (a + 1) * chunk) for a in range(chunks)]
    for h in range(heads):
        lanes = slice(h * size, (h + 1) * size)
        rate = jnp.exp(jnp.full((1, size), rates[h], f32))
        for rows in tiles:
            raw = running_ref[rows, lanes] + bias_ref[:, lanes]
            softplus = jnp.maximum(raw, 0.0) + jnp.log(1.0 + jnp.exp(-jnp.abs(raw)))
            log_decay = -rate * softplus
            high = log_decay.astype(bf16)
            parts_ref[rows, lanes] = high
            rest = (log_decay - high.astype(f32)).astype(bf16)
            parts_ref[count + rows.start : count + rows.stop, lanes] = rest
    row = lax.broadcasted_iota(jnp.int32, (count, count), 0)
    col = lax.broadcasted_iota(jnp.int32, (count, count), 1)
    lower = jnp.where(row >= col, 1.0, 0.0).astype(bf16)
    running_ref[...] = dot(jnp.concatenate([lower, lower], axis=1), parts_ref[...])

    def convolved(c, rows, h):
        taps = conv_ref[c].astype(f32)[:, h * size : (h + 1) * size]
        total = None
        for i in range(tap_count):
            first = RIM - tap_count + 1 + i + rows.start
            term = projected[c * heads + h, pl.ds(first, chunk), :] * taps[i : i + 1]
            total = term if total is None else total + term
        half = 0.5 * total
        return half + half * jnp.tanh(half)

    for copy in streams:
        copy.wait()
    stops = []
    for h in range(heads):
        lanes = slice(h * size, (h + 1) * size)
        last = running_ref[count - 1 : count, lanes]
        middles, key_falls, stop, lefts = [], [], [], []
        for rows in tiles:
            running = running_ref[rows, lanes]
            middle = running[chunk // 2 : chunk // 2 + 1]
            above = running - middle
            rise, entry = jnp.exp(above), jnp.exp(middle)
            queries = convolved(0, rows, h)
            power = jnp.sum(queries * queries, -1, keepdims=True)
            queries = queries * (lax.rsqrt(power + 1e-06) * size ** (-0.5)) * rise
            start_ref[h, rows, :] = (queries * entry).astype(bf16)
            keys = convolved(1, rows, h)
            power = jnp.sum(keys * keys, -1, keepdims=True)
            keys = keys * lax.rsqrt(power + 1e-06)
            key_fall = keys * strength[rows, h : h + 1] * jnp.exp(-above)
            keys = keys * rise
            sides[h, rows, :size] = (keys * entry).astype(bf16)
            stop.append((key_fall * jnp.exp(last - middle)).astype(bf16))
            middles.append(middle)
            key_falls.append(key_fall)
            lefts.append(jnp.concatenate([keys.astype(bf16), queries.astype(bf16)], axis=0))
        stops.append((jnp.concatenate(stop, axis=0), jnp.exp(last)))
        project_next(pl.cdiv(2, share))
        for a in range(chunks):
            rows = tiles[a]
            reach = (a * chunk // block + 1) * block
            falls = []
            for b in range(reach // chunk):
                if b < a:
                    falls.append(key_falls[b] * jnp.exp(middles[a] - middles[b]))
                elif b == a:
                    falls.append(key_falls[b])
                else:
                    falls.append(jnp.zeros((chunk, size), f32))
            right = jnp.concatenate(falls, axis=0).astype(bf16)
            scores = dot(lefts[a], right, ((1,), (1,)))
            inside = slice(reach - block, reach)
            if reach > block:
                before = slice(0, reach - block)
                mixing[h, rows, before] = scores[:chunk, before].astype(bf16)
                attend_ref[h, rows, before] = scores[chunk:, before].astype(bf16)
            at, to = row[rows, inside], col[rows, inside]
            mixing[h, rows, inside] = jnp.where(at > to, scores[:chunk, inside], 0.0).astype(bf16)
            attend_ref[h, rows, inside] = jnp.where(
                at >= to, scores[chunk:, inside], 0.0
            ).astype(bf16)

    def value_side(h):
        for rows in tiles:
            sides[h, rows, size:] = convolved(2, rows, h).astype(bf16)

    between = [functools.partial(project, 2, p, value_weight[:, p]) for p in pieces]
    between += [functools.partial(value_side, h) for h in range(heads)]

    at, to = row[:block, :block], col[:block, :block]
    eye = jnp.where(at == to, 1.0, 0.0).astype(bf16)
    base = math.gcd(block, BASE)
    near = jnp.where(at // base == to // base, -1.0, 0.0).astype(bf16)
    corners = [(h, slice(d * block, (d + 1) * block)) for h in range(heads) for d in range(blocks)]
    powers = [mixing[h, d, d] * near for h, d in corners]
    totals = [power + eye for power in powers]
    steps = (base - 1).bit_length() - 1
    if steps:
        powers = [dot(power, power).astype(bf16) for power in powers]
    for step in range(steps):
        for n in range(len(corners)):
            power, total = powers[n], totals[n]
            if step < steps - 1:
                both = dot(jnp.concatenate([power, total], axis=0), power)
                powers[n], more = both[:block].astype(bf16), both[block:]
            else:
                more = dot(total, power)
            totals[n] = (total.astype(f32) + more).astype(bf16)
        if between:
            between.pop(0)()
    for (h, d), total in zip(corners, totals):
        inverse[h, d, :] = total
    width = base
    while width < block:
        odd = range(width, block, 2 * width)
        pair_mask = (at // width % 2 == 1) & (to // width == at // width - 1)
        pair_mask = jnp.where(pair_mask, 1.0, 0.0).astype(bf16)
        halves = []
        for h, d in corners:
            parts = [inverse[h, d.start + i : d.start + i + width, :] for i in odd]
            chosen = jnp.concatenate(parts, axis=0)
            halves.append((chosen, dot(chosen, mixing[h, d, d] * pair_mask).astype(bf16)))
        for (h, d), (chosen, half) in zip(corners, halves):
            new = (chosen.astype(f32) - dot(half, inverse[h, d, :])).astype(bf16)
            for n, i in enumerate(odd):
                inverse[h, d.start + i : d.start + i + width, :] = new[n * width : (n + 1) * width]
        if between:
            between.pop(0)()
        width *= 2
    for work in between:
        work()

    for d in range(blocks):
        rows = slice(d * block, (d + 1) * block)
        for h in range(heads):
            side = sides[h, rows, :]
            if d:
                done = solved_ref[h, : d * block, :]
                side = (side.astype(f32) - dot(mixing[h, rows, : d * block], done)).astype(bf16)
            solved_ref[h, rows, :] = dot(inverse[h, rows, :], side).astype(bf16)
    pairs = []
    unit = row[:size, :size] == col[:size, :size]
    for h in range(heads):
        stop, fade = stops[h]
        moved = dot(stop, solved_ref[h], ((0,), (0,)))
        diagonal = jnp.where(unit, jnp.broadcast_to(fade, (size, size)), 0.0)
        pairs.append(jnp.concatenate([diagonal - moved[:, :size], moved[:, size:]], axis=1))
    upper = place("seq", 1) == 1
    for h in range(heads // 2):
        low, high = pairs[h], pairs[heads // 2 + h]
        group, at = divmod(h, own_refs[0].shape[0])
        own_refs[group][at] = jnp.where(upper, high, low).astype(bf16)
        other_refs[group][at] = jnp.where(upper, low, high).astype(bf16)


def front(rims, slabs, fetched, loaded, weight, size):
    slab_count, slab_rows = 1 + len(slabs), slabs[0].shape[0]
    count = slab_count * slab_rows
    _, width, channels = weight.shape
    heads, block = channels // size, math.gcd(count, 128)
    buffers = [pltpu.SMEM(loaded[0].shape, f32)]
    buffers += [pltpu.VMEM(part.shape, part.dtype) for part in loaded[1:]]
    return vmem_call(
        functools.partial(front_body, slab_count),
        (
            *[jax.ShapeDtypeStruct((heads // 2 // GROUPS, size, 2 * size), bf16)] * (2 * GROUPS),
            jax.ShapeDtypeStruct((heads, count, 2 * size), bf16),
            jax.ShapeDtypeStruct((heads, count, count), bf16),
            jax.ShapeDtypeStruct((heads, count, size), bf16),
            jax.ShapeDtypeStruct((RIM + count, width), bf16),
        ),
        (*rims, *slabs, *fetched, *loaded, weight),
        scratch=[
            *buffers,
            pltpu.VMEM((width, channels), bf16),
            pltpu.VMEM((3 * heads, RIM + count, size), f32),
            pltpu.VMEM((count, channels), f32),
            pltpu.VMEM((2 * count, channels), bf16),
            pltpu.VMEM((heads, count, count), bf16),
            pltpu.VMEM((heads, count, block), bf16),
            pltpu.VMEM((heads, count, 2 * size), bf16),
            pltpu.SemaphoreType.DMA((4 + len(column_pieces(channels)),)),
        ],
        hbm=1 + len(loaded),
        grant=24,
        flops=2 * count * width * channels * 4,
        moved=2 * 4 * width * channels,
    )


def rows_body(
    attend_ref, solved_ref, start_ref, rows_ref, down_ref, up_ref, raised_ref, output_ref, gate_ref
):
    heads, _, size = start_ref.shape
    low = dot(rows_ref[RIM:, :], down_ref[...]).astype(bf16)
    gate_ref[...] = jax.nn.sigmoid(dot(low, up_ref[...]))
    count = attend_ref.shape[1]
    block = math.gcd(count, 128)
    for h in range(heads):
        for begin in range(0, count, block):
            rows, reach = slice(begin, begin + block), slice(0, begin + block)
            both = dot(attend_ref[h, rows, reach], solved_ref[h, reach, :])
            raised_ref[h, rows, :] = (start_ref[h, rows, :].astype(f32) - both[:, :size]).astype(bf16)
            output_ref[rows, h * size : (h + 1) * size] = both[:, size:]


def composed(later, first, size):
    both = dot(later[:, :size], first)
    return both[:, :size], both[:, size:] + later[:, size:].astype(f32)


def put(ref, h, pair):
    size = ref.shape[1]
    if ref.shape[2] > size:
        ref[h, :, :size] = pair[0].astype(bf16)
    ref[h, :, ref.shape[2] - size :] = pair[1].astype(bf16)


def join_body(bit, own_ref, far_ref, total_ref):
    heads, size, _ = own_ref.shape
    for h in range(heads):
        own, far = own_ref[h], far_ref[h]
        upper = place("seq", bit) == 1
        later, first = jnp.where(upper, own, far), jnp.where(upper, far, own)
        put(total_ref, h, composed(later, first, size))


def join(bit, own, far, last):
    heads, size, width = own.shape
    return vmem_call(
        functools.partial(join_body, bit),
        jax.ShapeDtypeStruct((heads, size, size if last else width), bf16),
        (own, far),
        flops=2 * heads * size * size * width,
        moved=6 * heads * size * width,
    )


def before_body(bit, far_ref, *refs):
    *near_refs, out_ref = refs
    heads, size, width = far_ref.shape
    row = lax.broadcasted_iota(jnp.int32, (size, width), 0)
    col = lax.broadcasted_iota(jnp.int32, (size, width), 1)
    for h in range(heads):
        if near_refs:
            near = near_refs[0][h]
            pair = jnp.concatenate(composed(near, far_ref[h], size), axis=1)
            near = near.astype(f32)
        else:
            near, pair = jnp.where(row == col, 1.0, 0.0), far_ref[h].astype(f32)
        out_ref[h] = jnp.where(place("seq", bit) == 1, pair, near).astype(bf16)


def before(bit, near, far):
    return vmem_call(
        functools.partial(before_body, bit),
        jax.ShapeDtypeStruct(far.shape, bf16),
        (far, *near),
        flops=2 * math.prod(far.shape) * far.shape[1],
        moved=6 * math.prod(far.shape),
    )


def entry_body(bit, near_ref, far_ref, own_ref, partner_ref, keep_ref, send_ref):
    heads, size, _ = near_ref.shape
    arrived, upper = place("seq", bit) == 1, place("seq", 1) == 1
    for h in range(heads):
        state = dot(near_ref[h, :, :size], far_ref[h])
        state = jnp.where(arrived, state, 0.0) + near_ref[h, :, size:].astype(f32)
        first = jnp.where(upper, partner_ref[h], own_ref[h])
        state = state.astype(bf16)
        later = dot(first[:, :size], state) + first[:, size:].astype(f32)
        later = later.astype(bf16)
        keep_ref[h] = jnp.where(upper, later, state)
        send_ref[h] = jnp.where(upper, state, later)


def entry_states(own, other):
    heads, size, width = own.shape
    bits = bits_of(lax.axis_size("seq"))
    partner = swapped(other, "seq", 1)
    total = join(1, own, partner, len(bits) == 2)
    near = ()
    assert len(bits) > 2
    for bit in bits[1:-1]:
        far = swapped(total, "seq", bit)
        total = join(bit, total, far, 2 * bit == bits[-1])
        near = (before(bit, near, far),)
    far = swapped(total, "seq", bits[-1])
    state = jax.ShapeDtypeStruct((heads, size, size), bf16)
    keep, send = vmem_call(
        functools.partial(entry_body, bits[-1]),
        (state, state),
        (*near, far, own, partner),
        flops=4 * heads * size * size * size,
        moved=14 * heads * size * size,
    )
    return keep, swapped(send, "seq", 1)


def back_body(places, *refs):
    own_refs, other_refs, refs = refs[:GROUPS], refs[GROUPS : 2 * GROUPS], refs[2 * GROUPS :]
    raised_ref, output_ref, gate_ref, gain_ref, weight_ref, keep_ref, *rest = refs
    normed = rest[-1]
    size = gain_ref.shape[1]
    slab_rows = keep_ref.shape[0]
    share = own_refs[0].shape[0]
    half = GROUPS * share
    upper = place("seq", 1) == 1
    for k, away in enumerate(places):
        rows = pl.ds(pl.multiple_of((place("head") ^ away) * slab_rows, 16), slab_rows)
        for h in range(raised_ref.shape[0]):
            lanes = slice(h * size, (h + 1) * size)
            group, at = divmod(h % half, share)
            own, other = own_refs[group][at], other_refs[group][at]
            state = jnp.where(upper, other, own) if h < half else jnp.where(upper, own, other)
            attended = dot(raised_ref[h, rows, :], state) + output_ref[rows, lanes]
            power = jnp.sum(attended * attended, -1, keepdims=True) * (1.0 / size)
            normed[k * slab_rows : (k + 1) * slab_rows, lanes] = (
                attended * lax.rsqrt(power + 1e-05) * gain_ref[...] * gate_ref[rows, lanes]
            ).astype(bf16)
    total = dot(normed[...], weight_ref[...])
    keep_ref[...] = total[:slab_rows]
    if len(rest) > 1:
        rest[0][...] = total[slab_rows:].astype(bf16)


def back(places, states, raised, output_rows, out_gate, gain, weight, slab_rows):
    slab_count, width = len(places), weight.shape[1]
    shapes = [jax.ShapeDtypeStruct((slab_rows, width), f32)]
    if slab_count > 1:
        shapes.append(jax.ShapeDtypeStruct((slab_rows, width), bf16))
    return vmem_call(
        functools.partial(back_body, places),
        shapes,
        (*states, raised, output_rows, out_gate, gain, weight),
        scratch=[pltpu.VMEM((slab_count * slab_rows, weight.shape[0]), bf16)],
        grant=10,
        flops=2 * slab_count * slab_rows * weight.shape[0] * width,
        moved=2 * weight.shape[0] * width,
    )


def shards(
    hidden_in,
    qkv_weight,
    conv_weight,
    decay_log,
    dt_bias,
    decay_down,
    decay_up,
    beta_weight,
    gate_down,
    gate_up,
    norm_gain,
    out_weight,
):
    heads, size = decay_log.shape[0], norm_gain.shape[0]
    channels = heads * size
    devices = lax.axis_size("head")
    weight = qkv_weight.transpose(1, 0, 2)
    fetched = load(hidden_in, decay_down, beta_weight.T, weight)
    slabs, rims, fetched = gathered(hidden_in, fetched)
    *pairs, solved, attend, start, rows = front(
        rims, slabs, fetched, (decay_log, decay_up, dt_bias[None], conv_weight), weight, size
    )
    count = start.shape[1]
    raised, output_rows, out_gate = vmem_call(
        rows_body,
        (
            jax.ShapeDtypeStruct((heads, count, size), bf16),
            jax.ShapeDtypeStruct((count, channels), f32),
            jax.ShapeDtypeStruct((count, channels), f32),
        ),
        (attend, solved, start, rows, gate_down, gate_up),
        grant=8,
        flops=2 * heads * count * count * 2 * size,
        moved=4 * heads * count * count,
    )
    states = [entry_states(*both) for both in zip(pairs[:GROUPS], pairs[GROUPS:])]
    states = [own for own, _ in states] + [other for _, other in states]
    slab_rows = count // devices
    sums = {}
    for g in reversed(range(max(devices // 2, 1))):
        places = [2 * g, 2 * g + 1][:devices]
        keep, *send = back(
            places, states, raised, output_rows, out_gate, norm_gain[None], out_weight, slab_rows
        )
        near = [swapped(part, "head", 1).astype(f32) for part in send]
        sums[g] = [lax.optimization_barrier(sum([keep] + near))]
    for bit in bits_of(devices)[1:]:
        for g in sorted(sums):
            if 2 * g & bit:
                arrived = swapped(sum(sums.pop(g)).astype(bf16), "head", bit)
                sums[g ^ bit // 2].append(arrived.astype(f32))
    return sum(sums[0]).astype(bf16)


def solution(mesh):
    return jax.shard_map(
        shards,
        mesh=mesh,
        in_specs=(
            P(("seq", "head"), None),
            P(None, None, "head"),
            P(None, None, "head"),
            P("head"),
            P("head"),
            P(),
            P(None, "head"),
            P(None, "head"),
            P(),
            P(None, "head"),
            P(),
            P("head", None),
        ),
        out_specs=P(("seq", "head"), None),
        check_vma=False,
    )
```

```python
import functools
import math

import jax
import jax.numpy as jnp
from jax import lax
from jax.experimental import pallas as pl
from jax.experimental.pallas import tpu as pltpu
from jax.sharding import PartitionSpec as P

RIM = 16
BASE = 16
GROUPS = 1
MIB = 1024 * 1024
f32 = jnp.float32
bf16 = jnp.bfloat16


def dot(left, right, contract=((1,), (0,))):
    return lax.dot_general(left, right, (contract, ((), ())), preferred_element_type=f32)


def swapped(block, axis, bit):
    return lax.ppermute(block, axis, [(i, i ^ bit) for i in range(lax.axis_size(axis))])


def bits_of(size):
    assert size & (size - 1) == 0
    return [1 << i for i in range(size.bit_length() - 1)]


def rim_route(target):
    heads, seqs = lax.axis_size("head"), lax.axis_size("seq")
    return [(s * heads + heads - 1, (s + 1) * heads + target) for s in range(seqs - 1)]


def pick_body(targets, *refs):
    *tail_refs, rim_ref = refs
    rim = jnp.zeros(tail_refs[0].shape, f32)
    above = jnp.zeros((rim_ref.shape[0] - rim.shape[0], rim.shape[1]), f32)
    for target, ref in zip(targets, tail_refs):
        rim = jnp.where(place("head") == target, ref[...].astype(f32), rim)
    rim_ref[...] = jnp.concatenate([above, rim], axis=0).astype(rim_ref.dtype)


def gathered(own, loaded):
    heads = lax.axis_size("head")
    bits = bits_of(heads)
    assert bits
    slabs = {0: own}
    for bit in reversed(bits[1:]):
        for k in sorted(slabs):
            slabs[k ^ bit] = swapped(slabs[k], "head", bit)
    tail = own[own.shape[0] - RIM // 2 :]
    targets = [first if first == heads - 2 else first + 1 for first in range(0, heads, 2)][::-1]
    tails = [lax.ppermute(tail, ("seq", "head"), rim_route(target)) for target in targets]
    slabs[1] = swapped(own, "head", 1)
    arrived = [k for k in sorted(slabs) if k > 1]
    moved, tails, loaded = lax.optimization_barrier(
        ([slabs[k] for k in arrived], tails, loaded)
    )
    for k, slab in zip(arrived, moved):
        slabs[k], slabs[k ^ 1] = slab, swapped(slab, "head", 1)
    rim = vmem_call(
        functools.partial(pick_body, targets), jax.ShapeDtypeStruct((RIM, own.shape[1]), bf16), tails
    )
    return [slabs[k] for k in range(1, heads)], [rim, swapped(rim, "head", 1)], loaded


def vmem_call(body, out_shape, args, scratch=(), hbm=0, grant=4, flops=0, moved=0):
    here = len(args) - hbm
    args = [pltpu.with_memory_space_constraint(a, pltpu.HBM) if i >= here else a for i, a in enumerate(args)]
    spaces = [pltpu.VMEM] * here + [pltpu.HBM] * hbm
    return pl.pallas_call(
        body,
        out_shape=out_shape,
        in_specs=[pl.BlockSpec(memory_space=space) for space in spaces],
        out_specs=jax.tree.map(lambda _: pl.BlockSpec(memory_space=pltpu.VMEM), out_shape),
        scratch_shapes=list(scratch),
        compiler_params=pltpu.CompilerParams(vmem_limit_bytes=grant * MIB),
        cost_estimate=pl.CostEstimate(flops=flops, bytes_accessed=moved, transcendentals=0),
    )(*args)


def place(axis, bit=None):
    here = lax.axis_index(axis)
    return here if bit is None else here // bit % 2


def column_pieces(width):
    step = math.gcd(width, 512)
    return [slice(i, i + step) for i in range(0, width, step)]


def load_body(
    hidden_ref, decay_down_ref, beta_ref, weight_ref, own_ref, weights, downs, betas, sems
):
    rank, heads = decay_down_ref.shape[1], beta_ref.shape[0]
    beta = pltpu.make_async_copy(beta_ref, betas, sems.at[0])
    copies = [
        pltpu.make_async_copy(hidden_ref, own_ref, sems.at[1]),
        pltpu.make_async_copy(decay_down_ref, downs.at[:, pl.ds(0, rank)], sems.at[2]),
    ]
    for c in range(2):
        copies.append(pltpu.make_async_copy(weight_ref.at[c], weights.at[c], sems.at[3 + c]))
    for copy in [beta] + copies:
        copy.start()
    beta.wait()
    below = jnp.zeros((rank - heads, betas.shape[1]), f32)
    wide = jnp.concatenate([betas[...].astype(f32), below], axis=0)
    downs[:, rank:] = wide.T.astype(bf16)
    for copy in copies:
        copy.wait()


def load(own, decay_down, beta, weight):
    width, rank = decay_down.shape
    return vmem_call(
        load_body,
        (
            jax.ShapeDtypeStruct(own.shape, bf16),
            jax.ShapeDtypeStruct((2, *weight.shape[1:]), bf16),
            jax.ShapeDtypeStruct((width, 2 * rank), bf16),
        ),
        (own, decay_down, beta, weight),
        scratch=[pltpu.VMEM(beta.shape, bf16), pltpu.SemaphoreType.DMA((5,))],
        hbm=4,
        grant=12,
    )


def front_body(slab_count, *refs):
    (one_ref, two_ref, *slab_refs), refs = refs[: slab_count + 1], refs[slab_count + 1 :]
    (own_rows_ref, weights, downs), refs = refs[:3], refs[3:]
    hbm_refs, refs = refs[:5], refs[5:]
    (own_refs, other_refs), refs = (refs[:GROUPS], refs[GROUPS : 2 * GROUPS]), refs[2 * GROUPS :]
    (solved_ref, attend_ref, start_ref, rows_ref), refs = refs[:4], refs[4:]
    loaded, refs = refs[:5], refs[5:]
    projected, running_ref, parts_ref, mixing, inverse, sides, sems = refs
    rates, decay_up_ref, bias_ref, conv_ref, value_weight = loaded
    weight_ref = hbm_refs[-1]
    heads, count, size = start_ref.shape
    slab_rows = count // slab_count
    tap_count = conv_ref.shape[1]
    rank = decay_up_ref.shape[0]
    chunk = math.gcd(count, 64)
    chunks = count // chunk
    block = math.gcd(count, 128)
    blocks = count // block
    here = place("head")

    def rows_of(k):
        return pl.ds(pl.multiple_of(RIM + (here ^ k) * slab_rows, 16), slab_rows)

    small = [pltpu.make_async_copy(hbm_refs[i], loaded[i], sems.at[i]) for i in range(4)]
    pieces = column_pieces(heads * size)
    streams = []
    for i, piece in enumerate(pieces):
        streams.append(
            pltpu.make_async_copy(
                weight_ref.at[2, :, piece], value_weight.at[:, piece], sems.at[4 + i]
            )
        )
    for copy in small + streams:
        copy.start()
    rows_ref[:RIM, :] = (one_ref[...].astype(f32) + two_ref[...].astype(f32)).astype(bf16)
    for k, ref in enumerate([own_rows_ref, *slab_refs]):
        rows_ref[rows_of(k), :] = ref[...]

    def project(c, piece, weight):
        result = dot(rows_ref[...], weight)
        for begin in range(piece.start, piece.stop, size):
            at = begin - piece.start
            projected[c * heads + begin // size] = result[:, at : at + size]

    pending = [(c, piece) for piece in pieces for c in range(2)]
    share = (pieces[0].stop - pieces[0].start) // size

    def project_next(number):
        for c, piece in pending[:number]:
            project(c, piece, weights[c, :, piece])
        del pending[:number]

    project_next(2)
    low = dot(rows_ref[RIM:, :], downs[...])
    strength = jax.nn.sigmoid(low[:, rank:])
    for copy in small:
        copy.wait()
    running_ref[...] = dot(low[:, :rank].astype(bf16), decay_up_ref[...])
    tiles = [slice(a * chunk, (a + 1) * chunk) for a in range(chunks)]
    for h in range(heads):
        lanes = slice(h * size, (h + 1) * size)
        rate = jnp.exp(jnp.full((1, size), rates[h], f32))
        for rows in tiles:
            raw = running_ref[rows, lanes] + bias_ref[:, lanes]
            softplus = jnp.maximum(raw, 0.0) + jnp.log(1.0 + jnp.exp(-jnp.abs(raw)))
            log_decay = -rate * softplus
            high = log_decay.astype(bf16)
            parts_ref[rows, lanes] = high
            rest = (log_decay - high.astype(f32)).astype(bf16)
            parts_ref[count + rows.start : count + rows.stop, lanes] = rest
    row = lax.broadcasted_iota(jnp.int32, (count, count), 0)
    col = lax.broadcasted_iota(jnp.int32, (count, count), 1)
    lower = jnp.where(row >= col, 1.0, 0.0).astype(bf16)
    running_ref[...] = dot(jnp.concatenate([lower, lower], axis=1), parts_ref[...])

    def convolved(c, rows, h):
        taps = conv_ref[c].astype(f32)[:, h * size : (h + 1) * size]
        total = None
        for i in range(tap_count):
            first = RIM - tap_count + 1 + i + rows.start
            term = projected[c * heads + h, pl.ds(first, chunk), :] * taps[i : i + 1]
            total = term if total is None else total + term
        half = 0.5 * total
        return half + half * jnp.tanh(half)

    for copy in streams:
        copy.wait()
    stops = []
    for h in range(heads):
        lanes = slice(h * size, (h + 1) * size)
        last = running_ref[count - 1 : count, lanes]
        middles, key_falls, stop, lefts = [], [], [], []
        for rows in tiles:
            running = running_ref[rows, lanes]
            middle = running[chunk // 2 : chunk // 2 + 1]
            above = running - middle
            rise, entry = jnp.exp(above), jnp.exp(middle)
            queries = convolved(0, rows, h)
            power = jnp.sum(queries * queries, -1, keepdims=True)
            queries = queries * (lax.rsqrt(power + 1e-06) * size ** (-0.5)) * rise
            start_ref[h, rows, :] = (queries * entry).astype(bf16)
            keys = convolved(1, rows, h)
            power = jnp.sum(keys * keys, -1, keepdims=True)
            keys = keys * lax.rsqrt(power + 1e-06)
            key_fall = keys * strength[rows, h : h + 1] * jnp.exp(-above)
            keys = keys * rise
            sides[h, rows, :size] = (keys * entry).astype(bf16)
            stop.append((key_fall * jnp.exp(last - middle)).astype(bf16))
            middles.append(middle)
            key_falls.append(key_fall)
            lefts.append(jnp.concatenate([keys.astype(bf16), queries.astype(bf16)], axis=0))
        stops.append((jnp.concatenate(stop, axis=0), jnp.exp(last)))
        project_next(pl.cdiv(2, share))
        for a in range(chunks):
            rows = tiles[a]
            reach = (a * chunk // block + 1) * block
            falls = []
            for b in range(reach // chunk):
                if b < a:
                    falls.append(key_falls[b] * jnp.exp(middles[a] - middles[b]))
                elif b == a:
                    falls.append(key_falls[b])
                else:
                    falls.append(jnp.zeros((chunk, size), f32))
            right = jnp.concatenate(falls, axis=0).astype(bf16)
            scores = dot(lefts[a], right, ((1,), (1,)))
            inside = slice(reach - block, reach)
            if reach > block:
                before = slice(0, reach - block)
                mixing[h, rows, before] = scores[:chunk, before].astype(bf16)
                attend_ref[h, rows, before] = scores[chunk:, before].astype(bf16)
            at, to = row[rows, inside], col[rows, inside]
            mixing[h, rows, inside] = jnp.where(at > to, scores[:chunk, inside], 0.0).astype(bf16)
            attend_ref[h, rows, inside] = jnp.where(
                at >= to, scores[chunk:, inside], 0.0
            ).astype(bf16)

    def value_side(h):
        for rows in tiles:
            sides[h, rows, size:] = convolved(2, rows, h).astype(bf16)

    between = [functools.partial(project, 2, p, value_weight[:, p]) for p in pieces]
    between += [functools.partial(value_side, h) for h in range(heads)]

    at, to = row[:block, :block], col[:block, :block]
    eye = jnp.where(at == to, 1.0, 0.0).astype(bf16)
    base = math.gcd(block, BASE)
    near = jnp.where(at // base == to // base, -1.0, 0.0).astype(bf16)
    corners = [(h, slice(d * block, (d + 1) * block)) for h in range(heads) for d in range(blocks)]
    powers = [mixing[h, d, d] * near for h, d in corners]
    totals = [power + eye for power in powers]
    steps = (base - 1).bit_length() - 1
    if steps:
        powers = [dot(power, power).astype(bf16) for power in powers]
    for step in range(steps):
        for n in range(len(corners)):
            power, total = powers[n], totals[n]
            if step < steps - 1:
                both = dot(jnp.concatenate([power, total], axis=0), power)
                powers[n], more = both[:block].astype(bf16), both[block:]
            else:
                more = dot(total, power)
            totals[n] = (total.astype(f32) + more).astype(bf16)
        if between:
            between.pop(0)()
    for (h, d), total in zip(corners, totals):
        inverse[h, d, :] = total
    width = base
    while width < block:
        odd = range(width, block, 2 * width)
        pair_mask = (at // width % 2 == 1) & (to // width == at // width - 1)
        pair_mask = jnp.where(pair_mask, 1.0, 0.0).astype(bf16)
        halves = []
        for h, d in corners:
            parts = [inverse[h, d.start + i : d.start + i + width, :] for i in odd]
            chosen = jnp.concatenate(parts, axis=0)
            halves.append((chosen, dot(chosen, mixing[h, d, d] * pair_mask).astype(bf16)))
        for (h, d), (chosen, half) in zip(corners, halves):
            new = (chosen.astype(f32) - dot(half, inverse[h, d, :])).astype(bf16)
            for n, i in enumerate(odd):
                inverse[h, d.start + i : d.start + i + width, :] = new[n * width : (n + 1) * width]
        if between:
            between.pop(0)()
        width *= 2
    for work in between:
        work()

    for d in range(blocks):
        rows = slice(d * block, (d + 1) * block)
        for h in range(heads):
            side = sides[h, rows, :]
            if d:
                done = solved_ref[h, : d * block, :]
                side = (side.astype(f32) - dot(mixing[h, rows, : d * block], done)).astype(bf16)
            solved_ref[h, rows, :] = dot(inverse[h, rows, :], side).astype(bf16)
    pairs = []
    unit = row[:size, :size] == col[:size, :size]
    for h in range(heads):
        stop, fade = stops[h]
        moved = dot(stop, solved_ref[h], ((0,), (0,)))
        diagonal = jnp.where(unit, jnp.broadcast_to(fade, (size, size)), 0.0)
        pairs.append(jnp.concatenate([diagonal - moved[:, :size], moved[:, size:]], axis=1))
    upper = place("seq", 1) == 1
    for h in range(heads // 2):
        low, high = pairs[h], pairs[heads // 2 + h]
        group, at = divmod(h, own_refs[0].shape[0])
        own_refs[group][at] = jnp.where(upper, high, low).astype(bf16)
        other_refs[group][at] = jnp.where(upper, low, high).astype(bf16)


def front(rims, slabs, fetched, loaded, weight, size):
    slab_count, slab_rows = 1 + len(slabs), slabs[0].shape[0]
    count = slab_count * slab_rows
    _, width, channels = weight.shape
    heads, block = channels // size, math.gcd(count, 128)
    buffers = [pltpu.SMEM(loaded[0].shape, f32)]
    buffers += [pltpu.VMEM(part.shape, part.dtype) for part in loaded[1:]]
    return vmem_call(
        functools.partial(front_body, slab_count),
        (
            *[jax.ShapeDtypeStruct((heads // 2 // GROUPS, size, 2 * size), bf16)] * (2 * GROUPS),
            jax.ShapeDtypeStruct((heads, count, 2 * size), bf16),
            jax.ShapeDtypeStruct((heads, count, count), bf16),
            jax.ShapeDtypeStruct((heads, count, size), bf16),
            jax.ShapeDtypeStruct((RIM + count, width), bf16),
        ),
        (*rims, *slabs, *fetched, *loaded, weight),
        scratch=[
            *buffers,
            pltpu.VMEM((width, channels), bf16),
            pltpu.VMEM((3 * heads, RIM + count, size), f32),
            pltpu.VMEM((count, channels), f32),
            pltpu.VMEM((2 * count, channels), bf16),
            pltpu.VMEM((heads, count, count), bf16),
            pltpu.VMEM((heads, count, block), bf16),
            pltpu.VMEM((heads, count, 2 * size), bf16),
            pltpu.SemaphoreType.DMA((4 + len(column_pieces(channels)),)),
        ],
        hbm=1 + len(loaded),
        grant=24,
        flops=2 * count * width * channels * 4,
        moved=2 * 4 * width * channels,
    )


def rows_body(
    attend_ref, solved_ref, start_ref, rows_ref, down_ref, up_ref, raised_ref, output_ref, gate_ref
):
    heads, _, size = start_ref.shape
    low = dot(rows_ref[RIM:, :], down_ref[...]).astype(bf16)
    gate_ref[...] = jax.nn.sigmoid(dot(low, up_ref[...]))
    count = attend_ref.shape[1]
    block = math.gcd(count, 128)
    for h in range(heads):
        for begin in range(0, count, block):
            rows, reach = slice(begin, begin + block), slice(0, begin + block)
            both = dot(attend_ref[h, rows, reach], solved_ref[h, reach, :])
            raised_ref[h, rows, :] = (start_ref[h, rows, :].astype(f32) - both[:, :size]).astype(bf16)
            output_ref[rows, h * size : (h + 1) * size] = both[:, size:]


def composed(later, first, size):
    both = dot(later[:, :size], first)
    return both[:, :size], both[:, size:] + later[:, size:].astype(f32)


def put(ref, h, pair):
    size = ref.shape[1]
    if ref.shape[2] > size:
        ref[h, :, :size] = pair[0].astype(bf16)
    ref[h, :, ref.shape[2] - size :] = pair[1].astype(bf16)


def join_body(bit, own_ref, far_ref, total_ref):
    heads, size, _ = own_ref.shape
    for h in range(heads):
        own, far = own_ref[h], far_ref[h]
        upper = place("seq", bit) == 1
        later, first = jnp.where(upper, own, far), jnp.where(upper, far, own)
        put(total_ref, h, composed(later, first, size))


def join(bit, own, far, last):
    heads, size, width = own.shape
    return vmem_call(
        functools.partial(join_body, bit),
        jax.ShapeDtypeStruct((heads, size, size if last else width), bf16),
        (own, far),
        flops=2 * heads * size * size * width,
        moved=6 * heads * size * width,
    )


def before_body(bit, far_ref, *refs):
    *near_refs, out_ref = refs
    heads, size, width = far_ref.shape
    row = lax.broadcasted_iota(jnp.int32, (size, width), 0)
    col = lax.broadcasted_iota(jnp.int32, (size, width), 1)
    for h in range(heads):
        if near_refs:
            near = near_refs[0][h]
            pair = jnp.concatenate(composed(near, far_ref[h], size), axis=1)
            near = near.astype(f32)
        else:
            near, pair = jnp.where(row == col, 1.0, 0.0), far_ref[h].astype(f32)
        out_ref[h] = jnp.where(place("seq", bit) == 1, pair, near).astype(bf16)


def before(bit, near, far):
    return vmem_call(
        functools.partial(before_body, bit),
        jax.ShapeDtypeStruct(far.shape, bf16),
        (far, *near),
        flops=2 * math.prod(far.shape) * far.shape[1],
        moved=6 * math.prod(far.shape),
    )


def entry_body(bit, near_ref, far_ref, own_ref, partner_ref, keep_ref, send_ref):
    heads, size, _ = near_ref.shape
    arrived, upper = place("seq", bit) == 1, place("seq", 1) == 1
    for h in range(heads):
        state = dot(near_ref[h, :, :size], far_ref[h])
        state = jnp.where(arrived, state, 0.0) + near_ref[h, :, size:].astype(f32)
        first = jnp.where(upper, partner_ref[h], own_ref[h])
        state = state.astype(bf16)
        later = dot(first[:, :size], state) + first[:, size:].astype(f32)
        later = later.astype(bf16)
        keep_ref[h] = jnp.where(upper, later, state)
        send_ref[h] = jnp.where(upper, state, later)


def entry_states(own, other):
    heads, size, width = own.shape
    bits = bits_of(lax.axis_size("seq"))
    partner = swapped(other, "seq", 1)
    total = join(1, own, partner, len(bits) == 2)
    near = ()
    assert len(bits) > 2
    for bit in bits[1:-1]:
        far = swapped(total, "seq", bit)
        total = join(bit, total, far, 2 * bit == bits[-1])
        near = (before(bit, near, far),)
    far = swapped(total, "seq", bits[-1])
    state = jax.ShapeDtypeStruct((heads, size, size), bf16)
    keep, send = vmem_call(
        functools.partial(entry_body, bits[-1]),
        (state, state),
        (*near, far, own, partner),
        flops=4 * heads * size * size * size,
        moved=14 * heads * size * size,
    )
    return keep, swapped(send, "seq", 1)


def back_body(places, *refs):
    own_refs, other_refs, refs = refs[:GROUPS], refs[GROUPS : 2 * GROUPS], refs[2 * GROUPS :]
    raised_ref, output_ref, gate_ref, gain_ref, weight_ref, keep_ref, *rest = refs
    normed = rest[-1]
    size = gain_ref.shape[1]
    slab_rows = keep_ref.shape[0]
    share = own_refs[0].shape[0]
    half = GROUPS * share
    upper = place("seq", 1) == 1
    for k, away in enumerate(places):
        rows = pl.ds(pl.multiple_of((place("head") ^ away) * slab_rows, 16), slab_rows)
        for h in range(raised_ref.shape[0]):
            lanes = slice(h * size, (h + 1) * size)
            group, at = divmod(h % half, share)
            own, other = own_refs[group][at], other_refs[group][at]
            state = jnp.where(upper, other, own) if h < half else jnp.where(upper, own, other)
            attended = dot(raised_ref[h, rows, :], state) + output_ref[rows, lanes]
            power = jnp.sum(attended * attended, -1, keepdims=True) * (1.0 / size)
            normed[k * slab_rows : (k + 1) * slab_rows, lanes] = (
                attended * lax.rsqrt(power + 1e-05) * gain_ref[...] * gate_ref[rows, lanes]
            ).astype(bf16)
    total = dot(normed[...], weight_ref[...])
    keep_ref[...] = total[:slab_rows]
    if len(rest) > 1:
        rest[0][...] = total[slab_rows:].astype(bf16)


def back(places, states, raised, output_rows, out_gate, gain, weight, slab_rows):
    slab_count, width = len(places), weight.shape[1]
    shapes = [jax.ShapeDtypeStruct((slab_rows, width), f32)]
    if slab_count > 1:
        shapes.append(jax.ShapeDtypeStruct((slab_rows, width), bf16))
    return vmem_call(
        functools.partial(back_body, places),
        shapes,
        (*states, raised, output_rows, out_gate, gain, weight),
        scratch=[pltpu.VMEM((slab_count * slab_rows, weight.shape[0]), bf16)],
        grant=10,
        flops=2 * slab_count * slab_rows * weight.shape[0] * width,
        moved=2 * weight.shape[0] * width,
    )


def shards(
    hidden_in,
    qkv_weight,
    conv_weight,
    decay_log,
    dt_bias,
    decay_down,
    decay_up,
    beta_weight,
    gate_down,
    gate_up,
    norm_gain,
    out_weight,
):
    heads, size = decay_log.shape[0], norm_gain.shape[0]
    channels = heads * size
    devices = lax.axis_size("head")
    weight = qkv_weight.transpose(1, 0, 2)
    fetched = load(hidden_in, decay_down, beta_weight.T, weight)
    slabs, rims, fetched = gathered(hidden_in, fetched)
    *pairs, solved, attend, start, rows = front(
        rims, slabs, fetched, (decay_log, decay_up, dt_bias[None], conv_weight), weight, size
    )
    count = start.shape[1]
    raised, output_rows, out_gate = vmem_call(
        rows_body,
        (
            jax.ShapeDtypeStruct((heads, count, size), bf16),
            jax.ShapeDtypeStruct((count, channels), f32),
            jax.ShapeDtypeStruct((count, channels), f32),
        ),
        (attend, solved, start, rows, gate_down, gate_up),
        grant=8,
        flops=2 * heads * count * count * 2 * size,
        moved=4 * heads * count * count,
    )
    states = [entry_states(*both) for both in zip(pairs[:GROUPS], pairs[GROUPS:])]
    states = [own for own, _ in states] + [other for _, other in states]
    slab_rows = count // devices
    sums = {}
    for g in reversed(range(max(devices // 2, 1))):
        places = [2 * g, 2 * g + 1][:devices]
        keep, *send = back(
            places, states, raised, output_rows, out_gate, norm_gain[None], out_weight, slab_rows
        )
        near = [swapped(part, "head", 1).astype(f32) for part in send]
        sums[g] = [lax.optimization_barrier(sum([keep] + near))]
    for bit in bits_of(devices)[1:]:
        for g in sorted(sums):
            if 2 * g & bit:
                arrived = swapped(sum(sums.pop(g)).astype(bf16), "head", bit)
                sums[g ^ bit // 2].append(arrived.astype(f32))
    return sum(sums[0]).astype(bf16)


def solution(mesh):
    return jax.shard_map(
        shards,
        mesh=mesh,
        in_specs=(
            P(("seq", "head"), None),
            P(None, None, "head"),
            P(None, None, "head"),
            P("head"),
            P("head"),
            P(),
            P(None, "head"),
            P(None, "head"),
            P(),
            P(None, "head"),
            P(),
            P("head", None),
        ),
        out_specs=P(("seq", "head"), None),
        check_vma=False,
    )
```
